32 devices in a mesh: shot: 8 (over z, y), freq: 4 (over x, core).
Axes of the slice: x: 2, y: 2, z: 4, core: 2. Of those that a mesh axis runs over, the one named last changes fastest.
Arguments:
- blended: bfloat16 [2, 32, 512, 256], P(None, 'shot', 'freq'), may hold values from -6 to 6
- estimate: bfloat16 [2, 32, 512, 256], P(None, 'shot', 'freq'), may hold values from -5 to 5
- partner: int32 [32], P('shot'), may hold values from 0 to 31, as said below
- delays: int32 [32], replicated, may hold values from 0 to 256
- levels: int32 [8], replicated, may hold values from 1 to 4
Outputs:
- deblended: bfloat16 [2, 32, 512, 256], P(None, 'shot', 'freq')
The draws below stay inside these ranges and needn't reach their ends.
Inputs may be any that keep to these rules, and one draw needn't show every extreme that they name: Shot s of block b = s // 4 is paired with a shot of block (b + 4) modulo 32 / 4; the pairing is mutual, partner[partner[s]] = s.
All inputs are finite; a program needn't handle non-finite values.
Results may differ from the reference program's by a relative error of at most 0.005.
Values may be sent and summed in bfloat16 or wider, within the bound.
A program may use at most 64 MiB of HBM per device.

```python
import math
import jax
import jax.numpy as jnp
from jax import lax

NR = 256
NF = 512
NT = 1024
SHOT_DEV = 4
SHOTS = 32
WINDOWS = 8
PASSES = 2


def draw_partner(key, part):
    blocks = SHOTS // SHOT_DEV
    half_blocks = blocks // 2
    pair_keys = jax.random.split(jax.random.fold_in(key, 17), half_blocks)
    shuffles = jax.vmap(lambda one_key: jax.random.permutation(one_key, SHOT_DEV))(pair_keys)
    starts = jnp.arange(half_blocks, dtype=jnp.int32)[:, None] * SHOT_DEV
    lower_pairs = starts + half_blocks * SHOT_DEV + shuffles
    inverse = jnp.argsort(shuffles, axis=1)
    upper_pairs = starts + inverse
    return jnp.concatenate([lower_pairs.reshape(-1), upper_pairs.reshape(-1)]).astype(jnp.int32)


def set_ends(values, own_key, low, largest):
    dims = values.shape
    place = [jax.random.randint(jax.random.fold_in(own_key, axis), (), 0, dims[axis]) for axis in range(len(dims))]
    values = values.at[tuple(place)].set(low)
    longest = dims.index(max(dims))
    place[longest] = (place[longest] + 1) % dims[longest]
    return values.at[tuple(place)].set(largest)


def level_of(key, extent, cuts, smallest, high):
    loudness = 1.0
    for position, parts in cuts:
        draws = jax.random.uniform(jax.random.fold_in(jax.random.fold_in(key, 6), position), (parts,), jnp.float32, smallest / len(cuts), high / len(cuts))
        loudness = loudness * jnp.repeat(jnp.exp(draws), extent[position] // parts).reshape((-1,) + (1,) * (len(extent) - 1 - position))
    return loudness


def scatter_about(stream_key, dims, width, reach, cuts=(), kind=jnp.bfloat16):
    gain = level_of(stream_key, dims, cuts, -0.22, 0.18) if cuts else 1.0
    entries = jax.random.normal(stream_key, dims, jnp.float32) * width * gain
    return jnp.minimum(jnp.maximum(entries, -reach), reach).astype(kind)


def setup_inputs(seed: int = 0) -> dict:
    keys = jax.random.split(jax.random.key(seed), 6)
    blended = scatter_about(keys[0], (2, SHOTS, NF, NR), 1.0, 6.0, ((1, 8), (2, 4)))
    estimate = scatter_about(keys[1], (2, SHOTS, NF, NR), 0.7, 5.0, ((1, 8), (2, 4)))
    partner = draw_partner(jax.random.fold_in(keys[5], 71), 0)
    delays = set_ends(jax.random.randint(keys[3], (SHOTS,), 0, NT // 4 + 1), jax.random.fold_in(keys[3], 1), 0, (NT // 4 + 1) - 1).astype(jnp.int32)
    levels = set_ends(jax.random.randint(keys[4], (WINDOWS,), 1, 5), jax.random.fold_in(keys[4], 1), 1, 4).astype(jnp.int32)
    return dict(blended=blended, estimate=estimate, partner=partner, delays=delays, levels=levels)


relaxation = 0.5
level_scale = 0.25

def tables(length):
    indices = jnp.arange(length, dtype=jnp.int32)
    products = jnp.mod(indices[:, None] * indices[None, :], length)
    angles = 2.0 * math.pi / length * products.astype(jnp.float32)
    return (jnp.cos(angles), jnp.sin(angles))

def spectrum(real_part, imag_part, direction_sign, shot_cos, shot_sin, recv_cos, recv_sin):
    highest = lax.Precision.HIGHEST

    def receivers(values, table):
        return jnp.einsum('...n,nk->...k', values, table, precision=highest)

    def shots(values, table):
        return jnp.einsum('tk,...tfn->...kfn', table, values, precision=highest)
    first_real = receivers(real_part, recv_cos) + direction_sign * receivers(imag_part, recv_sin)
    first_imag = receivers(imag_part, recv_cos) - direction_sign * receivers(real_part, recv_sin)
    out_real = shots(first_real, shot_cos) + direction_sign * shots(first_imag, shot_sin)
    out_imag = shots(first_imag, shot_cos) - direction_sign * shots(first_real, shot_sin)
    scale = 1.0 / math.sqrt(shot_cos.shape[0] * recv_cos.shape[0])
    return (out_real * scale, out_imag * scale)

def shrink(real_part, imag_part, threshold):
    modulus = jnp.sqrt(real_part * real_part + imag_part * imag_part)
    factor = jnp.maximum(modulus - threshold, 0.0) / jnp.maximum(modulus, threshold)
    return (real_part * factor, imag_part * factor)

def one_pass(current, blended, partner, delays, levels):
    block = SHOT_DEV
    span = 2 * block
    current_f = current.astype(jnp.float32)
    partner_recs = current_f[:, partner]
    offsets = delays[partner] - delays
    frequency = jnp.arange(NF, dtype=jnp.int32)
    phase_index = jnp.mod(frequency[None, :] * offsets[:, None], NT)
    angles = 2.0 * math.pi / NT * phase_index.astype(jnp.float32)
    phase_cos = jnp.cos(angles)[:, :, None]
    phase_sin = jnp.sin(angles)[:, :, None]
    shifted_real = partner_recs[0] * phase_cos + partner_recs[1] * phase_sin
    shifted_imag = partner_recs[1] * phase_cos - partner_recs[0] * phase_sin
    shifted = jnp.stack([shifted_real, shifted_imag])
    updated = current_f + relaxation * (blended.astype(jnp.float32) - current_f - shifted)
    padded = jnp.concatenate([updated, jnp.zeros((2, block, NF, NR), jnp.float32)], axis=1)
    steps_t = jnp.arange(span, dtype=jnp.float32)
    taper = jnp.sin(math.pi * (steps_t + 0.5) / span) ** 2
    shot_cos, shot_sin = tables(span)
    recv_cos, recv_sin = tables(NR)

    def window(window_index):
        segment = lax.dynamic_slice_in_dim(padded, window_index * block, span, axis=1)
        segment = segment * taper[None, :, None, None]
        coef_real, coef_imag = spectrum(segment[0], segment[1], 1.0, shot_cos, shot_sin, recv_cos, recv_sin)
        modulus = jnp.sqrt(coef_real * coef_real + coef_imag * coef_imag)
        mean_mod = jnp.sum(modulus) / (span * NF * NR)
        threshold = level_scale * levels[window_index].astype(jnp.float32) * mean_mod
        kept_real, kept_imag = shrink(coef_real, coef_imag, threshold)
        back_real, back_imag = spectrum(kept_real, kept_imag, -1.0, shot_cos, shot_sin, recv_cos, recv_sin)
        result = jnp.stack([back_real, back_imag])
        return (result[:, :block], result[:, block:])
    firsts, seconds = lax.map(window, jnp.arange(WINDOWS, dtype=jnp.int32))
    firsts = jnp.transpose(firsts, (1, 0, 2, 3, 4)).reshape(2, SHOTS, NF, NR)
    seconds = jnp.transpose(seconds, (1, 0, 2, 3, 4)).reshape(2, SHOTS, NF, NR)
    seconds = jnp.concatenate([jnp.zeros((2, block, NF, NR), jnp.float32), seconds[:, :SHOTS - block]], axis=1)
    return (firsts + seconds).astype(jnp.bfloat16)

def reference(blended, estimate, partner, delays, levels):
    current = estimate
    for pass_index in range(PASSES):
        current = one_pass(current, blended, partner, delays, levels)
    return current
```

```python
import functools
import math

import jax
import jax.numpy as jnp
import numpy as np
from jax import lax
from jax.experimental import pallas as pl
from jax.experimental.pallas import tpu as pltpu
from jax.sharding import PartitionSpec as P

NF = 512
NT = 1024
PASSES = 2


relaxation = 0.5
level_scale = 0.25


def tables(length):
    indices = jnp.arange(length, dtype=jnp.int32)
    products = jnp.mod(indices[:, None] * indices[None, :], length)
    angles = 2.0 * math.pi / length * products.astype(jnp.float32)
    return (jnp.cos(angles), jnp.sin(angles))


def spectrum(real_part, imag_part, direction_sign, shot_cos, shot_sin, recv_cos, recv_sin):
    highest = lax.Precision.HIGHEST

    def receivers(values, table):
        return jnp.einsum("...n,nk->...k", values, table, precision=highest)

    def shots(values, table):
        return jnp.einsum("tk,...tfn->...kfn", table, values, precision=highest)

    first_real = receivers(real_part, recv_cos) + direction_sign * receivers(imag_part, recv_sin)
    first_imag = receivers(imag_part, recv_cos) - direction_sign * receivers(real_part, recv_sin)
    out_real = shots(first_real, shot_cos) + direction_sign * shots(first_imag, shot_sin)
    out_imag = shots(first_imag, shot_cos) - direction_sign * shots(first_real, shot_sin)
    scale = 1.0 / math.sqrt(shot_cos.shape[0] * recv_cos.shape[0])
    return (out_real * scale, out_imag * scale)


def shrink(real_part, imag_part, threshold):
    modulus = jnp.sqrt(real_part * real_part + imag_part * imag_part)
    factor = jnp.maximum(modulus - threshold, 0.0) / jnp.maximum(modulus, threshold)
    return (real_part * factor, imag_part * factor)


def phase_tables(offsets, frequency):
    phase_index = jnp.mod(frequency[None, :] * offsets[:, None], NT)
    angles = 2.0 * math.pi / NT * phase_index.astype(jnp.float32)
    return (jnp.cos(angles)[:, :, None], jnp.sin(angles)[:, :, None])


def relax_step(current, blended, partner_recs, phase_cos, phase_sin):
    shifted_real = partner_recs[0] * phase_cos + partner_recs[1] * phase_sin
    shifted_imag = partner_recs[1] * phase_cos - partner_recs[0] * phase_sin
    shifted = jnp.stack([shifted_real, shifted_imag])
    current_f = current.astype(jnp.float32)
    return current_f + relaxation * (blended.astype(jnp.float32) - current_f - shifted)


def whole_pass(
    current, blended, partner_all, phase_cos, phase_sin, level_all, taper, tables_all, block
):
    shot_cos, shot_sin, recv_cos, recv_sin = tables_all
    total_shots = current.shape[1]
    few_freq = current.shape[2]
    receivers_count = current.shape[3]
    count = total_shots // block
    partner_recs = jnp.take(current, partner_all, axis=1).astype(jnp.float32)
    updated = relax_step(current, blended, partner_recs, phase_cos, phase_sin)
    grouped = jnp.transpose(
        updated.reshape(2, count, block, few_freq, receivers_count), (1, 0, 2, 3, 4)
    )
    following = jnp.concatenate([grouped[1:], jnp.zeros_like(grouped[:1])], axis=0)
    segments = jnp.concatenate([grouped, following], axis=2) * taper[None, None, :, None, None]
    coef_real, coef_imag = spectrum(
        segments[:, 0], segments[:, 1], 1.0, shot_cos, shot_sin, recv_cos, recv_sin
    )
    modulus = jnp.sqrt(coef_real * coef_real + coef_imag * coef_imag)
    local_sum = jnp.sum(modulus, axis=(1, 2, 3))
    total_sum = lax.psum(local_sum, ("shot", "freq"))
    span = 2 * block
    threshold = (level_scale * level_all * total_sum / (span * NF * receivers_count))[
        :, None, None, None
    ]
    kept_real, kept_imag = shrink(coef_real, coef_imag, threshold)
    back_real, back_imag = spectrum(
        kept_real, kept_imag, -1.0, shot_cos, shot_sin, recv_cos, recv_sin
    )
    result = jnp.stack([back_real, back_imag], axis=1)
    firsts = result[:, :, :block]
    seconds = jnp.concatenate(
        [jnp.zeros_like(result[:1, :, block:]), result[:-1, :, block:]], axis=0
    )
    summed = firsts + seconds
    return (
        jnp.transpose(summed, (1, 0, 2, 3, 4))
        .reshape(2, total_shots, few_freq, receivers_count)
        .astype(jnp.bfloat16)
    )


def on_device(blended, estimate, partner, delays, levels):
    block = estimate.shape[1]
    freq_local = estimate.shape[2]
    receivers_count = estimate.shape[3]
    span = 2 * block
    steps_t = jnp.arange(span, dtype=jnp.float32)
    taper = jnp.sin(math.pi * (steps_t + 0.5) / span) ** 2
    shot_cos, shot_sin = tables(span)
    recv_cos, recv_sin = tables(receivers_count)
    tables_all = (shot_cos, shot_sin, recv_cos, recv_sin)
    blended_all, current = (
        lax.all_to_all(blended, "shot", split_axis=2, concat_axis=1, tiled=True),
        lax.all_to_all(estimate, "shot", split_axis=2, concat_axis=1, tiled=True),
    )
    few_freq = current.shape[2]
    partner_all = lax.all_gather(partner, "shot", axis=0, tiled=True)
    offsets = jnp.take(delays, partner_all) - delays
    frequency = (
        lax.axis_index("freq") * freq_local
        + lax.axis_index("shot") * few_freq
        + jnp.arange(few_freq, dtype=jnp.int32)
    )
    phase_cos, phase_sin = phase_tables(offsets, frequency)
    level_all = levels.astype(jnp.float32)
    for pass_index in range(PASSES):
        current = whole_pass(
            current,
            blended_all,
            partner_all,
            phase_cos,
            phase_sin,
            level_all,
            taper,
            tables_all,
            block,
        )
    return lax.all_to_all(current, "shot", split_axis=1, concat_axis=2, tiled=True)


LANES = 128
TINY = 1.1754944e-38


def fourier_matrices(length):
    indices = np.arange(length)
    angles = 2.0 * np.pi / length * (np.outer(indices, indices) % length)
    cos, sin = np.cos(angles), np.sin(angles)
    forward = np.block([[cos, -sin], [sin, cos]])

    def split(matrix):
        hi = matrix.astype(jnp.bfloat16)
        lo = (matrix - hi.astype(np.float64)).astype(jnp.bfloat16)
        return np.stack([hi, lo])

    return split(forward), split(forward.T)


def short_fourier(values, sign):
    count = len(values)
    if count == 1:
        return values
    even = short_fourier(values[0::2], sign)
    odd = short_fourier(values[1::2], sign)
    low, high = [], []
    for k in range(count // 2):
        real, imag = odd[k]
        if 4 * k == count:
            real, imag = (-imag, real) if sign > 0 else (imag, -real)
        elif 8 * k == count or 8 * k == 3 * count:
            half = math.sqrt(0.5)
            turned = (real - sign * imag, imag + sign * real)
            if 8 * k == 3 * count:
                turned = (-real - sign * imag, sign * real - imag)
            real, imag = turned[0] * half, turned[1] * half
        elif k:
            cos = math.cos(2.0 * math.pi * k / count)
            sin = sign * math.sin(2.0 * math.pi * k / count)
            real, imag = real * cos - imag * sin, imag * cos + real * sin
        low.append((even[k][0] + real, even[k][1] + imag))
        high.append((even[k][0] - real, even[k][1] - imag))
    return low + high


def flipped(index, mask, count):
    result, bit = 0, 1
    while bit < count:
        result = result + (index // bit + mask // bit) % 2 * bit
        bit *= 2
    return result


def deblend_kernel(
    n,
    nf,
    block,
    few,
    nr,
    blended_ref,
    estimate_ref,
    partner_ref,
    delays_ref,
    levels_ref,
    forward_hbm,
    inverse_hbm,
    out_ref,
    e_all,
    b_all,
    info,
    turn_cos,
    turn_sin,
    turn_pick,
    x_hi,
    x_lo,
    lines,
    coefs,
    carry,
    limit,
    near_sums,
    far_sums,
    forward,
    inverse,
    local_sem,
    info_send,
    info_recv,
    e_send,
    e_recv,
    b_send,
    b_recv,
    near_send,
    near_recv,
    far_send,
    far_recv,
    out_send,
    out_recv,
):
    total = n * block
    span = 2 * block
    half = n // 2
    me = lax.axis_index("shot")
    column = lax.axis_index("freq")
    mesh_id = pl.DeviceIdType.MESH
    peers = [flipped(me, k, n) for k in range(n)]
    order = list(range(half, n)) + list(range(1, half))
    others = [lax.rem(column + k, nf) for k in range(nf)]

    barrier = pltpu.get_barrier_semaphore()
    for k in order:
        pl.semaphore_signal(barrier, inc=1, device_id={"shot": peers[k]}, device_id_type=mesh_id)
    for k in range(1, nf):
        pl.semaphore_signal(barrier, inc=1, device_id={"freq": others[k]}, device_id_type=mesh_id)

    local_copies = [
        pltpu.make_async_copy(forward_hbm, forward, local_sem.at[0]),
        pltpu.make_async_copy(inverse_hbm, inverse, local_sem.at[1]),
        pltpu.make_async_copy(
            estimate_ref.at[:, :, pl.ds(me * few, few), :],
            e_all.at[:, pl.ds(me * block, block)],
            local_sem.at[2],
        ),
        pltpu.make_async_copy(
            blended_ref.at[:, :, pl.ds(me * few, few), :],
            b_all.at[:, pl.ds(me * block, block)],
            local_sem.at[3],
        ),
    ]
    for copy in local_copies:
        copy.start()

    lane = lax.broadcasted_iota(jnp.int32, (8, LANES), 1)
    row = lax.broadcasted_iota(jnp.int32, (8, LANES), 0)
    tile = jnp.zeros((8, LANES), jnp.int32)
    for i in range(block):
        own = me * block + i
        mate = partner_ref[i]
        offset = delays_ref[mate] - delays_ref[own]
        here = lane == own
        tile = jnp.where(here & (row == 0), mate, tile)
        tile = jnp.where(here & (row == 1), offset, tile)
    info[0] = tile

    pl.semaphore_wait(barrier, n + nf - 2)

    def send(source, target, send_sem, recv_sem, where):
        copy = pltpu.make_async_remote_copy(
            src_ref=source,
            dst_ref=target,
            send_sem=send_sem,
            recv_sem=recv_sem,
            device_id=where,
            device_id_type=mesh_id,
        )
        copy.start()
        return copy

    info_copies = [
        send(info.at[0], info.at[k], info_send.at[k], info_recv.at[k], {"shot": peers[k]})
        for k in order
    ]
    record_copies = []
    for k in order:
        for held, whole, sent, received in (
            (estimate_ref, e_all, e_send, e_recv),
            (blended_ref, b_all, b_send, b_recv),
        ):
            record_copies.append(
                send(
                    held.at[:, :, pl.ds(peers[k] * few, few), :],
                    whole.at[:, pl.ds(me * block, block)],
                    sent.at[k],
                    received.at[k],
                    {"shot": peers[k]},
                )
            )

    lines[pl.ds(total, block)] = jnp.zeros((block, few, 2 * nr), jnp.float32)
    for copy in info_copies:
        copy.wait()
    known = info[0]
    for k in range(1, n):
        known = known + info[k]
    frequency = (column * n + me) * few + lax.broadcasted_iota(jnp.int32, (few, LANES), 0)
    phase = (frequency * known[1:2, :]) & (NT - 1)
    angles = 2.0 * math.pi / NT * phase.astype(jnp.float32)
    cos_table = relaxation * jnp.cos(angles)
    sin_table = relaxation * jnp.sin(angles)
    for s in range(total):
        first = (s // block + half) % n * block
        turn_cos[s] = jnp.broadcast_to(cos_table[:, s : s + 1], (few, LANES))
        turn_sin[s] = jnp.broadcast_to(sin_table[:, s : s + 1], (few, LANES))
        turn_pick[s] = jnp.broadcast_to(known[0:1, s : s + 1] - first, (few, LANES))

    for copy in record_copies:
        copy.wait()
    for copy in local_copies:
        copy.wait()

    def keep(s, lanes, value):
        top = value.astype(jnp.bfloat16)
        x_hi[s, :, lanes] = top
        x_lo[s, :, lanes] = (value - top.astype(jnp.float32)).astype(jnp.bfloat16)

    def relax(pair, carried):
        for c in range(0, nr, LANES):
            lanes = slice(c, c + LANES)
            records = [
                [
                    [
                        e_all[part, (pair + side * half) * block + i, :, lanes].astype(jnp.float32)
                        for part in range(2)
                    ]
                    for i in range(block)
                ]
                for side in range(2)
            ]
            for side in range(2):
                for i in range(block):
                    s = (pair + side * half) * block + i
                    pick = turn_pick[s]
                    cos, sin = turn_cos[s], turn_sin[s]
                    mate_real, mate_imag = records[1 - side][0]
                    for j in range(1, block):
                        mate_real = jnp.where(pick == j, records[1 - side][j][0], mate_real)
                        mate_imag = jnp.where(pick == j, records[1 - side][j][1], mate_imag)
                    real, imag = records[side][i]
                    seen_real = b_all[0, s, :, lanes].astype(jnp.float32)
                    seen_imag = b_all[1, s, :, lanes].astype(jnp.float32)
                    keep(
                        s,
                        lanes,
                        real + relaxation * (seen_real - real) - (mate_real * cos + mate_imag * sin),
                    )
                    keep(
                        s,
                        slice(nr + c, nr + c + LANES),
                        imag + relaxation * (seen_imag - imag) - (mate_imag * cos - mate_real * sin),
                    )
        return carried

    def receivers(start, table):
        rows = (total // 2) * few
        top = x_hi[pl.ds(start, total // 2)].reshape(rows, 2 * nr)
        rest = x_lo[pl.ds(start, total // 2)].reshape(rows, 2 * nr)
        result = jnp.dot(top, table[0], preferred_element_type=jnp.float32)
        result = result + jnp.dot(rest, table[0], preferred_element_type=jnp.float32)
        result = result + jnp.dot(top, table[1], preferred_element_type=jnp.float32)
        return result.reshape(total // 2, few, 2 * nr)

    weights = [math.sin(math.pi * (t + 0.5) / span) ** 2 for t in range(span)]

    def analyse(step):
        def window(j, carried):
            summed = jnp.zeros((few, LANES), jnp.float32)
            for c in range(0, nr, LANES):
                values = [
                    (
                        lines[j * block + t, :, c : c + LANES] * weights[t],
                        lines[j * block + t, :, nr + c : nr + c + LANES] * weights[t],
                    )
                    for t in range(span)
                ]
                for k, (real, imag) in enumerate(short_fourier(values, -1)):
                    power = real * real + imag * imag
                    summed = summed + power * lax.rsqrt(jnp.maximum(power, TINY))
                    coefs[j, k, :, c : c + LANES] = real
                    coefs[j, k, :, nr + c : nr + c + LANES] = imag
            near_sums[step, 0, pl.ds(j, 1), :] = jnp.sum(summed, axis=0, keepdims=True)
            return carried

        lax.fori_loop(0, n, window, 0)

    def thresholds(step):
        copies = [
            send(
                near_sums.at[step, 0],
                near_sums.at[step, k],
                near_send.at[step, k],
                near_recv.at[step, k],
                {"shot": peers[k]},
            )
            for k in order
        ]
        for copy in copies:
            copy.wait()
        part = near_sums[step, 0]
        for k in range(1, n):
            part = part + near_sums[step, k]
        far_sums[step, 0] = part
        copies = [
            send(
                far_sums.at[step, 0],
                far_sums.at[step, k],
                far_send.at[step, k],
                far_recv.at[step, k],
                {"freq": others[k]},
            )
            for k in range(1, nf)
        ]
        for copy in copies:
            copy.wait()
        for k in range(1, nf):
            part = part + far_sums[step, k]
        limit[...] = jnp.broadcast_to(jnp.sum(part, axis=1, keepdims=True), (n, LANES))

    scale = 1.0 / (span * nr)
    count = span * few * n * nf * nr

    def synthesise(j, carried):
        level = levels_ref[j].astype(jnp.float32) * (level_scale * scale / count)
        bound = limit[pl.ds(j, 1), :] * level
        for c in range(0, nr, LANES):
            values = []
            for k in range(span):
                real = coefs[j, k, :, c : c + LANES]
                imag = coefs[j, k, :, nr + c : nr + c + LANES]
                power = real * real + imag * imag
                factor = jnp.maximum(scale - bound * lax.rsqrt(power), 0.0)
                values.append((real * factor, imag * factor))
            for t, parts in enumerate(short_fourier(values, 1)):
                for part in range(2):
                    lanes = slice(part * nr + c, part * nr + c + LANES)
                    if t < block:
                        keep(j * block + t, lanes, parts[part] + carry[t, :, lanes])
                    else:
                        carry[t - block, :, lanes] = parts[part]
        return carried

    for step in range(PASSES):
        lax.fori_loop(0, half, relax, 0)
        for start in (0, total // 2):
            lines[pl.ds(start, total // 2)] = receivers(start, forward)
        analyse(step)
        thresholds(step)
        carry[...] = jnp.zeros_like(carry)
        lax.fori_loop(0, n, synthesise, 0)
        if step < PASSES - 1:
            for start in (0, total // 2):
                result = receivers(start, inverse).astype(jnp.bfloat16)
                e_all[0, pl.ds(start, total // 2)] = result[:, :, :nr]
                e_all[1, pl.ds(start, total // 2)] = result[:, :, nr:]

    copies = []
    mine = me // half
    for side, group in ((1 - mine, range(half, n)), (mine, range(1, half))):
        start = side * (total // 2)
        result = receivers(start, inverse).astype(jnp.bfloat16)
        e_all[0, pl.ds(start, total // 2)] = result[:, :, :nr]
        e_all[1, pl.ds(start, total // 2)] = result[:, :, nr:]
        for k in group:
            copies.append(
                send(
                    e_all.at[:, pl.ds(peers[k] * block, block)],
                    out_ref.at[:, :, pl.ds(me * few, few), :],
                    out_send.at[k],
                    out_recv.at[k],
                    {"shot": peers[k]},
                )
            )
    last = pltpu.make_async_copy(
        e_all.at[:, pl.ds(me * block, block)],
        out_ref.at[:, :, pl.ds(me * few, few), :],
        local_sem.at[0],
    )
    last.start()
    for copy in copies:
        copy.wait()
    last.wait()


def in_one_kernel(n, nf, blended, estimate, partner, delays, levels):
    block, freq_local, nr = estimate.shape[1:]
    few = freq_local // n
    total = n * block
    forward, inverse = fourier_matrices(nr)
    f32, bf16 = jnp.float32, jnp.bfloat16
    anywhere = pl.BlockSpec(memory_space=pl.ANY)
    scalars = pl.BlockSpec(memory_space=pltpu.SMEM)
    dma = pltpu.SemaphoreType.DMA
    return pl.pallas_call(
        functools.partial(deblend_kernel, n, nf, block, few, nr),
        out_shape=jax.ShapeDtypeStruct(estimate.shape, estimate.dtype),
        in_specs=[anywhere, anywhere, scalars, scalars, scalars, anywhere, anywhere],
        out_specs=anywhere,
        scratch_shapes=[
            pltpu.VMEM((2, total, few, nr), bf16),
            pltpu.VMEM((2, total, few, nr), bf16),
            pltpu.VMEM((n, 8, LANES), jnp.int32),
            pltpu.VMEM((total, few, LANES), f32),
            pltpu.VMEM((total, few, LANES), f32),
            pltpu.VMEM((total, few, LANES), jnp.int32),
            pltpu.VMEM((total, few, 2 * nr), bf16),
            pltpu.VMEM((total, few, 2 * nr), bf16),
            pltpu.VMEM((total + block, few, 2 * nr), f32),
            pltpu.VMEM((n, 2 * block, few, 2 * nr), f32),
            pltpu.VMEM((block, few, 2 * nr), f32),
            pltpu.VMEM((n, LANES), f32),
            pltpu.VMEM((PASSES, n, n, LANES), f32),
            pltpu.VMEM((PASSES, nf, n, LANES), f32),
            pltpu.VMEM(forward.shape, bf16),
            pltpu.VMEM(inverse.shape, bf16),
            dma((4,)),
            dma((n,)),
            dma((n,)),
            dma((n,)),
            dma((n,)),
            dma((n,)),
            dma((n,)),
            dma((PASSES, n)),
            dma((PASSES, n)),
            dma((PASSES, nf)),
            dma((PASSES, nf)),
            dma((n,)),
            dma((n,)),
        ],
        compiler_params=pltpu.CompilerParams(
            collective_id=0, has_side_effects=True, vmem_limit_bytes=48 * 1024 * 1024
        ),
    )(blended, estimate, partner, delays, levels, jnp.asarray(forward), jnp.asarray(inverse))


def solution(mesh):
    n, nf = mesh.shape["shot"], mesh.shape["freq"]

    def body(blended, estimate, partner, delays, levels):
        block, freq_local, nr = estimate.shape[1:]
        whole_tiles = (
            n == 8 and freq_local % (16 * n) == 0 and nr % LANES == 0 and n * block <= LANES
        )
        if whole_tiles:
            return in_one_kernel(n, nf, blended, estimate, partner, delays, levels)
        return on_device(blended, estimate, partner, delays, levels)

    return jax.shard_map(
        body,
        mesh=mesh,
        in_specs=(
            P(None, "shot", "freq", None),
            P(None, "shot", "freq", None),
            P("shot"),
            P(),
            P(),
        ),
        out_specs=P(None, "shot", "freq", None),
        check_vma=False,
    )
```

```python
import functools
import math

import jax
import jax.numpy as jnp
import numpy as np
from jax import lax
from jax.experimental import pallas as pl
from jax.experimental.pallas import tpu as pltpu
from jax.sharding import PartitionSpec as P

NF = 512
NT = 1024
PASSES = 2


relaxation = 0.5
level_scale = 0.25


def tables(length):
    indices = jnp.arange(length, dtype=jnp.int32)
    products = jnp.mod(indices[:, None] * indices[None, :], length)
    angles = 2.0 * math.pi / length * products.astype(jnp.float32)
    return (jnp.cos(angles), jnp.sin(angles))


def spectrum(real_part, imag_part, direction_sign, shot_cos, shot_sin, recv_cos, recv_sin):
    highest = lax.Precision.HIGHEST

    def receivers(values, table):
        return jnp.einsum("...n,nk->...k", values, table, precision=highest)

    def shots(values, table):
        return jnp.einsum("tk,...tfn->...kfn", table, values, precision=highest)

    first_real = receivers(real_part, recv_cos) + direction_sign * receivers(imag_part, recv_sin)
    first_imag = receivers(imag_part, recv_cos) - direction_sign * receivers(real_part, recv_sin)
    out_real = shots(first_real, shot_cos) + direction_sign * shots(first_imag, shot_sin)
    out_imag = shots(first_imag, shot_cos) - direction_sign * shots(first_real, shot_sin)
    scale = 1.0 / math.sqrt(shot_cos.shape[0] * recv_cos.shape[0])
    return (out_real * scale, out_imag * scale)


def shrink(real_part, imag_part, threshold):
    modulus = jnp.sqrt(real_part * real_part + imag_part * imag_part)
    factor = jnp.maximum(modulus - threshold, 0.0) / jnp.maximum(modulus, threshold)
    return (real_part * factor, imag_part * factor)


def phase_tables(offsets, frequency):
    phase_index = jnp.mod(frequency[None, :] * offsets[:, None], NT)
    angles = 2.0 * math.pi / NT * phase_index.astype(jnp.float32)
    return (jnp.cos(angles)[:, :, None], jnp.sin(angles)[:, :, None])


def relax_step(current, blended, partner_recs, phase_cos, phase_sin):
    shifted_real = partner_recs[0] * phase_cos + partner_recs[1] * phase_sin
    shifted_imag = partner_recs[1] * phase_cos - partner_recs[0] * phase_sin
    shifted = jnp.stack([shifted_real, shifted_imag])
    current_f = current.astype(jnp.float32)
    return current_f + relaxation * (blended.astype(jnp.float32) - current_f - shifted)


def whole_pass(
    current, blended, partner_all, phase_cos, phase_sin, level_all, taper, tables_all, block
):
    shot_cos, shot_sin, recv_cos, recv_sin = tables_all
    total_shots = current.shape[1]
    few_freq = current.shape[2]
    receivers_count = current.shape[3]
    count = total_shots // block
    partner_recs = jnp.take(current, partner_all, axis=1).astype(jnp.float32)
    updated = relax_step(current, blended, partner_recs, phase_cos, phase_sin)
    grouped = jnp.transpose(
        updated.reshape(2, count, block, few_freq, receivers_count), (1, 0, 2, 3, 4)
    )
    following = jnp.concatenate([grouped[1:], jnp.zeros_like(grouped[:1])], axis=0)
    segments = jnp.concatenate([grouped, following], axis=2) * taper[None, None, :, None, None]
    coef_real, coef_imag = spectrum(
        segments[:, 0], segments[:, 1], 1.0, shot_cos, shot_sin, recv_cos, recv_sin
    )
    modulus = jnp.sqrt(coef_real * coef_real + coef_imag * coef_imag)
    local_sum = jnp.sum(modulus, axis=(1, 2, 3))
    total_sum = lax.psum(local_sum, ("shot", "freq"))
    span = 2 * block
    threshold = (level_scale * level_all * total_sum / (span * NF * receivers_count))[
        :, None, None, None
    ]
    kept_real, kept_imag = shrink(coef_real, coef_imag, threshold)
    back_real, back_imag = spectrum(
        kept_real, kept_imag, -1.0, shot_cos, shot_sin, recv_cos, recv_sin
    )
    result = jnp.stack([back_real, back_imag], axis=1)
    firsts = result[:, :, :block]
    seconds = jnp.concatenate(
        [jnp.zeros_like(result[:1, :, block:]), result[:-1, :, block:]], axis=0
    )
    summed = firsts + seconds
    return (
        jnp.transpose(summed, (1, 0, 2, 3, 4))
        .reshape(2, total_shots, few_freq, receivers_count)
        .astype(jnp.bfloat16)
    )


def on_device(blended, estimate, partner, delays, levels):
    block = estimate.shape[1]
    freq_local = estimate.shape[2]
    receivers_count = estimate.shape[3]
    span = 2 * block
    steps_t = jnp.arange(span, dtype=jnp.float32)
    taper = jnp.sin(math.pi * (steps_t + 0.5) / span) ** 2
    shot_cos, shot_sin = tables(span)
    recv_cos, recv_sin = tables(receivers_count)
    tables_all = (shot_cos, shot_sin, recv_cos, recv_sin)
    blended_all, current = (
        lax.all_to_all(blended, "shot", split_axis=2, concat_axis=1, tiled=True),
        lax.all_to_all(estimate, "shot", split_axis=2, concat_axis=1, tiled=True),
    )
    few_freq = current.shape[2]
    partner_all = lax.all_gather(partner, "shot", axis=0, tiled=True)
    offsets = jnp.take(delays, partner_all) - delays
    frequency = (
        lax.axis_index("freq") * freq_local
        + lax.axis_index("shot") * few_freq
        + jnp.arange(few_freq, dtype=jnp.int32)
    )
    phase_cos, phase_sin = phase_tables(offsets, frequency)
    level_all = levels.astype(jnp.float32)
    for pass_index in range(PASSES):
        current = whole_pass(
            current,
            blended_all,
            partner_all,
            phase_cos,
            phase_sin,
            level_all,
            taper,
            tables_all,
            block,
        )
    return lax.all_to_all(current, "shot", split_axis=1, concat_axis=2, tiled=True)


LANES = 128
TINY = 1.1754944e-38


def fourier_matrices(length):
    half = np.arange(length // 2)

    def turns(parity):
        angles = 2.0 * np.pi / length * (np.outer(half, 2 * half + parity) % length)
        cos, sin = np.cos(angles), np.sin(angles)
        return np.block([[cos, -sin], [sin, cos]])

    forward = np.stack([turns(0), turns(1)]).astype(np.float32)
    return np.stack([forward, np.swapaxes(forward, 1, 2)])


def short_fourier(values, sign):
    count = len(values)
    if count == 1:
        return values
    even = short_fourier(values[0::2], sign)
    odd = short_fourier(values[1::2], sign)
    low, high = [], []
    for k in range(count // 2):
        real, imag = odd[k]
        if 4 * k == count:
            real, imag = (-imag, real) if sign > 0 else (imag, -real)
        elif 8 * k == count or 8 * k == 3 * count:
            half = math.sqrt(0.5)
            turned = (real - sign * imag, imag + sign * real)
            if 8 * k == 3 * count:
                turned = (-real - sign * imag, sign * real - imag)
            real, imag = turned[0] * half, turned[1] * half
        elif k:
            cos = math.cos(2.0 * math.pi * k / count)
            sin = sign * math.sin(2.0 * math.pi * k / count)
            real, imag = real * cos - imag * sin, imag * cos + real * sin
        low.append((even[k][0] + real, even[k][1] + imag))
        high.append((even[k][0] - real, even[k][1] - imag))
    return low + high


def flipped(index, mask, count):
    result, bit = 0, 1
    while bit < count:
        result = result + (index // bit + mask // bit) % 2 * bit
        bit *= 2
    return result


def deblend_kernel(
    n,
    nf,
    block,
    few,
    nr,
    blended_ref,
    estimate_ref,
    partner_hbm,
    delays_hbm,
    levels_hbm,
    tables_hbm,
    out_ref,
    partner_ref,
    delays_ref,
    levels_ref,
    e_all,
    b_all,
    info,
    turn_cos,
    turn_sin,
    turn_pick,
    x_hi,
    x_lo,
    lines,
    coefs,
    carry,
    limit,
    near_sums,
    far_sums,
    exact,
    forward,
    inverse,
    local_sem,
    info_send,
    info_recv,
    e_send,
    e_recv,
    b_send,
    b_recv,
    near_send,
    near_recv,
    far_send,
    far_recv,
    out_send,
    out_recv,
):
    total = n * block
    span = 2 * block
    half = n // 2
    hr = nr // 2
    columns = [parity * nr + c for parity in range(2) for c in range(0, hr, LANES)]
    me = lax.axis_index("shot")
    column = lax.axis_index("freq")
    mesh_id = pl.DeviceIdType.MESH
    peers = [flipped(me, k, n) for k in range(n)]
    order = list(range(half, n)) + list(range(1, half))
    others = [lax.rem(column + k, nf) for k in range(nf)]

    barrier = pltpu.get_barrier_semaphore()
    for k in order:
        pl.semaphore_signal(barrier, inc=1, device_id={"shot": peers[k]}, device_id_type=mesh_id)
    for k in range(1, nf):
        pl.semaphore_signal(barrier, inc=1, device_id={"freq": others[k]}, device_id_type=mesh_id)

    scalar_copies = [
        pltpu.make_async_copy(partner_hbm, partner_ref, local_sem.at[3]),
        pltpu.make_async_copy(delays_hbm, delays_ref, local_sem.at[4]),
        pltpu.make_async_copy(levels_hbm, levels_ref, local_sem.at[5]),
    ]
    for copy in scalar_copies:
        copy.start()
    local_copies = [
        pltpu.make_async_copy(tables_hbm, exact, local_sem.at[0]),
        pltpu.make_async_copy(
            estimate_ref.at[:, :, pl.ds(me * few, few), :],
            e_all.at[:, pl.ds(me * block, block)],
            local_sem.at[1],
        ),
        pltpu.make_async_copy(
            blended_ref.at[:, :, pl.ds(me * few, few), :],
            b_all.at[:, pl.ds(me * block, block)],
            local_sem.at[2],
        ),
    ]
    for copy in local_copies:
        copy.start()

    for copy in scalar_copies:
        copy.wait()
    lane = lax.broadcasted_iota(jnp.int32, (8, LANES), 1)
    row = lax.broadcasted_iota(jnp.int32, (8, LANES), 0)
    tile = jnp.zeros((8, LANES), jnp.int32)
    for i in range(block):
        own = me * block + i
        mate = partner_ref[i]
        offset = delays_ref[mate] - delays_ref[own]
        here = lane == own
        tile = jnp.where(here & (row == 0), mate, tile)
        tile = jnp.where(here & (row == 1), offset, tile)
    info[0] = tile

    pl.semaphore_wait(barrier, n + nf - 2)

    def send(source, target, send_sem, recv_sem, where):
        copy = pltpu.make_async_remote_copy(
            src_ref=source,
            dst_ref=target,
            send_sem=send_sem,
            recv_sem=recv_sem,
            device_id=where,
            device_id_type=mesh_id,
        )
        copy.start()
        return copy

    info_copies = [
        send(info.at[0], info.at[k], info_send.at[k], info_recv.at[k], {"shot": peers[k]})
        for k in order
    ]
    record_copies = []
    for k in order:
        for held, whole, sent, received in (
            (estimate_ref, e_all, e_send, e_recv),
            (blended_ref, b_all, b_send, b_recv),
        ):
            record_copies.append(
                send(
                    held.at[:, :, pl.ds(peers[k] * few, few), :],
                    whole.at[:, pl.ds(me * block, block)],
                    sent.at[k],
                    received.at[k],
                    {"shot": peers[k]},
                )
            )

    lines[pl.ds(total, block)] = jnp.zeros((block, few, 2 * nr), jnp.float32)
    for copy in info_copies:
        copy.wait()
    known = info[0]
    for k in range(1, n):
        known = known + info[k]
    frequency = (column * n + me) * few + lax.broadcasted_iota(jnp.int32, (few, LANES), 0)
    phase = (frequency * known[1:2, :]) & (NT - 1)
    angles = 2.0 * math.pi / NT * phase.astype(jnp.float32)
    cos_table = relaxation * jnp.cos(angles)
    sin_table = relaxation * jnp.sin(angles)
    for s in range(total):
        first = (s // block + half) % n * block
        turn_cos[s] = jnp.broadcast_to(cos_table[:, s : s + 1], (few, LANES))
        turn_sin[s] = jnp.broadcast_to(sin_table[:, s : s + 1], (few, LANES))
        turn_pick[s] = jnp.broadcast_to(known[0:1, s : s + 1] - first, (few, LANES))

    local_copies[0].wait()
    for index, pair in enumerate((forward, inverse)):
        top = exact[index].astype(jnp.bfloat16)
        pair[0] = top
        pair[1] = (exact[index] - top.astype(jnp.float32)).astype(jnp.bfloat16)

    for copy in record_copies:
        copy.wait()
    for copy in local_copies[1:]:
        copy.wait()

    def keep(s, lanes, value):
        top = value.astype(jnp.bfloat16)
        x_hi[s, :, lanes] = top
        x_lo[s, :, lanes] = (value - top.astype(jnp.float32)).astype(jnp.bfloat16)

    def relax(pair, carried):
        for c in range(0, hr, LANES):
            halves = (slice(c, c + LANES), slice(hr + c, hr + c + LANES))
            for side in range(2):
                first = (pair + side * half) * block
                other = (pair + (1 - side) * half) * block
                for i in range(block):
                    s = first + i
                    pick = turn_pick[s]
                    cos, sin = turn_cos[s], turn_sin[s]
                    moved = []
                    for lanes in halves:
                        mate_real = e_all[0, other, :, lanes].astype(jnp.float32)
                        mate_imag = e_all[1, other, :, lanes].astype(jnp.float32)
                        for j in range(1, block):
                            here = pick == j
                            real = e_all[0, other + j, :, lanes].astype(jnp.float32)
                            imag = e_all[1, other + j, :, lanes].astype(jnp.float32)
                            mate_real = jnp.where(here, real, mate_real)
                            mate_imag = jnp.where(here, imag, mate_imag)
                        real = e_all[0, s, :, lanes].astype(jnp.float32)
                        imag = e_all[1, s, :, lanes].astype(jnp.float32)
                        seen_real = b_all[0, s, :, lanes].astype(jnp.float32)
                        seen_imag = b_all[1, s, :, lanes].astype(jnp.float32)
                        shift_real = mate_real * cos + mate_imag * sin
                        shift_imag = mate_imag * cos - mate_real * sin
                        moved.append(
                            (
                                real + relaxation * (seen_real - real) - shift_real,
                                imag + relaxation * (seen_imag - imag) - shift_imag,
                            )
                        )
                    for part in range(2):
                        at = part * hr + c
                        keep(s, slice(at, at + LANES), moved[0][part] + moved[1][part])
                        at = nr + at
                        keep(s, slice(at, at + LANES), moved[0][part] - moved[1][part])
        return carried

    def receivers(start, table):
        rows = (total // 2) * few
        results = []
        for parity in range(2):
            lanes = slice(parity * nr, (parity + 1) * nr)
            top = x_hi[pl.ds(start, total // 2), :, lanes].reshape(rows, nr)
            rest = x_lo[pl.ds(start, total // 2), :, lanes].reshape(rows, nr)
            result = jnp.dot(top, table[0, parity], preferred_element_type=jnp.float32)
            result = result + jnp.dot(rest, table[0, parity], preferred_element_type=jnp.float32)
            result = result + jnp.dot(top, table[1, parity], preferred_element_type=jnp.float32)
            results.append(result.reshape(total // 2, few, nr))
        return results

    def to_lines(start):
        for parity, result in enumerate(receivers(start, forward)):
            lines[pl.ds(start, total // 2), :, parity * nr : (parity + 1) * nr] = result

    def to_estimate(start):
        even, odd = receivers(start, inverse)
        for lanes, result in ((slice(0, hr), even + odd), (slice(hr, nr), even - odd)):
            for part in range(2):
                e_all[part, pl.ds(start, total // 2), :, lanes] = result[
                    :, :, part * hr : (part + 1) * hr
                ].astype(jnp.bfloat16)

    weights = [math.sin(math.pi * (t + 0.5) / span) ** 2 for t in range(span)]

    def analyse(step):
        def window(j, carried):
            summed = jnp.zeros((few, LANES), jnp.float32)
            for c in columns:
                values = [
                    (
                        lines[j * block + t, :, c : c + LANES] * weights[t],
                        lines[j * block + t, :, hr + c : hr + c + LANES] * weights[t],
                    )
                    for t in range(span)
                ]
                for k, (real, imag) in enumerate(short_fourier(values, -1)):
                    power = real * real + imag * imag
                    summed = summed + power * lax.rsqrt(jnp.maximum(power, TINY))
                    coefs[j, k, :, c : c + LANES] = real
                    coefs[j, k, :, hr + c : hr + c + LANES] = imag
            near_sums[step, 0, pl.ds(j, 1), :] = jnp.sum(summed, axis=0, keepdims=True)
            return carried

        lax.fori_loop(0, n, window, 0)

    def thresholds(step):
        copies = [
            send(
                near_sums.at[step, 0],
                near_sums.at[step, k],
                near_send.at[step, k],
                near_recv.at[step, k],
                {"shot": peers[k]},
            )
            for k in order
        ]
        for copy in copies:
            copy.wait()
        part = near_sums[step, 0]
        for k in range(1, n):
            part = part + near_sums[step, k]
        far_sums[step, 0] = part
        copies = [
            send(
                far_sums.at[step, 0],
                far_sums.at[step, k],
                far_send.at[step, k],
                far_recv.at[step, k],
                {"freq": others[k]},
            )
            for k in range(1, nf)
        ]
        for copy in copies:
            copy.wait()
        for k in range(1, nf):
            part = part + far_sums[step, k]
        limit[...] = jnp.broadcast_to(jnp.sum(part, axis=1, keepdims=True), (n, LANES))

    scale = 1.0 / (span * nr)
    count = span * few * n * nf * nr

    def synthesise(j, carried):
        level = levels_ref[j].astype(jnp.float32) * (level_scale * scale / count)
        bound = limit[pl.ds(j, 1), :] * level
        for c in columns:
            values = []
            for k in range(span):
                real = coefs[j, k, :, c : c + LANES]
                imag = coefs[j, k, :, hr + c : hr + c + LANES]
                power = real * real + imag * imag
                factor = jnp.maximum(scale - bound * lax.rsqrt(power), 0.0)
                values.append((real * factor, imag * factor))
            for t, parts in enumerate(short_fourier(values, 1)):
                for part in range(2):
                    lanes = slice(part * hr + c, part * hr + c + LANES)
                    if t < block:
                        keep(j * block + t, lanes, parts[part] + carry[t, :, lanes])
                    else:
                        carry[t - block, :, lanes] = parts[part]
        return carried

    for step in range(PASSES):
        lax.fori_loop(0, half, relax, 0)
        for start in (0, total // 2):
            to_lines(start)
        analyse(step)
        thresholds(step)
        carry[...] = jnp.zeros_like(carry)
        lax.fori_loop(0, n, synthesise, 0)
        if step < PASSES - 1:
            for start in (0, total // 2):
                to_estimate(start)

    copies = []
    mine = me // half
    for side, group in ((1 - mine, range(half, n)), (mine, range(1, half))):
        start = side * (total // 2)
        to_estimate(start)
        for k in group:
            copies.append(
                send(
                    e_all.at[:, pl.ds(peers[k] * block, block)],
                    out_ref.at[:, :, pl.ds(me * few, few), :],
                    out_send.at[k],
                    out_recv.at[k],
                    {"shot": peers[k]},
                )
            )
    last = pltpu.make_async_copy(
        e_all.at[:, pl.ds(me * block, block)],
        out_ref.at[:, :, pl.ds(me * few, few), :],
        local_sem.at[0],
    )
    last.start()
    for copy in copies:
        copy.wait()
    last.wait()


def in_one_kernel(n, nf, blended, estimate, partner, delays, levels):
    block, freq_local, nr = estimate.shape[1:]
    few = freq_local // n
    total = n * block
    tables_both = fourier_matrices(nr)
    f32, bf16 = jnp.float32, jnp.bfloat16
    anywhere = pl.BlockSpec(memory_space=pl.ANY)
    dma = pltpu.SemaphoreType.DMA
    return pl.pallas_call(
        functools.partial(deblend_kernel, n, nf, block, few, nr),
        out_shape=jax.ShapeDtypeStruct(estimate.shape, estimate.dtype),
        in_specs=[anywhere] * 6,
        out_specs=anywhere,
        scratch_shapes=[
            pltpu.SMEM(partner.shape, jnp.int32),
            pltpu.SMEM(delays.shape, jnp.int32),
            pltpu.SMEM(levels.shape, jnp.int32),
            pltpu.VMEM((2, total, few, nr), bf16),
            pltpu.VMEM((2, total, few, nr), bf16),
            pltpu.VMEM((n, 8, LANES), jnp.int32),
            pltpu.VMEM((total, few, LANES), f32),
            pltpu.VMEM((total, few, LANES), f32),
            pltpu.VMEM((total, few, LANES), jnp.int32),
            pltpu.VMEM((total, few, 2 * nr), bf16),
            pltpu.VMEM((total, few, 2 * nr), bf16),
            pltpu.VMEM((total + block, few, 2 * nr), f32),
            pltpu.VMEM((n, 2 * block, few, 2 * nr), f32),
            pltpu.VMEM((block, few, 2 * nr), f32),
            pltpu.VMEM((n, LANES), f32),
            pltpu.VMEM((PASSES, n, n, LANES), f32),
            pltpu.VMEM((PASSES, nf, n, LANES), f32),
            pltpu.VMEM(tables_both.shape, f32),
            pltpu.VMEM(tables_both.shape, bf16),
            pltpu.VMEM(tables_both.shape, bf16),
            dma((6,)),
            dma((n,)),
            dma((n,)),
            dma((n,)),
            dma((n,)),
            dma((n,)),
            dma((n,)),
            dma((PASSES, n)),
            dma((PASSES, n)),
            dma((PASSES, nf)),
            dma((PASSES, nf)),
            dma((n,)),
            dma((n,)),
        ],
        compiler_params=pltpu.CompilerParams(
            collective_id=0, has_side_effects=True, vmem_limit_bytes=60 * 1024 * 1024
        ),
    )(blended, estimate, partner, delays, levels, jnp.asarray(tables_both))


def solution(mesh):
    n, nf = mesh.shape["shot"], mesh.shape["freq"]

    def body(blended, estimate, partner, delays, levels):
        block, freq_local, nr = estimate.shape[1:]
        whole_tiles = (
            n == 8 and freq_local % (16 * n) == 0 and nr % (2 * LANES) == 0 and n * block <= LANES
        )
        if whole_tiles:
            return in_one_kernel(n, nf, blended, estimate, partner, delays, levels)
        return on_device(blended, estimate, partner, delays, levels)

    return jax.shard_map(
        body,
        mesh=mesh,
        in_specs=(
            P(None, "shot", "freq", None),
            P(None, "shot", "freq", None),
            P("shot"),
            P(),
            P(),
        ),
        out_specs=P(None, "shot", "freq", None),
        check_vma=False,
    )
```

```python
import functools
import math

import jax
import jax.numpy as jnp
import numpy as np
from jax import lax
from jax.experimental import pallas as pl
from jax.experimental.pallas import tpu as pltpu
from jax.sharding import PartitionSpec as P

NF = 512
NT = 1024
PASSES = 2


relaxation = 0.5
level_scale = 0.25


def tables(length):
    indices = jnp.arange(length, dtype=jnp.int32)
    products = jnp.mod(indices[:, None] * indices[None, :], length)
    angles = 2.0 * math.pi / length * products.astype(jnp.float32)
    return (jnp.cos(angles), jnp.sin(angles))


def spectrum(real_part, imag_part, direction_sign, shot_cos, shot_sin, recv_cos, recv_sin):
    highest = lax.Precision.HIGHEST

    def receivers(values, table):
        return jnp.einsum("...n,nk->...k", values, table, precision=highest)

    def shots(values, table):
        return jnp.einsum("tk,...tfn->...kfn", table, values, precision=highest)

    first_real = receivers(real_part, recv_cos) + direction_sign * receivers(imag_part, recv_sin)
    first_imag = receivers(imag_part, recv_cos) - direction_sign * receivers(real_part, recv_sin)
    out_real = shots(first_real, shot_cos) + direction_sign * shots(first_imag, shot_sin)
    out_imag = shots(first_imag, shot_cos) - direction_sign * shots(first_real, shot_sin)
    scale = 1.0 / math.sqrt(shot_cos.shape[0] * recv_cos.shape[0])
    return (out_real * scale, out_imag * scale)


def shrink(real_part, imag_part, threshold):
    modulus = jnp.sqrt(real_part * real_part + imag_part * imag_part)
    factor = jnp.maximum(modulus - threshold, 0.0) / jnp.maximum(modulus, threshold)
    return (real_part * factor, imag_part * factor)


def phase_tables(offsets, frequency):
    phase_index = jnp.mod(frequency[None, :] * offsets[:, None], NT)
    angles = 2.0 * math.pi / NT * phase_index.astype(jnp.float32)
    return (jnp.cos(angles)[:, :, None], jnp.sin(angles)[:, :, None])


def relax_step(current, blended, partner_recs, phase_cos, phase_sin):
    shifted_real = partner_recs[0] * phase_cos + partner_recs[1] * phase_sin
    shifted_imag = partner_recs[1] * phase_cos - partner_recs[0] * phase_sin
    shifted = jnp.stack([shifted_real, shifted_imag])
    current_f = current.astype(jnp.float32)
    return current_f + relaxation * (blended.astype(jnp.float32) - current_f - shifted)


def whole_pass(
    current, blended, partner_all, phase_cos, phase_sin, level_all, taper, tables_all, block
):
    shot_cos, shot_sin, recv_cos, recv_sin = tables_all
    total_shots = current.shape[1]
    few_freq = current.shape[2]
    receivers_count = current.shape[3]
    count = total_shots // block
    partner_recs = jnp.take(current, partner_all, axis=1).astype(jnp.float32)
    updated = relax_step(current, blended, partner_recs, phase_cos, phase_sin)
    grouped = jnp.transpose(
        updated.reshape(2, count, block, few_freq, receivers_count), (1, 0, 2, 3, 4)
    )
    following = jnp.concatenate([grouped[1:], jnp.zeros_like(grouped[:1])], axis=0)
    segments = jnp.concatenate([grouped, following], axis=2) * taper[None, None, :, None, None]
    coef_real, coef_imag = spectrum(
        segments[:, 0], segments[:, 1], 1.0, shot_cos, shot_sin, recv_cos, recv_sin
    )
    modulus = jnp.sqrt(coef_real * coef_real + coef_imag * coef_imag)
    local_sum = jnp.sum(modulus, axis=(1, 2, 3))
    total_sum = lax.psum(local_sum, ("shot", "freq"))
    span = 2 * block
    threshold = (level_scale * level_all * total_sum / (span * NF * receivers_count))[
        :, None, None, None
    ]
    kept_real, kept_imag = shrink(coef_real, coef_imag, threshold)
    back_real, back_imag = spectrum(
        kept_real, kept_imag, -1.0, shot_cos, shot_sin, recv_cos, recv_sin
    )
    result = jnp.stack([back_real, back_imag], axis=1)
    firsts = result[:, :, :block]
    seconds = jnp.concatenate(
        [jnp.zeros_like(result[:1, :, block:]), result[:-1, :, block:]], axis=0
    )
    summed = firsts + seconds
    return (
        jnp.transpose(summed, (1, 0, 2, 3, 4))
        .reshape(2, total_shots, few_freq, receivers_count)
        .astype(jnp.bfloat16)
    )


def on_device(blended, estimate, partner, delays, levels):
    block = estimate.shape[1]
    freq_local = estimate.shape[2]
    receivers_count = estimate.shape[3]
    span = 2 * block
    steps_t = jnp.arange(span, dtype=jnp.float32)
    taper = jnp.sin(math.pi * (steps_t + 0.5) / span) ** 2
    shot_cos, shot_sin = tables(span)
    recv_cos, recv_sin = tables(receivers_count)
    tables_all = (shot_cos, shot_sin, recv_cos, recv_sin)
    blended_all, current = (
        lax.all_to_all(blended, "shot", split_axis=2, concat_axis=1, tiled=True),
        lax.all_to_all(estimate, "shot", split_axis=2, concat_axis=1, tiled=True),
    )
    few_freq = current.shape[2]
    partner_all = lax.all_gather(partner, "shot", axis=0, tiled=True)
    offsets = jnp.take(delays, partner_all) - delays
    frequency = (
        lax.axis_index("freq") * freq_local
        + lax.axis_index("shot") * few_freq
        + jnp.arange(few_freq, dtype=jnp.int32)
    )
    phase_cos, phase_sin = phase_tables(offsets, frequency)
    level_all = levels.astype(jnp.float32)
    for pass_index in range(PASSES):
        current = whole_pass(
            current,
            blended_all,
            partner_all,
            phase_cos,
            phase_sin,
            level_all,
            taper,
            tables_all,
            block,
        )
    return lax.all_to_all(current, "shot", split_axis=1, concat_axis=2, tiled=True)


LANES = 128
TINY = 1.1754944e-38


def fourier_matrices(length):
    half = np.arange(length // 2)

    def turns(parity):
        angles = 2.0 * np.pi / length * (np.outer(half, 2 * half + parity) % length)
        cos, sin = np.cos(angles), np.sin(angles)
        return np.block([[cos, -sin], [sin, cos]])

    forward = np.stack([turns(0), turns(1)]).astype(np.float32)
    return np.stack([forward, np.swapaxes(forward, 1, 2)])


def short_fourier(values, sign):
    count = len(values)
    if count == 1:
        return values
    even = short_fourier(values[0::2], sign)
    odd = short_fourier(values[1::2], sign)
    low, high = [], []
    for k in range(count // 2):
        real, imag = odd[k]
        if 4 * k == count:
            real, imag = (-imag, real) if sign > 0 else (imag, -real)
        elif 8 * k == count or 8 * k == 3 * count:
            half = math.sqrt(0.5)
            turned = (real - sign * imag, imag + sign * real)
            if 8 * k == 3 * count:
                turned = (-real - sign * imag, sign * real - imag)
            real, imag = turned[0] * half, turned[1] * half
        elif k:
            cos = math.cos(2.0 * math.pi * k / count)
            sin = sign * math.sin(2.0 * math.pi * k / count)
            real, imag = real * cos - imag * sin, imag * cos + real * sin
        low.append((even[k][0] + real, even[k][1] + imag))
        high.append((even[k][0] - real, even[k][1] - imag))
    return low + high


def flipped(index, mask, count):
    result, bit = 0, 1
    while bit < count:
        result = result + (index // bit + mask // bit) % 2 * bit
        bit *= 2
    return result


def deblend_kernel(
    n,
    nf,
    block,
    few,
    nr,
    blended_ref,
    estimate_ref,
    partner_hbm,
    delays_hbm,
    levels_hbm,
    tables_hbm,
    out_ref,
    partner_ref,
    delays_ref,
    levels_ref,
    e_all,
    b_all,
    info,
    turn_cos,
    turn_sin,
    turn_pick,
    x_hi,
    x_lo,
    lines,
    coefs,
    carry,
    limit,
    sums,
    exact,
    forward,
    inverse,
    local_sem,
    info_send,
    info_recv,
    e_send,
    e_recv,
    b_send,
    b_recv,
    sums_send,
    sums_recv,
    out_send,
    out_recv,
):
    total = n * block
    span = 2 * block
    half = n // 2
    hr = nr // 2
    columns = [parity * nr + c for parity in range(2) for c in range(0, hr, LANES)]
    me = lax.axis_index("shot")
    column = lax.axis_index("freq")
    mesh_id = pl.DeviceIdType.MESH
    peers = [flipped(me, k, n) for k in range(n)]
    order = [half] + [k for near in range(1, half) for k in (near + half, near)]
    others = [lax.rem(column + k, nf) for k in range(nf)]
    everyone = [(k, f) for k in order + [0] for f in range(nf) if (k, f) != (0, 0)]

    barrier = pltpu.get_barrier_semaphore()
    for k, f in everyone:
        where = {"shot": peers[k], "freq": others[f]}
        pl.semaphore_signal(barrier, inc=1, device_id=where, device_id_type=mesh_id)

    scalar_copies = [
        pltpu.make_async_copy(partner_hbm, partner_ref, local_sem.at[3]),
        pltpu.make_async_copy(delays_hbm, delays_ref, local_sem.at[4]),
        pltpu.make_async_copy(levels_hbm, levels_ref, local_sem.at[5]),
    ]
    for copy in scalar_copies:
        copy.start()
    local_copies = [
        pltpu.make_async_copy(tables_hbm, exact, local_sem.at[0]),
        pltpu.make_async_copy(
            estimate_ref.at[:, :, pl.ds(me * few, few), :],
            e_all.at[:, pl.ds(me * block, block)],
            local_sem.at[1],
        ),
        pltpu.make_async_copy(
            blended_ref.at[:, :, pl.ds(me * few, few), :],
            b_all.at[:, pl.ds(me * block, block)],
            local_sem.at[2],
        ),
    ]
    for copy in local_copies:
        copy.start()

    for copy in scalar_copies:
        copy.wait()
    lane = lax.broadcasted_iota(jnp.int32, (8, LANES), 1)
    row = lax.broadcasted_iota(jnp.int32, (8, LANES), 0)
    tile = jnp.zeros((8, LANES), jnp.int32)
    for i in range(block):
        own = me * block + i
        mate = partner_ref[i]
        offset = delays_ref[mate] - delays_ref[own]
        here = lane == own
        tile = jnp.where(here & (row == 0), mate, tile)
        tile = jnp.where(here & (row == 1), offset, tile)
    info[0] = tile

    pl.semaphore_wait(barrier, n * nf - 1)

    def send(source, target, send_sem, recv_sem, where):
        copy = pltpu.make_async_remote_copy(
            src_ref=source,
            dst_ref=target,
            send_sem=send_sem,
            recv_sem=recv_sem,
            device_id=where,
            device_id_type=mesh_id,
        )
        copy.start()
        return copy

    info_copies = [
        send(info.at[0], info.at[k], info_send.at[k], info_recv.at[k], {"shot": peers[k]})
        for k in order
    ]
    record_copies = {k: [] for k in range(n)}
    record_copies[0] = local_copies[1:]
    for k in order:
        for held, whole, sent, received in (
            (estimate_ref, e_all, e_send, e_recv),
            (blended_ref, b_all, b_send, b_recv),
        ):
            record_copies[k].append(
                send(
                    held.at[:, :, pl.ds(peers[k] * few, few), :],
                    whole.at[:, pl.ds(me * block, block)],
                    sent.at[k],
                    received.at[k],
                    {"shot": peers[k]},
                )
            )

    lines[pl.ds(total, block)] = jnp.zeros((block, few, 2 * nr), jnp.float32)
    for copy in info_copies:
        copy.wait()
    known = info[0]
    for k in range(1, n):
        known = known + info[k]
    frequency = (column * n + me) * few + lax.broadcasted_iota(jnp.int32, (few, LANES), 0)
    phase = (frequency * known[1:2, :]) & (NT - 1)
    angles = 2.0 * math.pi / NT * phase.astype(jnp.float32)
    cos_table = relaxation * jnp.cos(angles)
    sin_table = relaxation * jnp.sin(angles)
    for s in range(total):
        first = (s // block + half) % n * block
        turn_cos[s] = jnp.broadcast_to(cos_table[:, s : s + 1], (few, LANES))
        turn_sin[s] = jnp.broadcast_to(sin_table[:, s : s + 1], (few, LANES))
        turn_pick[s] = jnp.broadcast_to(known[0:1, s : s + 1] - first, (few, LANES))

    local_copies[0].wait()
    for index, pair in enumerate((forward, inverse)):
        top = exact[index].astype(jnp.bfloat16)
        pair[0] = top
        pair[1] = (exact[index] - top.astype(jnp.float32)).astype(jnp.bfloat16)

    def keep(s, lanes, value):
        top = value.astype(jnp.bfloat16)
        x_hi[s, :, lanes] = top
        x_lo[s, :, lanes] = (value - top.astype(jnp.float32)).astype(jnp.bfloat16)

    def relax(pair, carried):
        for c in range(0, hr, LANES):
            halves = (slice(c, c + LANES), slice(hr + c, hr + c + LANES))
            for side in range(2):
                first = (pair + side * half) * block
                other = (pair + (1 - side) * half) * block
                for i in range(block):
                    s = first + i
                    pick = turn_pick[s]
                    cos, sin = turn_cos[s], turn_sin[s]
                    moved = []
                    for lanes in halves:
                        mate_real = e_all[0, other, :, lanes].astype(jnp.float32)
                        mate_imag = e_all[1, other, :, lanes].astype(jnp.float32)
                        for j in range(1, block):
                            here = pick == j
                            real = e_all[0, other + j, :, lanes].astype(jnp.float32)
                            imag = e_all[1, other + j, :, lanes].astype(jnp.float32)
                            mate_real = jnp.where(here, real, mate_real)
                            mate_imag = jnp.where(here, imag, mate_imag)
                        real = e_all[0, s, :, lanes].astype(jnp.float32)
                        imag = e_all[1, s, :, lanes].astype(jnp.float32)
                        seen_real = b_all[0, s, :, lanes].astype(jnp.float32)
                        seen_imag = b_all[1, s, :, lanes].astype(jnp.float32)
                        shift_real = mate_real * cos + mate_imag * sin
                        shift_imag = mate_imag * cos - mate_real * sin
                        moved.append(
                            (
                                real + relaxation * (seen_real - real) - shift_real,
                                imag + relaxation * (seen_imag - imag) - shift_imag,
                            )
                        )
                    place = (2 * pair + side) * block + i
                    for part in range(2):
                        at = part * hr + c
                        keep(place, slice(at, at + LANES), moved[0][part] + moved[1][part])
                        at = nr + at
                        keep(place, slice(at, at + LANES), moved[0][part] - moved[1][part])
        return carried

    def receivers(start, shots, table):
        results = []
        for parity in range(2):
            lanes = slice(parity * nr, (parity + 1) * nr)
            top = x_hi[pl.ds(start, shots), :, lanes].reshape(shots * few, nr)
            rest = x_lo[pl.ds(start, shots), :, lanes].reshape(shots * few, nr)
            result = jnp.dot(top, table[0, parity], preferred_element_type=jnp.float32)
            result = result + jnp.dot(rest, table[0, parity], preferred_element_type=jnp.float32)
            result = result + jnp.dot(top, table[1, parity], preferred_element_type=jnp.float32)
            results.append(result.reshape(shots, few, nr))
        return results

    def to_lines(pair, pairs):
        for parity, result in enumerate(receivers(pair * span, pairs * span, forward)):
            lanes = slice(parity * nr, (parity + 1) * nr)
            for p in range(pairs):
                for side in range(2):
                    at = (2 * p + side) * block
                    target = pl.ds((pair + p + side * half) * block, block)
                    lines[target, :, lanes] = result[at : at + block]

    def to_estimate(start, shots):
        even, odd = receivers(start, shots, inverse)
        for lanes, result in ((slice(0, hr), even + odd), (slice(hr, nr), even - odd)):
            for part in range(2):
                e_all[part, pl.ds(start, shots), :, lanes] = result[
                    :, :, part * hr : (part + 1) * hr
                ].astype(jnp.bfloat16)

    weights = [math.sin(math.pi * (t + 0.5) / span) ** 2 for t in range(span)]

    def analyse(step):
        def window(j, carried):
            summed = jnp.zeros((few, LANES), jnp.float32)
            for c in columns:
                values = [
                    (
                        lines[j * block + t, :, c : c + LANES] * weights[t],
                        lines[j * block + t, :, hr + c : hr + c + LANES] * weights[t],
                    )
                    for t in range(span)
                ]
                for k, (real, imag) in enumerate(short_fourier(values, -1)):
                    power = real * real + imag * imag
                    summed = summed + power * lax.rsqrt(jnp.maximum(power, TINY))
                    coefs[j, k, :, c : c + LANES] = real
                    coefs[j, k, :, hr + c : hr + c + LANES] = imag
            limit[pl.ds(j, 1), :] = jnp.sum(summed, axis=0, keepdims=True)
            return carried

        lax.fori_loop(0, n, window, 0)

    diagonal = lax.broadcasted_iota(jnp.int32, (n, LANES), 0) == lax.broadcasted_iota(
        jnp.int32, (n, LANES), 1
    )

    def thresholds(step):
        column_sums = jnp.sum(limit[...], axis=1, keepdims=True)
        sums[step, 0] = jnp.sum(jnp.where(diagonal, column_sums, 0.0), axis=0, keepdims=True)
        copies = [
            send(
                sums.at[step, 0],
                sums.at[step, k * nf + f],
                sums_send.at[step, k * nf + f],
                sums_recv.at[step, k * nf + f],
                {"shot": peers[k], "freq": others[f]},
            )
            for k, f in everyone
        ]
        for copy in copies:
            copy.wait()
        whole = jnp.sum(sums[step], axis=0)
        column_sums = jnp.sum(jnp.where(diagonal, whole, 0.0), axis=1, keepdims=True)
        limit[...] = jnp.broadcast_to(column_sums, (n, LANES))

    scale = 1.0 / (span * nr)
    count = span * few * n * nf * nr

    def synthesise(j, carried):
        level = levels_ref[j].astype(jnp.float32) * (level_scale * scale / count)
        bound = limit[pl.ds(j, 1), :] * level
        for c in columns:
            values = []
            for k in range(span):
                real = coefs[j, k, :, c : c + LANES]
                imag = coefs[j, k, :, hr + c : hr + c + LANES]
                power = real * real + imag * imag
                factor = jnp.maximum(scale - bound * lax.rsqrt(power), 0.0)
                values.append((real * factor, imag * factor))
            for t, parts in enumerate(short_fourier(values, 1)):
                for part in range(2):
                    lanes = slice(part * hr + c, part * hr + c + LANES)
                    if t < block:
                        keep(j * block + t, lanes, parts[part] + carry[t, :, lanes])
                    else:
                        carry[t - block, :, lanes] = parts[part]
        return carried

    for step in range(PASSES):
        if step == 0:
            for near in range(half):
                for copy in record_copies[near] + record_copies[near + half]:
                    copy.wait()
                pair = peers[near] % half
                relax(pair, 0)
                to_lines(pair, 1)
        else:
            lax.fori_loop(0, half, relax, 0)
            for pair in range(0, half, half // 2):
                to_lines(pair, half // 2)
        analyse(step)
        thresholds(step)
        carry[...] = jnp.zeros_like(carry)
        lax.fori_loop(0, n, synthesise, 0)
        if step < PASSES - 1:
            for start in (0, total // 2):
                to_estimate(start, total // 2)

    copies = []
    for group in [(k, k + 1) for k in range(half, n, 2)] + [(2, 3), (0, 1)]:
        to_estimate(peers[group[0]] // 2 * 2 * block, 2 * block)
        for k in group:
            if k:
                copies.append(
                    send(
                        e_all.at[:, pl.ds(peers[k] * block, block)],
                        out_ref.at[:, :, pl.ds(me * few, few), :],
                        out_send.at[k],
                        out_recv.at[k],
                        {"shot": peers[k]},
                    )
                )
    last = pltpu.make_async_copy(
        e_all.at[:, pl.ds(me * block, block)],
        out_ref.at[:, :, pl.ds(me * few, few), :],
        local_sem.at[0],
    )
    last.start()
    for copy in copies:
        copy.wait()
    last.wait()


def in_one_kernel(n, nf, blended, estimate, partner, delays, levels):
    block, freq_local, nr = estimate.shape[1:]
    few = freq_local // n
    total = n * block
    tables_both = fourier_matrices(nr)
    f32, bf16 = jnp.float32, jnp.bfloat16
    anywhere = pl.BlockSpec(memory_space=pl.ANY)
    dma = pltpu.SemaphoreType.DMA
    return pl.pallas_call(
        functools.partial(deblend_kernel, n, nf, block, few, nr),
        out_shape=jax.ShapeDtypeStruct(estimate.shape, estimate.dtype),
        in_specs=[anywhere] * 6,
        out_specs=anywhere,
        scratch_shapes=[
            pltpu.SMEM(partner.shape, jnp.int32),
            pltpu.SMEM(delays.shape, jnp.int32),
            pltpu.SMEM(levels.shape, jnp.int32),
            pltpu.VMEM((2, total, few, nr), bf16),
            pltpu.VMEM((2, total, few, nr), bf16),
            pltpu.VMEM((n, 8, LANES), jnp.int32),
            pltpu.VMEM((total, few, LANES), f32),
            pltpu.VMEM((total, few, LANES), f32),
            pltpu.VMEM((total, few, LANES), jnp.int32),
            pltpu.VMEM((total, few, 2 * nr), bf16),
            pltpu.VMEM((total, few, 2 * nr), bf16),
            pltpu.VMEM((total + block, few, 2 * nr), f32),
            pltpu.VMEM((n, 2 * block, few, 2 * nr), f32),
            pltpu.VMEM((block, few, 2 * nr), f32),
            pltpu.VMEM((n, LANES), f32),
            pltpu.VMEM((PASSES, n * nf, 1, LANES), f32),
            pltpu.VMEM(tables_both.shape, f32),
            pltpu.VMEM(tables_both.shape, bf16),
            pltpu.VMEM(tables_both.shape, bf16),
            dma((6,)),
            dma((n,)),
            dma((n,)),
            dma((n,)),
            dma((n,)),
            dma((n,)),
            dma((n,)),
            dma((PASSES, n * nf)),
            dma((PASSES, n * nf)),
            dma((n,)),
            dma((n,)),
        ],
        compiler_params=pltpu.CompilerParams(
            collective_id=0, has_side_effects=True, vmem_limit_bytes=60 * 1024 * 1024
        ),
    )(blended, estimate, partner, delays, levels, jnp.asarray(tables_both))


def solution(mesh):
    n, nf = mesh.shape["shot"], mesh.shape["freq"]

    def body(blended, estimate, partner, delays, levels):
        block, freq_local, nr = estimate.shape[1:]
        whole_tiles = (
            n == 8 and freq_local % (16 * n) == 0 and nr % (2 * LANES) == 0 and n * block <= LANES
        )
        if whole_tiles:
            return in_one_kernel(n, nf, blended, estimate, partner, delays, levels)
        return on_device(blended, estimate, partner, delays, levels)

    return jax.shard_map(
        body,
        mesh=mesh,
        in_specs=(
            P(None, "shot", "freq", None),
            P(None, "shot", "freq", None),
            P("shot"),
            P(),
            P(),
        ),
        out_specs=P(None, "shot", "freq", None),
        check_vma=False,
    )
```

```python
import functools
import math

import jax
import jax.numpy as jnp
import numpy as np
from jax import lax
from jax.experimental import pallas as pl
from jax.experimental.pallas import tpu as pltpu
from jax.sharding import PartitionSpec as P

NF = 512
NT = 1024
PASSES = 2


relaxation = 0.5
level_scale = 0.25


def tables(length):
    indices = jnp.arange(length, dtype=jnp.int32)
    products = jnp.mod(indices[:, None] * indices[None, :], length)
    angles = 2.0 * math.pi / length * products.astype(jnp.float32)
    return (jnp.cos(angles), jnp.sin(angles))


def spectrum(real_part, imag_part, direction_sign, shot_cos, shot_sin, recv_cos, recv_sin):
    highest = lax.Precision.HIGHEST

    def receivers(values, table):
        return jnp.einsum("...n,nk->...k", values, table, precision=highest)

    def shots(values, table):
        return jnp.einsum("tk,...tfn->...kfn", table, values, precision=highest)

    first_real = receivers(real_part, recv_cos) + direction_sign * receivers(imag_part, recv_sin)
    first_imag = receivers(imag_part, recv_cos) - direction_sign * receivers(real_part, recv_sin)
    out_real = shots(first_real, shot_cos) + direction_sign * shots(first_imag, shot_sin)
    out_imag = shots(first_imag, shot_cos) - direction_sign * shots(first_real, shot_sin)
    scale = 1.0 / math.sqrt(shot_cos.shape[0] * recv_cos.shape[0])
    return (out_real * scale, out_imag * scale)


def shrink(real_part, imag_part, threshold):
    modulus = jnp.sqrt(real_part * real_part + imag_part * imag_part)
    factor = jnp.maximum(modulus - threshold, 0.0) / jnp.maximum(modulus, threshold)
    return (real_part * factor, imag_part * factor)


def phase_tables(offsets, frequency):
    phase_index = jnp.mod(frequency[None, :] * offsets[:, None], NT)
    angles = 2.0 * math.pi / NT * phase_index.astype(jnp.float32)
    return (jnp.cos(angles)[:, :, None], jnp.sin(angles)[:, :, None])


def relax_step(current, blended, partner_recs, phase_cos, phase_sin):
    shifted_real = partner_recs[0] * phase_cos + partner_recs[1] * phase_sin
    shifted_imag = partner_recs[1] * phase_cos - partner_recs[0] * phase_sin
    shifted = jnp.stack([shifted_real, shifted_imag])
    current_f = current.astype(jnp.float32)
    return current_f + relaxation * (blended.astype(jnp.float32) - current_f - shifted)


def whole_pass(
    current, blended, partner_all, phase_cos, phase_sin, level_all, taper, tables_all, block
):
    shot_cos, shot_sin, recv_cos, recv_sin = tables_all
    total_shots = current.shape[1]
    few_freq = current.shape[2]
    receivers_count = current.shape[3]
    count = total_shots // block
    partner_recs = jnp.take(current, partner_all, axis=1).astype(jnp.float32)
    updated = relax_step(current, blended, partner_recs, phase_cos, phase_sin)
    grouped = jnp.transpose(
        updated.reshape(2, count, block, few_freq, receivers_count), (1, 0, 2, 3, 4)
    )
    following = jnp.concatenate([grouped[1:], jnp.zeros_like(grouped[:1])], axis=0)
    segments = jnp.concatenate([grouped, following], axis=2) * taper[None, None, :, None, None]
    coef_real, coef_imag = spectrum(
        segments[:, 0], segments[:, 1], 1.0, shot_cos, shot_sin, recv_cos, recv_sin
    )
    modulus = jnp.sqrt(coef_real * coef_real + coef_imag * coef_imag)
    local_sum = jnp.sum(modulus, axis=(1, 2, 3))
    total_sum = lax.psum(local_sum, ("shot", "freq"))
    span = 2 * block
    threshold = (level_scale * level_all * total_sum / (span * NF * receivers_count))[
        :, None, None, None
    ]
    kept_real, kept_imag = shrink(coef_real, coef_imag, threshold)
    back_real, back_imag = spectrum(
        kept_real, kept_imag, -1.0, shot_cos, shot_sin, recv_cos, recv_sin
    )
    result = jnp.stack([back_real, back_imag], axis=1)
    firsts = result[:, :, :block]
    seconds = jnp.concatenate(
        [jnp.zeros_like(result[:1, :, block:]), result[:-1, :, block:]], axis=0
    )
    summed = firsts + seconds
    return (
        jnp.transpose(summed, (1, 0, 2, 3, 4))
        .reshape(2, total_shots, few_freq, receivers_count)
        .astype(jnp.bfloat16)
    )


def on_device(blended, estimate, partner, delays, levels):
    block = estimate.shape[1]
    freq_local = estimate.shape[2]
    receivers_count = estimate.shape[3]
    span = 2 * block
    steps_t = jnp.arange(span, dtype=jnp.float32)
    taper = jnp.sin(math.pi * (steps_t + 0.5) / span) ** 2
    shot_cos, shot_sin = tables(span)
    recv_cos, recv_sin = tables(receivers_count)
    tables_all = (shot_cos, shot_sin, recv_cos, recv_sin)
    blended_all, current = (
        lax.all_to_all(blended, "shot", split_axis=2, concat_axis=1, tiled=True),
        lax.all_to_all(estimate, "shot", split_axis=2, concat_axis=1, tiled=True),
    )
    few_freq = current.shape[2]
    partner_all = lax.all_gather(partner, "shot", axis=0, tiled=True)
    offsets = jnp.take(delays, partner_all) - delays
    frequency = (
        lax.axis_index("freq") * freq_local
        + lax.axis_index("shot") * few_freq
        + jnp.arange(few_freq, dtype=jnp.int32)
    )
    phase_cos, phase_sin = phase_tables(offsets, frequency)
    level_all = levels.astype(jnp.float32)
    for pass_index in range(PASSES):
        current = whole_pass(
            current,
            blended_all,
            partner_all,
            phase_cos,
            phase_sin,
            level_all,
            taper,
            tables_all,
            block,
        )
    return lax.all_to_all(current, "shot", split_axis=1, concat_axis=2, tiled=True)


LANES = 128
TINY = 1.1754944e-38


def fourier_matrices(length):
    half = np.arange(length // 2)

    def turns(parity):
        angles = 2.0 * np.pi / length * (np.outer(half, 2 * half + parity) % length)
        cos, sin = np.cos(angles), np.sin(angles)
        return np.block([[cos, -sin], [sin, cos]])

    forward = np.stack([turns(0), turns(1)]).astype(np.float32)
    return np.stack([forward, np.swapaxes(forward, 1, 2)])


def short_fourier(values, sign):
    count = len(values)
    if count == 1:
        return values
    even = short_fourier(values[0::2], sign)
    odd = short_fourier(values[1::2], sign)
    low, high = [], []
    for k in range(count // 2):
        real, imag = odd[k]
        if 4 * k == count:
            real, imag = (-imag, real) if sign > 0 else (imag, -real)
        elif 8 * k == count or 8 * k == 3 * count:
            half = math.sqrt(0.5)
            turned = (real - sign * imag, imag + sign * real)
            if 8 * k == 3 * count:
                turned = (-real - sign * imag, sign * real - imag)
            real, imag = turned[0] * half, turned[1] * half
        elif k:
            cos = math.cos(2.0 * math.pi * k / count)
            sin = sign * math.sin(2.0 * math.pi * k / count)
            real, imag = real * cos - imag * sin, imag * cos + real * sin
        low.append((even[k][0] + real, even[k][1] + imag))
        high.append((even[k][0] - real, even[k][1] - imag))
    return low + high


def flipped(index, mask, count):
    result, bit = 0, 1
    while bit < count:
        result = result + (index // bit + mask // bit) % 2 * bit
        bit *= 2
    return result


def deblend_kernel(
    n,
    nf,
    block,
    few,
    nr,
    blended_ref,
    estimate_ref,
    partner_hbm,
    delays_hbm,
    levels_hbm,
    tables_hbm,
    out_ref,
    partner_ref,
    delays_ref,
    levels_ref,
    e_all,
    b_all,
    info,
    turn_cos,
    turn_sin,
    turn_pick,
    x,
    lines,
    coefs,
    carry,
    limit,
    sums,
    exact,
    forward,
    inverse,
    local_sem,
    info_send,
    info_recv,
    e_send,
    e_recv,
    b_send,
    b_recv,
    sums_send,
    sums_recv,
    out_send,
    out_recv,
):
    total = n * block
    span = 2 * block
    half = n // 2
    hr = nr // 2
    columns = [(parity, c) for parity in range(2) for c in range(0, hr, LANES)]
    me = lax.axis_index("shot")
    column = lax.axis_index("freq")
    mesh_id = pl.DeviceIdType.MESH
    peers = [flipped(me, k, n) for k in range(n)]
    order = [half] + [k for near in range(1, half) for k in (near + half, near)]
    others = [lax.rem(column + k, nf) for k in range(nf)]
    everyone = [(k, f) for k in order + [0] for f in range(nf) if (k, f) != (0, 0)]

    barrier = pltpu.get_barrier_semaphore()
    for k, f in everyone:
        where = {"shot": peers[k], "freq": others[f]}
        pl.semaphore_signal(barrier, inc=1, device_id=where, device_id_type=mesh_id)

    scalar_copies = [
        pltpu.make_async_copy(partner_hbm, partner_ref, local_sem.at[3]),
        pltpu.make_async_copy(delays_hbm, delays_ref, local_sem.at[4]),
        pltpu.make_async_copy(levels_hbm, levels_ref, local_sem.at[5]),
    ]
    for copy in scalar_copies:
        copy.start()
    local_copies = [
        pltpu.make_async_copy(tables_hbm, exact, local_sem.at[0]),
        pltpu.make_async_copy(
            estimate_ref.at[:, :, pl.ds(me * few, few), :],
            e_all.at[:, pl.ds(me * block, block)],
            local_sem.at[1],
        ),
        pltpu.make_async_copy(
            blended_ref.at[:, :, pl.ds(me * few, few), :],
            b_all.at[:, pl.ds(me * block, block)],
            local_sem.at[2],
        ),
    ]
    for copy in local_copies:
        copy.start()

    for copy in scalar_copies:
        copy.wait()
    lane = lax.broadcasted_iota(jnp.int32, (8, LANES), 1)
    row = lax.broadcasted_iota(jnp.int32, (8, LANES), 0)
    tile = jnp.zeros((8, LANES), jnp.int32)
    for i in range(block):
        own = me * block + i
        mate = partner_ref[i]
        offset = delays_ref[mate] - delays_ref[own]
        here = lane == own
        tile = jnp.where(here & (row == 0), mate, tile)
        tile = jnp.where(here & (row == 1), offset, tile)
    info[0] = tile

    pl.semaphore_wait(barrier, n * nf - 1)

    def send(source, target, send_sem, recv_sem, where):
        copy = pltpu.make_async_remote_copy(
            src_ref=source,
            dst_ref=target,
            send_sem=send_sem,
            recv_sem=recv_sem,
            device_id=where,
            device_id_type=mesh_id,
        )
        copy.start()
        return copy

    info_copies = [
        send(info.at[0], info.at[k], info_send.at[k], info_recv.at[k], {"shot": peers[k]})
        for k in order
    ]
    record_copies = {k: [] for k in range(n)}
    record_copies[0] = local_copies[1:]
    for k in order:
        for held, whole, sent, received in (
            (estimate_ref, e_all, e_send, e_recv),
            (blended_ref, b_all, b_send, b_recv),
        ):
            record_copies[k].append(
                send(
                    held.at[:, :, pl.ds(peers[k] * few, few), :],
                    whole.at[:, pl.ds(me * block, block)],
                    sent.at[k],
                    received.at[k],
                    {"shot": peers[k]},
                )
            )

    lines[pl.ds(total, block)] = jnp.zeros((block, few, 2 * nr), jnp.float32)
    for copy in info_copies:
        copy.wait()
    known = info[0]
    for k in range(1, n):
        known = known + info[k]
    frequency = (column * n + me) * few + lax.broadcasted_iota(jnp.int32, (few, LANES), 0)
    phase = (frequency * known[1:2, :]) & (NT - 1)
    angles = 2.0 * math.pi / NT * phase.astype(jnp.float32)
    cos_table = relaxation * jnp.cos(angles)
    sin_table = relaxation * jnp.sin(angles)
    for s in range(total):
        first = (s // block + half) % n * block
        turn_cos[s] = jnp.broadcast_to(cos_table[:, s : s + 1], (few, LANES))
        turn_sin[s] = jnp.broadcast_to(sin_table[:, s : s + 1], (few, LANES))
        turn_pick[s] = jnp.broadcast_to(known[0:1, s : s + 1] - first, (few, LANES))

    local_copies[0].wait()
    for index, stack in enumerate((forward, inverse)):
        top = exact[index].astype(jnp.bfloat16)
        stack[:, :nr] = top
        stack[:, nr : 2 * nr] = top
        stack[:, 2 * nr :] = (exact[index] - top.astype(jnp.float32)).astype(jnp.bfloat16)

    def keep(s, parity, at, value):
        start = 2 * nr * parity + at
        top = value.astype(jnp.bfloat16)
        x[s, :, start : start + LANES] = top
        rest = value - top.astype(jnp.float32)
        x[s, :, start + nr : start + nr + LANES] = rest.astype(jnp.bfloat16)

    def relax(pair, carried):
        for c in range(0, hr, LANES):
            halves = (slice(c, c + LANES), slice(hr + c, hr + c + LANES))
            for side in range(2):
                first = (pair + side * half) * block
                other = (pair + (1 - side) * half) * block
                for i in range(block):
                    s = first + i
                    pick = turn_pick[s]
                    cos, sin = turn_cos[s], turn_sin[s]
                    moved = []
                    for lanes in halves:
                        mate_real = e_all[0, other, :, lanes].astype(jnp.float32)
                        mate_imag = e_all[1, other, :, lanes].astype(jnp.float32)
                        for j in range(1, block):
                            here = pick == j
                            real = e_all[0, other + j, :, lanes].astype(jnp.float32)
                            imag = e_all[1, other + j, :, lanes].astype(jnp.float32)
                            mate_real = jnp.where(here, real, mate_real)
                            mate_imag = jnp.where(here, imag, mate_imag)
                        real = e_all[0, s, :, lanes].astype(jnp.float32)
                        imag = e_all[1, s, :, lanes].astype(jnp.float32)
                        seen_real = b_all[0, s, :, lanes].astype(jnp.float32)
                        seen_imag = b_all[1, s, :, lanes].astype(jnp.float32)
                        shift_real = mate_real * cos + mate_imag * sin
                        shift_imag = mate_imag * cos - mate_real * sin
                        moved.append(
                            (
                                real + relaxation * (seen_real - real) - shift_real,
                                imag + relaxation * (seen_imag - imag) - shift_imag,
                            )
                        )
                    place = (2 * pair + side) * block + i
                    for part in range(2):
                        at = part * hr + c
                        keep(place, 0, at, moved[0][part] + moved[1][part])
                        keep(place, 1, at, moved[0][part] - moved[1][part])
        return carried

    def receivers(start, shots, table):
        results = []
        for parity in range(2):
            start_lane = 2 * nr * parity
            both = x[pl.ds(start, shots), :, start_lane : start_lane + 2 * nr]
            both = both.reshape(shots * few, 2 * nr)
            rows = jnp.concatenate([both, both[:, :nr]], axis=1)
            result = jnp.dot(rows, table[parity], preferred_element_type=jnp.float32)
            results.append(result.reshape(shots, few, nr))
        return results

    def to_lines(pair, pairs):
        for parity, result in enumerate(receivers(pair * span, pairs * span, forward)):
            lanes = slice(parity * nr, (parity + 1) * nr)
            for p in range(pairs):
                for side in range(2):
                    at = (2 * p + side) * block
                    target = pl.ds((pair + p + side * half) * block, block)
                    lines[target, :, lanes] = result[at : at + block]

    def to_estimate(start, shots):
        even, odd = receivers(start, shots, inverse)
        for lanes, result in ((slice(0, hr), even + odd), (slice(hr, nr), even - odd)):
            for part in range(2):
                e_all[part, pl.ds(start, shots), :, lanes] = result[
                    :, :, part * hr : (part + 1) * hr
                ].astype(jnp.bfloat16)

    weights = [math.sin(math.pi * (t + 0.5) / span) ** 2 for t in range(span)]

    def analyse(step):
        def window(j, carried):
            summed = jnp.zeros((few, LANES), jnp.float32)
            for parity, c in columns:
                c += parity * nr
                values = [
                    (
                        lines[j * block + t, :, c : c + LANES] * weights[t],
                        lines[j * block + t, :, hr + c : hr + c + LANES] * weights[t],
                    )
                    for t in range(span)
                ]
                for k, (real, imag) in enumerate(short_fourier(values, -1)):
                    power = real * real + imag * imag
                    summed = summed + power * lax.rsqrt(jnp.maximum(power, TINY))
                    coefs[j, k, :, c : c + LANES] = real
                    coefs[j, k, :, hr + c : hr + c + LANES] = imag
            limit[pl.ds(j, 1), :] = jnp.sum(summed, axis=0, keepdims=True)
            return carried

        lax.fori_loop(0, n, window, 0)

    departures = []
    diagonal = lax.broadcasted_iota(jnp.int32, (n, LANES), 0) == lax.broadcasted_iota(
        jnp.int32, (n, LANES), 1
    )

    def thresholds(step):
        column_sums = jnp.sum(limit[...], axis=1, keepdims=True)
        sums[step, 0] = jnp.sum(jnp.where(diagonal, column_sums, 0.0), axis=0, keepdims=True)
        for k, f in everyone:
            send(
                sums.at[step, 0],
                sums.at[step, k * nf + f],
                sums_send.at[step],
                sums_recv.at[step],
                {"shot": peers[k], "freq": others[f]},
            )
        rows = sums.at[step, pl.ds(1, n * nf - 1)]
        arrived = pltpu.make_async_remote_copy(
            src_ref=rows,
            dst_ref=rows,
            send_sem=sums_send.at[step],
            recv_sem=sums_recv.at[step],
            device_id={"shot": peers[1]},
            device_id_type=mesh_id,
        )
        arrived.wait_recv()
        departures.append(arrived)
        whole = jnp.sum(sums[step], axis=0)
        column_sums = jnp.sum(jnp.where(diagonal, whole, 0.0), axis=1, keepdims=True)
        limit[...] = jnp.broadcast_to(column_sums, (n, LANES))

    scale = 1.0 / (span * nr)
    count = span * few * n * nf * nr

    def synthesise(j, carried):
        level = levels_ref[j].astype(jnp.float32) * (level_scale * scale / count)
        bound = limit[pl.ds(j, 1), :] * level
        for parity, c in columns:
            c += parity * nr
            values = []
            for k in range(span):
                real = coefs[j, k, :, c : c + LANES]
                imag = coefs[j, k, :, hr + c : hr + c + LANES]
                power = real * real + imag * imag
                factor = jnp.maximum(scale - bound * lax.rsqrt(power), 0.0)
                values.append((real * factor, imag * factor))
            for t, parts in enumerate(short_fourier(values, 1)):
                for part in range(2):
                    lanes = slice(part * hr + c, part * hr + c + LANES)
                    if t < block:
                        value = parts[part] + carry[t, :, lanes]
                        keep(j * block + t, parity, part * hr + c - parity * nr, value)
                    else:
                        carry[t - block, :, lanes] = parts[part]
        return carried

    for step in range(PASSES):
        if step == 0:
            for near in range(half):
                for copy in record_copies[near] + record_copies[near + half]:
                    copy.wait()
                pair = peers[near] % half
                relax(pair, 0)
                to_lines(pair, 1)
        else:
            lax.fori_loop(0, half, relax, 0)
            for pair in range(0, half, half // 2):
                to_lines(pair, half // 2)
        analyse(step)
        thresholds(step)
        carry[...] = jnp.zeros_like(carry)
        lax.fori_loop(0, n, synthesise, 0)
        if step < PASSES - 1:
            for start in (0, total // 2):
                to_estimate(start, total // 2)

    copies = []
    for group in [(k, k + 1) for k in range(half, n, 2)] + [(2, 3), (0, 1)]:
        to_estimate(peers[group[0]] // 2 * 2 * block, 2 * block)
        for k in group:
            if k:
                copies.append(
                    send(
                        e_all.at[:, pl.ds(peers[k] * block, block)],
                        out_ref.at[:, :, pl.ds(me * few, few), :],
                        out_send.at[k],
                        out_recv.at[k],
                        {"shot": peers[k]},
                    )
                )
    last = pltpu.make_async_copy(
        e_all.at[:, pl.ds(me * block, block)],
        out_ref.at[:, :, pl.ds(me * few, few), :],
        local_sem.at[0],
    )
    last.start()
    for copy in copies:
        copy.wait()
    for copy in departures:
        copy.wait_send()
    last.wait()


def in_one_kernel(n, nf, blended, estimate, partner, delays, levels):
    block, freq_local, nr = estimate.shape[1:]
    few = freq_local // n
    total = n * block
    tables_both = fourier_matrices(nr)
    f32, bf16 = jnp.float32, jnp.bfloat16
    in_hbm = pl.BlockSpec(memory_space=pltpu.HBM)
    dma = pltpu.SemaphoreType.DMA
    return pl.pallas_call(
        functools.partial(deblend_kernel, n, nf, block, few, nr),
        out_shape=jax.ShapeDtypeStruct(estimate.shape, estimate.dtype),
        in_specs=[in_hbm] * 6,
        out_specs=pl.BlockSpec(memory_space=pl.ANY),
        scratch_shapes=[
            pltpu.SMEM(partner.shape, jnp.int32),
            pltpu.SMEM(delays.shape, jnp.int32),
            pltpu.SMEM(levels.shape, jnp.int32),
            pltpu.VMEM((2, total, few, nr), bf16),
            pltpu.VMEM((2, total, few, nr), bf16),
            pltpu.VMEM((n, 8, LANES), jnp.int32),
            pltpu.VMEM((total, few, LANES), f32),
            pltpu.VMEM((total, few, LANES), f32),
            pltpu.VMEM((total, few, LANES), jnp.int32),
            pltpu.VMEM((total, few, 4 * nr), bf16),
            pltpu.VMEM((total + block, few, 2 * nr), f32),
            pltpu.VMEM((n, 2 * block, few, 2 * nr), f32),
            pltpu.VMEM((block, few, 2 * nr), f32),
            pltpu.VMEM((n, LANES), f32),
            pltpu.VMEM((PASSES, n * nf, 1, LANES), f32),
            pltpu.VMEM(tables_both.shape, f32),
            pltpu.VMEM((2, 3 * nr, nr), bf16),
            pltpu.VMEM((2, 3 * nr, nr), bf16),
            dma((6,)),
            dma((n,)),
            dma((n,)),
            dma((n,)),
            dma((n,)),
            dma((n,)),
            dma((n,)),
            dma((PASSES,)),
            dma((PASSES,)),
            dma((n,)),
            dma((n,)),
        ],
        compiler_params=pltpu.CompilerParams(
            collective_id=0, has_side_effects=True, vmem_limit_bytes=40 * 1024 * 1024
        ),
    )(blended, estimate, partner, delays, levels, jnp.asarray(tables_both))


def solution(mesh):
    n, nf = mesh.shape["shot"], mesh.shape["freq"]

    def body(blended, estimate, partner, delays, levels):
        block, freq_local, nr = estimate.shape[1:]
        whole_tiles = (
            n == 8 and freq_local % (16 * n) == 0 and nr % (2 * LANES) == 0 and n * block <= LANES
        )
        if whole_tiles:
            return in_one_kernel(n, nf, blended, estimate, partner, delays, levels)
        return on_device(blended, estimate, partner, delays, levels)

    return jax.shard_map(
        body,
        mesh=mesh,
        in_specs=(
            P(None, "shot", "freq", None),
            P(None, "shot", "freq", None),
            P("shot"),
            P(),
            P(),
        ),
        out_specs=P(None, "shot", "freq", None),
        check_vma=False,
    )
```

```python
import functools
import math

import jax
import jax.numpy as jnp
import numpy as np
from jax import lax
from jax.experimental import pallas as pl
from jax.experimental.pallas import tpu as pltpu
from jax.sharding import PartitionSpec as P

NF = 512
NT = 1024
PASSES = 2


relaxation = 0.5
level_scale = 0.25


def tables(length):
    indices = jnp.arange(length, dtype=jnp.int32)
    products = jnp.mod(indices[:, None] * indices[None, :], length)
    angles = 2.0 * math.pi / length * products.astype(jnp.float32)
    return (jnp.cos(angles), jnp.sin(angles))


def spectrum(real_part, imag_part, direction_sign, shot_cos, shot_sin, recv_cos, recv_sin):
    highest = lax.Precision.HIGHEST

    def receivers(values, table):
        return jnp.einsum("...n,nk->...k", values, table, precision=highest)

    def shots(values, table):
        return jnp.einsum("tk,...tfn->...kfn", table, values, precision=highest)

    first_real = receivers(real_part, recv_cos) + direction_sign * receivers(imag_part, recv_sin)
    first_imag = receivers(imag_part, recv_cos) - direction_sign * receivers(real_part, recv_sin)
    out_real = shots(first_real, shot_cos) + direction_sign * shots(first_imag, shot_sin)
    out_imag = shots(first_imag, shot_cos) - direction_sign * shots(first_real, shot_sin)
    scale = 1.0 / math.sqrt(shot_cos.shape[0] * recv_cos.shape[0])
    return (out_real * scale, out_imag * scale)


def shrink(real_part, imag_part, threshold):
    modulus = jnp.sqrt(real_part * real_part + imag_part * imag_part)
    factor = jnp.maximum(modulus - threshold, 0.0) / jnp.maximum(modulus, threshold)
    return (real_part * factor, imag_part * factor)


def phase_tables(offsets, frequency):
    phase_index = jnp.mod(frequency[None, :] * offsets[:, None], NT)
    angles = 2.0 * math.pi / NT * phase_index.astype(jnp.float32)
    return (jnp.cos(angles)[:, :, None], jnp.sin(angles)[:, :, None])


def relax_step(current, blended, partner_recs, phase_cos, phase_sin):
    shifted_real = partner_recs[0] * phase_cos + partner_recs[1] * phase_sin
    shifted_imag = partner_recs[1] * phase_cos - partner_recs[0] * phase_sin
    shifted = jnp.stack([shifted_real, shifted_imag])
    current_f = current.astype(jnp.float32)
    return current_f + relaxation * (blended.astype(jnp.float32) - current_f - shifted)


def whole_pass(
    current, blended, partner_all, phase_cos, phase_sin, level_all, taper, tables_all, block
):
    shot_cos, shot_sin, recv_cos, recv_sin = tables_all
    total_shots = current.shape[1]
    few_freq = current.shape[2]
    receivers_count = current.shape[3]
    count = total_shots // block
    partner_recs = jnp.take(current, partner_all, axis=1).astype(jnp.float32)
    updated = relax_step(current, blended, partner_recs, phase_cos, phase_sin)
    grouped = jnp.transpose(
        updated.reshape(2, count, block, few_freq, receivers_count), (1, 0, 2, 3, 4)
    )
    following = jnp.concatenate([grouped[1:], jnp.zeros_like(grouped[:1])], axis=0)
    segments = jnp.concatenate([grouped, following], axis=2) * taper[None, None, :, None, None]
    coef_real, coef_imag = spectrum(
        segments[:, 0], segments[:, 1], 1.0, shot_cos, shot_sin, recv_cos, recv_sin
    )
    modulus = jnp.sqrt(coef_real * coef_real + coef_imag * coef_imag)
    local_sum = jnp.sum(modulus, axis=(1, 2, 3))
    total_sum = lax.psum(local_sum, ("shot", "freq"))
    span = 2 * block
    threshold = (level_scale * level_all * total_sum / (span * NF * receivers_count))[
        :, None, None, None
    ]
    kept_real, kept_imag = shrink(coef_real, coef_imag, threshold)
    back_real, back_imag = spectrum(
        kept_real, kept_imag, -1.0, shot_cos, shot_sin, recv_cos, recv_sin
    )
    result = jnp.stack([back_real, back_imag], axis=1)
    firsts = result[:, :, :block]
    seconds = jnp.concatenate(
        [jnp.zeros_like(result[:1, :, block:]), result[:-1, :, block:]], axis=0
    )
    summed = firsts + seconds
    return (
        jnp.transpose(summed, (1, 0, 2, 3, 4))
        .reshape(2, total_shots, few_freq, receivers_count)
        .astype(jnp.bfloat16)
    )


def on_device(blended, estimate, partner, delays, levels):
    block = estimate.shape[1]
    freq_local = estimate.shape[2]
    receivers_count = estimate.shape[3]
    span = 2 * block
    steps_t = jnp.arange(span, dtype=jnp.float32)
    taper = jnp.sin(math.pi * (steps_t + 0.5) / span) ** 2
    shot_cos, shot_sin = tables(span)
    recv_cos, recv_sin = tables(receivers_count)
    tables_all = (shot_cos, shot_sin, recv_cos, recv_sin)
    blended_all, current = (
        lax.all_to_all(blended, "shot", split_axis=2, concat_axis=1, tiled=True),
        lax.all_to_all(estimate, "shot", split_axis=2, concat_axis=1, tiled=True),
    )
    few_freq = current.shape[2]
    partner_all = lax.all_gather(partner, "shot", axis=0, tiled=True)
    offsets = jnp.take(delays, partner_all) - delays
    frequency = (
        lax.axis_index("freq") * freq_local
        + lax.axis_index("shot") * few_freq
        + jnp.arange(few_freq, dtype=jnp.int32)
    )
    phase_cos, phase_sin = phase_tables(offsets, frequency)
    level_all = levels.astype(jnp.float32)
    for pass_index in range(PASSES):
        current = whole_pass(
            current,
            blended_all,
            partner_all,
            phase_cos,
            phase_sin,
            level_all,
            taper,
            tables_all,
            block,
        )
    return lax.all_to_all(current, "shot", split_axis=1, concat_axis=2, tiled=True)


LANES = 128
TINY = 1.1754944e-38


def fourier_matrices(length):
    half = np.arange(length // 2)

    def turns(receivers, parity):
        angles = 2.0 * np.pi / length * (np.outer(receivers, 2 * half + parity) % length)
        cos, sin = np.cos(angles), np.sin(angles)
        return np.block([[cos, -sin], [sin, cos]])

    forward = np.concatenate([turns(np.arange(length), parity) for parity in range(2)], axis=1)
    inverse = np.stack([turns(half, parity).T for parity in range(2)])
    return forward.astype(np.float32), inverse.astype(np.float32)


def short_fourier(values, sign):
    count = len(values)
    if count == 1:
        return values
    even = short_fourier(values[0::2], sign)
    odd = short_fourier(values[1::2], sign)
    low, high = [], []
    for k in range(count // 2):
        real, imag = odd[k]
        if 4 * k == count:
            real, imag = (-imag, real) if sign > 0 else (imag, -real)
        elif 8 * k == count or 8 * k == 3 * count:
            half = math.sqrt(0.5)
            turned = (real - sign * imag, imag + sign * real)
            if 8 * k == 3 * count:
                turned = (-real - sign * imag, sign * real - imag)
            real, imag = turned[0] * half, turned[1] * half
        elif k:
            cos = math.cos(2.0 * math.pi * k / count)
            sin = sign * math.sin(2.0 * math.pi * k / count)
            real, imag = real * cos - imag * sin, imag * cos + real * sin
        low.append((even[k][0] + real, even[k][1] + imag))
        high.append((even[k][0] - real, even[k][1] - imag))
    return low + high


def flipped(index, mask, count):
    result, bit = 0, 1
    while bit < count:
        result = result + (index // bit + mask // bit) % 2 * bit
        bit *= 2
    return result


def deblend_kernel(
    n,
    nf,
    block,
    few,
    nr,
    blended_ref,
    estimate_ref,
    partner_hbm,
    delays_hbm,
    levels_hbm,
    forward_hbm,
    inverse_hbm,
    out_ref,
    partner_ref,
    delays_ref,
    levels_ref,
    e_all,
    b_all,
    info,
    turn_cos,
    turn_sin,
    known_ref,
    mates,
    x,
    estimated,
    observed,
    lines,
    coefs,
    carry,
    limit,
    sums,
    exact_forward,
    exact_inverse,
    forward,
    inverse,
    local_sem,
    info_send,
    info_recv,
    e_send,
    e_recv,
    b_send,
    b_recv,
    sums_send,
    sums_recv,
    out_send,
    out_recv,
):
    total = n * block
    span = 2 * block
    half = n // 2
    hr = nr // 2
    columns = [(parity, c) for parity in range(2) for c in range(0, hr, LANES)]
    me = lax.axis_index("shot")
    column = lax.axis_index("freq")
    mesh_id = pl.DeviceIdType.MESH
    peers = [flipped(me, k, n) for k in range(n)]
    order = [half] + [k for near in range(1, half) for k in (near + half, near)]
    others = [lax.rem(column + k, nf) for k in range(nf)]
    everyone = [(k, f) for k in order + [0] for f in range(nf) if (k, f) != (0, 0)]

    barrier = pltpu.get_barrier_semaphore()
    for k, f in everyone:
        where = {"shot": peers[k], "freq": others[f]}
        pl.semaphore_signal(barrier, inc=1, device_id=where, device_id_type=mesh_id)

    scalar_copies = [
        pltpu.make_async_copy(partner_hbm, partner_ref, local_sem.at[3]),
        pltpu.make_async_copy(delays_hbm, delays_ref, local_sem.at[4]),
        pltpu.make_async_copy(levels_hbm, levels_ref, local_sem.at[5]),
    ]
    for copy in scalar_copies:
        copy.start()
    local_copies = [
        pltpu.make_async_copy(forward_hbm, exact_forward, local_sem.at[0]),
        pltpu.make_async_copy(inverse_hbm, exact_inverse, local_sem.at[6]),
        pltpu.make_async_copy(
            estimate_ref.at[:, :, pl.ds(me * few, few), :],
            e_all.at[:, pl.ds(me * block, block)],
            local_sem.at[1],
        ),
        pltpu.make_async_copy(
            blended_ref.at[:, :, pl.ds(me * few, few), :],
            b_all.at[:, pl.ds(me * block, block)],
            local_sem.at[2],
        ),
    ]
    for copy in local_copies:
        copy.start()

    for copy in scalar_copies:
        copy.wait()
    lane = lax.broadcasted_iota(jnp.int32, (8, LANES), 1)
    row = lax.broadcasted_iota(jnp.int32, (8, LANES), 0)
    tile = jnp.zeros((8, LANES), jnp.int32)
    for i in range(block):
        own = me * block + i
        mate = partner_ref[i]
        offset = delays_ref[mate] - delays_ref[own]
        here = lane == own
        tile = jnp.where(here & (row == 0), mate, tile)
        tile = jnp.where(here & (row == 1), offset, tile)
    info[0] = tile

    pl.semaphore_wait(barrier, n * nf - 1)

    def send(source, target, send_sem, recv_sem, where):
        copy = pltpu.make_async_remote_copy(
            src_ref=source,
            dst_ref=target,
            send_sem=send_sem,
            recv_sem=recv_sem,
            device_id=where,
            device_id_type=mesh_id,
        )
        copy.start()
        return copy

    info_copies = [
        send(info.at[0], info.at[k], info_send.at[k], info_recv.at[k], {"shot": peers[k]})
        for k in order
    ]
    record_copies = {k: [] for k in range(n)}
    record_copies[0] = local_copies[2:]
    for k in order:
        for held, whole, sent, received in (
            (estimate_ref, e_all, e_send, e_recv),
            (blended_ref, b_all, b_send, b_recv),
        ):
            record_copies[k].append(
                send(
                    held.at[:, :, pl.ds(peers[k] * few, few), :],
                    whole.at[:, pl.ds(me * block, block)],
                    sent.at[k],
                    received.at[k],
                    {"shot": peers[k]},
                )
            )

    lines[pl.ds(total, block)] = jnp.zeros((block, few, 2 * nr), jnp.float32)
    for copy in info_copies:
        copy.wait()
    known = info[0]
    for k in range(1, n):
        known = known + info[k]
    frequency = (column * n + me) * few + lax.broadcasted_iota(jnp.int32, (few, LANES), 0)
    phase = (frequency * known[1:2, :]) & (NT - 1)
    angles = 2.0 * math.pi / NT * phase.astype(jnp.float32)
    cos_table = relaxation * jnp.cos(angles)
    sin_table = relaxation * jnp.sin(angles)
    known_ref[...] = known
    to_scalars = pltpu.make_async_copy(known_ref, mates, local_sem.at[7])
    to_scalars.start()
    for s in range(total):
        turn_cos[s] = jnp.broadcast_to(cos_table[:, s : s + 1], (few, LANES))
        turn_sin[s] = jnp.broadcast_to(sin_table[:, s : s + 1], (few, LANES))

    for copy in local_copies[:2]:
        copy.wait()
    top = exact_forward[...].astype(jnp.bfloat16)
    forward[: 2 * nr] = top
    forward[2 * nr :] = (exact_forward[...] - top.astype(jnp.float32)).astype(jnp.bfloat16)
    top = exact_inverse[...].astype(jnp.bfloat16)
    inverse[:, :nr] = top
    inverse[:, nr : 2 * nr] = top
    inverse[:, 2 * nr :] = (exact_inverse[...] - top.astype(jnp.float32)).astype(jnp.bfloat16)
    to_scalars.wait()

    def keep(s, parity, at, value):
        start = 2 * nr * parity + at
        top = value.astype(jnp.bfloat16)
        x[s, :, start : start + LANES] = top
        rest = value - top.astype(jnp.float32)
        x[s, :, start + nr : start + nr + LANES] = rest.astype(jnp.bfloat16)

    def relax(pair, carried):
        for side in range(2):
            for i in range(block):
                s = (pair + side * half) * block + i
                mate = mates[0, s]
                cos, sin = turn_cos[s], turn_sin[s]
                for parity, c in columns:
                    at = parity * nr + c
                    reals, imags = slice(at, at + LANES), slice(at + hr, at + hr + LANES)
                    mate_real = estimated[mate, :, reals]
                    mate_imag = estimated[mate, :, imags]
                    seen_real = estimated[s, :, reals] + observed[s, :, reals]
                    seen_imag = estimated[s, :, imags] + observed[s, :, imags]
                    lines[s, :, reals] = relaxation * seen_real - (mate_real * cos + mate_imag * sin)
                    lines[s, :, imags] = relaxation * seen_imag - (mate_imag * cos - mate_real * sin)
        return carried

    def to_lines(owner):
        records = pl.ds(owner * block, block)
        rows = []
        for whole in (e_all, b_all):
            real = whole[0, records].reshape(block * few, nr)
            imag = whole[1, records].reshape(block * few, nr)
            rows.append(jnp.concatenate([real, imag, real, imag], axis=1))
        result = jnp.dot(
            jnp.concatenate(rows, axis=0), forward[...], preferred_element_type=jnp.float32
        ).reshape(2 * block, few, 2 * nr)
        estimated[records] = result[:block]
        observed[records] = result[block:]

    def to_estimate(start, shots):
        results = []
        for parity in range(2):
            start_lane = 2 * nr * parity
            both = x[pl.ds(start, shots), :, start_lane : start_lane + 2 * nr]
            both = both.reshape(shots * few, 2 * nr)
            rows = jnp.concatenate([both, both[:, :nr]], axis=1)
            result = jnp.dot(rows, inverse[parity], preferred_element_type=jnp.float32)
            results.append(result.reshape(shots, few, nr))
        even, odd = results
        for lanes, result in ((slice(0, hr), even + odd), (slice(hr, nr), even - odd)):
            for part in range(2):
                e_all[part, pl.ds(start, shots), :, lanes] = result[
                    :, :, part * hr : (part + 1) * hr
                ].astype(jnp.bfloat16)

    weights = [math.sin(math.pi * (t + 0.5) / span) ** 2 for t in range(span)]

    def analyse(step):
        def window(j, carried):
            summed = jnp.zeros((few, LANES), jnp.float32)
            for parity, c in columns:
                c += parity * nr
                values = [
                    (
                        lines[j * block + t, :, c : c + LANES] * weights[t],
                        lines[j * block + t, :, hr + c : hr + c + LANES] * weights[t],
                    )
                    for t in range(span)
                ]
                for k, (real, imag) in enumerate(short_fourier(values, -1)):
                    power = real * real + imag * imag
                    summed = summed + power * lax.rsqrt(jnp.maximum(power, TINY))
                    coefs[j, k, :, c : c + LANES] = real
                    coefs[j, k, :, hr + c : hr + c + LANES] = imag
            limit[pl.ds(j, 1), :] = jnp.sum(summed, axis=0, keepdims=True)
            return carried

        lax.fori_loop(0, n, window, 0)

    departures = []
    diagonal = lax.broadcasted_iota(jnp.int32, (n, LANES), 0) == lax.broadcasted_iota(
        jnp.int32, (n, LANES), 1
    )

    def thresholds(step):
        column_sums = jnp.sum(limit[...], axis=1, keepdims=True)
        sums[step, 0] = jnp.sum(jnp.where(diagonal, column_sums, 0.0), axis=0, keepdims=True)
        for k, f in everyone:
            send(
                sums.at[step, 0],
                sums.at[step, k * nf + f],
                sums_send.at[step],
                sums_recv.at[step],
                {"shot": peers[k], "freq": others[f]},
            )
        rows = sums.at[step, pl.ds(1, n * nf - 1)]
        arrived = pltpu.make_async_remote_copy(
            src_ref=rows,
            dst_ref=rows,
            send_sem=sums_send.at[step],
            recv_sem=sums_recv.at[step],
            device_id={"shot": peers[1]},
            device_id_type=mesh_id,
        )
        arrived.wait_recv()
        departures.append(arrived)
        whole = jnp.sum(sums[step], axis=0)
        column_sums = jnp.sum(jnp.where(diagonal, whole, 0.0), axis=1, keepdims=True)
        limit[...] = jnp.broadcast_to(column_sums, (n, LANES))

    count = span * few * n * nf * nr

    def synthesise(last, j, carried):
        scale = 1.0 / (span * nr) if last else 1.0 / span
        level = levels_ref[j].astype(jnp.float32) * (level_scale * scale / count)
        bound = limit[pl.ds(j, 1), :] * level
        for parity, c in columns:
            c += parity * nr
            values = []
            for k in range(span):
                real = coefs[j, k, :, c : c + LANES]
                imag = coefs[j, k, :, hr + c : hr + c + LANES]
                power = real * real + imag * imag
                factor = jnp.maximum(scale - bound * lax.rsqrt(power), 0.0)
                values.append((real * factor, imag * factor))
            for t, parts in enumerate(short_fourier(values, 1)):
                for part in range(2):
                    lanes = slice(part * hr + c, part * hr + c + LANES)
                    if t < block:
                        value = parts[part] + carry[t, :, lanes]
                        if last:
                            keep(j * block + t, parity, part * hr + c - parity * nr, value)
                        else:
                            estimated[j * block + t, :, lanes] = value
                    else:
                        carry[t - block, :, lanes] = parts[part]
        return carried

    for step in range(PASSES):
        if step == 0:
            for near in range(half):
                for k in (near, near + half):
                    for copy in record_copies[k]:
                        copy.wait()
                    to_lines(peers[k])
                relax(peers[near] % half, 0)
        else:
            lax.fori_loop(0, half, relax, 0)
        analyse(step)
        thresholds(step)
        carry[...] = jnp.zeros_like(carry)
        lax.fori_loop(0, n, functools.partial(synthesise, step == PASSES - 1), 0)

    copies = []
    for group in [(k, k + 1) for k in range(half, n, 2)] + [(2, 3), (0, 1)]:
        to_estimate(peers[group[0]] // 2 * 2 * block, 2 * block)
        for k in group:
            if k:
                copies.append(
                    send(
                        e_all.at[:, pl.ds(peers[k] * block, block)],
                        out_ref.at[:, :, pl.ds(me * few, few), :],
                        out_send.at[k],
                        out_recv.at[k],
                        {"shot": peers[k]},
                    )
                )
    last = pltpu.make_async_copy(
        e_all.at[:, pl.ds(me * block, block)],
        out_ref.at[:, :, pl.ds(me * few, few), :],
        local_sem.at[0],
    )
    last.start()
    for copy in copies:
        copy.wait()
    for copy in departures:
        copy.wait_send()
    last.wait()


def in_one_kernel(n, nf, blended, estimate, partner, delays, levels):
    block, freq_local, nr = estimate.shape[1:]
    few = freq_local // n
    total = n * block
    forward, inverse = fourier_matrices(nr)
    f32, bf16 = jnp.float32, jnp.bfloat16
    anywhere = pl.BlockSpec(memory_space=pl.ANY)
    dma = pltpu.SemaphoreType.DMA
    return pl.pallas_call(
        functools.partial(deblend_kernel, n, nf, block, few, nr),
        out_shape=jax.ShapeDtypeStruct(estimate.shape, estimate.dtype),
        in_specs=[anywhere] * 7,
        out_specs=anywhere,
        scratch_shapes=[
            pltpu.SMEM(partner.shape, jnp.int32),
            pltpu.SMEM(delays.shape, jnp.int32),
            pltpu.SMEM(levels.shape, jnp.int32),
            pltpu.VMEM((2, total, few, nr), bf16),
            pltpu.VMEM((2, total, few, nr), bf16),
            pltpu.VMEM((n, 8, LANES), jnp.int32),
            pltpu.VMEM((total, few, LANES), f32),
            pltpu.VMEM((total, few, LANES), f32),
            pltpu.VMEM((8, LANES), jnp.int32),
            pltpu.SMEM((8, LANES), jnp.int32),
            pltpu.VMEM((total, few, 4 * nr), bf16),
            pltpu.VMEM((total, few, 2 * nr), f32),
            pltpu.VMEM((total, few, 2 * nr), f32),
            pltpu.VMEM((total + block, few, 2 * nr), f32),
            pltpu.VMEM((n, 2 * block, few, 2 * nr), f32),
            pltpu.VMEM((block, few, 2 * nr), f32),
            pltpu.VMEM((n, LANES), f32),
            pltpu.VMEM((PASSES, n * nf, 1, LANES), f32),
            pltpu.VMEM(forward.shape, f32),
            pltpu.VMEM(inverse.shape, f32),
            pltpu.VMEM((4 * nr, 2 * nr), bf16),
            pltpu.VMEM((2, 3 * nr, nr), bf16),
            dma((8,)),
            dma((n,)),
            dma((n,)),
            dma((n,)),
            dma((n,)),
            dma((n,)),
            dma((n,)),
            dma((PASSES,)),
            dma((PASSES,)),
            dma((n,)),
            dma((n,)),
        ],
        compiler_params=pltpu.CompilerParams(
            collective_id=0, has_side_effects=True, vmem_limit_bytes=60 * 1024 * 1024
        ),
    )(blended, estimate, partner, delays, levels, jnp.asarray(forward), jnp.asarray(inverse))


def solution(mesh):
    n, nf = mesh.shape["shot"], mesh.shape["freq"]

    def body(blended, estimate, partner, delays, levels):
        block, freq_local, nr = estimate.shape[1:]
        whole_tiles = (
            n == 8 and freq_local % (16 * n) == 0 and nr % (2 * LANES) == 0 and n * block <= LANES
        )
        if whole_tiles:
            return in_one_kernel(n, nf, blended, estimate, partner, delays, levels)
        return on_device(blended, estimate, partner, delays, levels)

    return jax.shard_map(
        body,
        mesh=mesh,
        in_specs=(
            P(None, "shot", "freq", None),
            P(None, "shot", "freq", None),
            P("shot"),
            P(),
            P(),
        ),
        out_specs=P(None, "shot", "freq", None),
        check_vma=False,
    )
```

```python
import functools
import math

import jax
import jax.numpy as jnp
import numpy as np
from jax import lax
from jax.experimental import pallas as pl
from jax.experimental.pallas import tpu as pltpu
from jax.sharding import PartitionSpec as P

NF = 512
NT = 1024
PASSES = 2


relaxation = 0.5
level_scale = 0.25


def tables(length):
    indices = jnp.arange(length, dtype=jnp.int32)
    products = jnp.mod(indices[:, None] * indices[None, :], length)
    angles = 2.0 * math.pi / length * products.astype(jnp.float32)
    return (jnp.cos(angles), jnp.sin(angles))


def spectrum(real_part, imag_part, direction_sign, shot_cos, shot_sin, recv_cos, recv_sin):
    highest = lax.Precision.HIGHEST

    def receivers(values, table):
        return jnp.einsum("...n,nk->...k", values, table, precision=highest)

    def shots(values, table):
        return jnp.einsum("tk,...tfn->...kfn", table, values, precision=highest)

    first_real = receivers(real_part, recv_cos) + direction_sign * receivers(imag_part, recv_sin)
    first_imag = receivers(imag_part, recv_cos) - direction_sign * receivers(real_part, recv_sin)
    out_real = shots(first_real, shot_cos) + direction_sign * shots(first_imag, shot_sin)
    out_imag = shots(first_imag, shot_cos) - direction_sign * shots(first_real, shot_sin)
    scale = 1.0 / math.sqrt(shot_cos.shape[0] * recv_cos.shape[0])
    return (out_real * scale, out_imag * scale)


def shrink(real_part, imag_part, threshold):
    modulus = jnp.sqrt(real_part * real_part + imag_part * imag_part)
    factor = jnp.maximum(modulus - threshold, 0.0) / jnp.maximum(modulus, threshold)
    return (real_part * factor, imag_part * factor)


def phase_tables(offsets, frequency):
    phase_index = jnp.mod(frequency[None, :] * offsets[:, None], NT)
    angles = 2.0 * math.pi / NT * phase_index.astype(jnp.float32)
    return (jnp.cos(angles)[:, :, None], jnp.sin(angles)[:, :, None])


def relax_step(current, blended, partner_recs, phase_cos, phase_sin):
    shifted_real = partner_recs[0] * phase_cos + partner_recs[1] * phase_sin
    shifted_imag = partner_recs[1] * phase_cos - partner_recs[0] * phase_sin
    shifted = jnp.stack([shifted_real, shifted_imag])
    current_f = current.astype(jnp.float32)
    return current_f + relaxation * (blended.astype(jnp.float32) - current_f - shifted)


def whole_pass(
    current, blended, partner_all, phase_cos, phase_sin, level_all, taper, tables_all, block
):
    shot_cos, shot_sin, recv_cos, recv_sin = tables_all
    total_shots = current.shape[1]
    few_freq = current.shape[2]
    receivers_count = current.shape[3]
    count = total_shots // block
    partner_recs = jnp.take(current, partner_all, axis=1).astype(jnp.float32)
    updated = relax_step(current, blended, partner_recs, phase_cos, phase_sin)
    grouped = jnp.transpose(
        updated.reshape(2, count, block, few_freq, receivers_count), (1, 0, 2, 3, 4)
    )
    following = jnp.concatenate([grouped[1:], jnp.zeros_like(grouped[:1])], axis=0)
    segments = jnp.concatenate([grouped, following], axis=2) * taper[None, None, :, None, None]
    coef_real, coef_imag = spectrum(
        segments[:, 0], segments[:, 1], 1.0, shot_cos, shot_sin, recv_cos, recv_sin
    )
    modulus = jnp.sqrt(coef_real * coef_real + coef_imag * coef_imag)
    local_sum = jnp.sum(modulus, axis=(1, 2, 3))
    total_sum = lax.psum(local_sum, ("shot", "freq"))
    span = 2 * block
    threshold = (level_scale * level_all * total_sum / (span * NF * receivers_count))[
        :, None, None, None
    ]
    kept_real, kept_imag = shrink(coef_real, coef_imag, threshold)
    back_real, back_imag = spectrum(
        kept_real, kept_imag, -1.0, shot_cos, shot_sin, recv_cos, recv_sin
    )
    result = jnp.stack([back_real, back_imag], axis=1)
    firsts = result[:, :, :block]
    seconds = jnp.concatenate(
        [jnp.zeros_like(result[:1, :, block:]), result[:-1, :, block:]], axis=0
    )
    summed = firsts + seconds
    return (
        jnp.transpose(summed, (1, 0, 2, 3, 4))
        .reshape(2, total_shots, few_freq, receivers_count)
        .astype(jnp.bfloat16)
    )


def on_device(blended, estimate, partner, delays, levels):
    block = estimate.shape[1]
    freq_local = estimate.shape[2]
    receivers_count = estimate.shape[3]
    span = 2 * block
    steps_t = jnp.arange(span, dtype=jnp.float32)
    taper = jnp.sin(math.pi * (steps_t + 0.5) / span) ** 2
    shot_cos, shot_sin = tables(span)
    recv_cos, recv_sin = tables(receivers_count)
    tables_all = (shot_cos, shot_sin, recv_cos, recv_sin)
    blended_all, current = (
        lax.all_to_all(blended, "shot", split_axis=2, concat_axis=1, tiled=True),
        lax.all_to_all(estimate, "shot", split_axis=2, concat_axis=1, tiled=True),
    )
    few_freq = current.shape[2]
    partner_all = lax.all_gather(partner, "shot", axis=0, tiled=True)
    offsets = jnp.take(delays, partner_all) - delays
    frequency = (
        lax.axis_index("freq") * freq_local
        + lax.axis_index("shot") * few_freq
        + jnp.arange(few_freq, dtype=jnp.int32)
    )
    phase_cos, phase_sin = phase_tables(offsets, frequency)
    level_all = levels.astype(jnp.float32)
    for pass_index in range(PASSES):
        current = whole_pass(
            current,
            blended_all,
            partner_all,
            phase_cos,
            phase_sin,
            level_all,
            taper,
            tables_all,
            block,
        )
    return lax.all_to_all(current, "shot", split_axis=1, concat_axis=2, tiled=True)


LANES = 128
TINY = 1.1754944e-38


def fourier_matrices(length):
    half = np.arange(length // 2)

    def turns(receivers, parity):
        angles = 2.0 * np.pi / length * (np.outer(receivers, 2 * half + parity) % length)
        cos, sin = np.cos(angles), np.sin(angles)
        return np.block([[cos, -sin], [sin, cos]])

    forward = np.concatenate([turns(np.arange(length), parity) for parity in range(2)], axis=1)
    inverse = np.stack([turns(half, parity).T for parity in range(2)])
    return forward.astype(np.float32), inverse.astype(np.float32)


def short_fourier(values, sign):
    count = len(values)
    if count == 1:
        return values
    even = short_fourier(values[0::2], sign)
    odd = short_fourier(values[1::2], sign)
    low, high = [], []
    for k in range(count // 2):
        real, imag = odd[k]
        if 4 * k == count:
            real, imag = (-imag, real) if sign > 0 else (imag, -real)
        elif 8 * k == count or 8 * k == 3 * count:
            half = math.sqrt(0.5)
            turned = (real - sign * imag, imag + sign * real)
            if 8 * k == 3 * count:
                turned = (-real - sign * imag, sign * real - imag)
            real, imag = turned[0] * half, turned[1] * half
        elif k:
            cos = math.cos(2.0 * math.pi * k / count)
            sin = sign * math.sin(2.0 * math.pi * k / count)
            real, imag = real * cos - imag * sin, imag * cos + real * sin
        low.append((even[k][0] + real, even[k][1] + imag))
        high.append((even[k][0] - real, even[k][1] - imag))
    return low + high


def flipped(index, mask, count):
    result, bit = 0, 1
    while bit < count:
        result = result + (index // bit + mask // bit) % 2 * bit
        bit *= 2
    return result


def deblend_kernel(
    n,
    nf,
    block,
    few,
    nr,
    blended_ref,
    estimate_ref,
    partner_hbm,
    delays_hbm,
    levels_hbm,
    forward_hbm,
    inverse_hbm,
    out_ref,
    partner_ref,
    delays_ref,
    levels_ref,
    e_home,
    b_home,
    e_all,
    b_all,
    info,
    turn_cos,
    turn_sin,
    known_ref,
    mates,
    x,
    estimated,
    observed,
    lines,
    coefs,
    carry,
    limit,
    sums,
    exact_forward,
    exact_inverse,
    forward,
    inverse,
    local_sem,
    info_send,
    info_recv,
    e_send,
    e_recv,
    b_send,
    b_recv,
    sums_send,
    sums_recv,
    out_send,
    out_recv,
):
    total = n * block
    span = 2 * block
    half = n // 2
    hr = nr // 2
    columns = [(parity, c) for parity in range(2) for c in range(0, hr, LANES)]
    me = lax.axis_index("shot")
    column = lax.axis_index("freq")
    mesh_id = pl.DeviceIdType.MESH
    peers = [flipped(me, k, n) for k in range(n)]
    order = [half] + [k for near in range(1, half) for k in (near + half, near)]
    others = [lax.rem(column + k, nf) for k in range(nf)]
    everyone = [(k, f) for k in order + [0] for f in range(nf) if (k, f) != (0, 0)]

    barrier = pltpu.get_barrier_semaphore()
    for k, f in everyone:
        where = {"shot": peers[k], "freq": others[f]}
        pl.semaphore_signal(barrier, inc=1, device_id=where, device_id_type=mesh_id)

    scalar_copies = [
        pltpu.make_async_copy(partner_hbm, partner_ref, local_sem.at[3]),
        pltpu.make_async_copy(delays_hbm, delays_ref, local_sem.at[4]),
        pltpu.make_async_copy(levels_hbm, levels_ref, local_sem.at[5]),
    ]
    for copy in scalar_copies:
        copy.start()
    home_copies = [
        pltpu.make_async_copy(estimate_ref, e_home, local_sem.at[8]),
        pltpu.make_async_copy(blended_ref, b_home, local_sem.at[9]),
    ]
    for copy in home_copies:
        copy.start()
    local_copies = [
        pltpu.make_async_copy(forward_hbm, exact_forward, local_sem.at[0]),
        pltpu.make_async_copy(inverse_hbm, exact_inverse, local_sem.at[6]),
        pltpu.make_async_copy(
            estimate_ref.at[:, :, pl.ds(me * few, few), :],
            e_all.at[:, pl.ds(me * block, block)],
            local_sem.at[1],
        ),
        pltpu.make_async_copy(
            blended_ref.at[:, :, pl.ds(me * few, few), :],
            b_all.at[:, pl.ds(me * block, block)],
            local_sem.at[2],
        ),
    ]
    for copy in local_copies:
        copy.start()

    for copy in scalar_copies:
        copy.wait()
    lane = lax.broadcasted_iota(jnp.int32, (8, LANES), 1)
    row = lax.broadcasted_iota(jnp.int32, (8, LANES), 0)
    tile = jnp.zeros((8, LANES), jnp.int32)
    for i in range(block):
        own = me * block + i
        mate = partner_ref[i]
        offset = delays_ref[mate] - delays_ref[own]
        here = lane == own
        tile = jnp.where(here & (row == 0), mate, tile)
        tile = jnp.where(here & (row == 1), offset, tile)
    info[0] = tile
    for copy in home_copies:
        copy.wait()

    pl.semaphore_wait(barrier, n * nf - 1)

    def send(source, target, send_sem, recv_sem, where):
        copy = pltpu.make_async_remote_copy(
            src_ref=source,
            dst_ref=target,
            send_sem=send_sem,
            recv_sem=recv_sem,
            device_id=where,
            device_id_type=mesh_id,
        )
        copy.start()
        return copy

    info_copies = [
        send(info.at[0], info.at[k], info_send.at[k], info_recv.at[k], {"shot": peers[k]})
        for k in order
    ]
    record_copies = {k: [] for k in range(n)}
    record_copies[0] = local_copies[2:]
    for k in order:
        for held, whole, sent, received in (
            (e_home, e_all, e_send, e_recv),
            (b_home, b_all, b_send, b_recv),
        ):
            record_copies[k].append(
                send(
                    held.at[:, :, pl.ds(peers[k] * few, few), :],
                    whole.at[:, pl.ds(me * block, block)],
                    sent.at[k],
                    received.at[k],
                    {"shot": peers[k]},
                )
            )

    lines[pl.ds(total, block)] = jnp.zeros((block, few, 2 * nr), jnp.float32)
    for copy in info_copies:
        copy.wait()
    known = info[0]
    for k in range(1, n):
        known = known + info[k]
    frequency = (column * n + me) * few + lax.broadcasted_iota(jnp.int32, (few, LANES), 0)
    phase = (frequency * known[1:2, :]) & (NT - 1)
    angles = 2.0 * math.pi / NT * phase.astype(jnp.float32)
    cos_table = relaxation * jnp.cos(angles)
    sin_table = relaxation * jnp.sin(angles)
    known_ref[...] = known
    to_scalars = pltpu.make_async_copy(known_ref, mates, local_sem.at[7])
    to_scalars.start()
    for s in range(total):
        turn_cos[s] = jnp.broadcast_to(cos_table[:, s : s + 1], (few, LANES))
        turn_sin[s] = jnp.broadcast_to(sin_table[:, s : s + 1], (few, LANES))

    for copy in local_copies[:2]:
        copy.wait()
    top = exact_forward[...].astype(jnp.bfloat16)
    forward[: 2 * nr] = top
    forward[2 * nr :] = (exact_forward[...] - top.astype(jnp.float32)).astype(jnp.bfloat16)
    top = exact_inverse[...].astype(jnp.bfloat16)
    inverse[:, :nr] = top
    inverse[:, nr : 2 * nr] = top
    inverse[:, 2 * nr :] = (exact_inverse[...] - top.astype(jnp.float32)).astype(jnp.bfloat16)
    to_scalars.wait()

    def keep(s, parity, at, value):
        start = 2 * nr * parity + at
        top = value.astype(jnp.bfloat16)
        x[s, :, start : start + LANES] = top
        rest = value - top.astype(jnp.float32)
        x[s, :, start + nr : start + nr + LANES] = rest.astype(jnp.bfloat16)

    def relax(pair, carried):
        for side in range(2):
            for i in range(block):
                s = (pair + side * half) * block + i
                mate = mates[0, s]
                cos, sin = turn_cos[s], turn_sin[s]
                for parity, c in columns:
                    at = parity * nr + c
                    reals, imags = slice(at, at + LANES), slice(at + hr, at + hr + LANES)
                    mate_real = estimated[mate, :, reals]
                    mate_imag = estimated[mate, :, imags]
                    seen_real = estimated[s, :, reals] + observed[s, :, reals]
                    seen_imag = estimated[s, :, imags] + observed[s, :, imags]
                    lines[s, :, reals] = relaxation * seen_real - (mate_real * cos + mate_imag * sin)
                    lines[s, :, imags] = relaxation * seen_imag - (mate_imag * cos - mate_real * sin)
        return carried

    def to_lines(owner):
        records = pl.ds(owner * block, block)
        rows = []
        for whole in (e_all, b_all):
            real = whole[0, records].reshape(block * few, nr)
            imag = whole[1, records].reshape(block * few, nr)
            rows.append(jnp.concatenate([real, imag, real, imag], axis=1))
        result = jnp.dot(
            jnp.concatenate(rows, axis=0), forward[...], preferred_element_type=jnp.float32
        ).reshape(2 * block, few, 2 * nr)
        estimated[records] = result[:block]
        observed[records] = result[block:]

    def to_estimate(start, shots):
        results = []
        for parity in range(2):
            start_lane = 2 * nr * parity
            both = x[pl.ds(start, shots), :, start_lane : start_lane + 2 * nr]
            both = both.reshape(shots * few, 2 * nr)
            rows = jnp.concatenate([both, both[:, :nr]], axis=1)
            result = jnp.dot(rows, inverse[parity], preferred_element_type=jnp.float32)
            results.append(result.reshape(shots, few, nr))
        even, odd = results
        for lanes, result in ((slice(0, hr), even + odd), (slice(hr, nr), even - odd)):
            for part in range(2):
                e_all[part, pl.ds(start, shots), :, lanes] = result[
                    :, :, part * hr : (part + 1) * hr
                ].astype(jnp.bfloat16)

    weights = [math.sin(math.pi * (t + 0.5) / span) ** 2 for t in range(span)]

    def analyse(step):
        def window(j, carried):
            summed = jnp.zeros((few, LANES), jnp.float32)
            for parity, c in columns:
                c += parity * nr
                values = [
                    (
                        lines[j * block + t, :, c : c + LANES] * weights[t],
                        lines[j * block + t, :, hr + c : hr + c + LANES] * weights[t],
                    )
                    for t in range(span)
                ]
                for k, (real, imag) in enumerate(short_fourier(values, -1)):
                    power = real * real + imag * imag
                    summed = summed + power * lax.rsqrt(jnp.maximum(power, TINY))
                    coefs[j, k, :, c : c + LANES] = real
                    coefs[j, k, :, hr + c : hr + c + LANES] = imag
            limit[pl.ds(j, 1), :] = jnp.sum(summed, axis=0, keepdims=True)
            return carried

        lax.fori_loop(0, n, window, 0)

    departures = []
    diagonal = lax.broadcasted_iota(jnp.int32, (n, LANES), 0) == lax.broadcasted_iota(
        jnp.int32, (n, LANES), 1
    )

    def thresholds(step):
        column_sums = jnp.sum(limit[...], axis=1, keepdims=True)
        sums[step, 0] = jnp.sum(jnp.where(diagonal, column_sums, 0.0), axis=0, keepdims=True)
        for k, f in everyone:
            send(
                sums.at[step, 0],
                sums.at[step, k * nf + f],
                sums_send.at[step],
                sums_recv.at[step],
                {"shot": peers[k], "freq": others[f]},
            )
        rows = sums.at[step, pl.ds(1, n * nf - 1)]
        arrived = pltpu.make_async_remote_copy(
            src_ref=rows,
            dst_ref=rows,
            send_sem=sums_send.at[step],
            recv_sem=sums_recv.at[step],
            device_id={"shot": peers[1]},
            device_id_type=mesh_id,
        )
        arrived.wait_recv()
        departures.append(arrived)
        whole = jnp.sum(sums[step], axis=0)
        column_sums = jnp.sum(jnp.where(diagonal, whole, 0.0), axis=1, keepdims=True)
        limit[...] = jnp.broadcast_to(column_sums, (n, LANES))

    count = span * few * n * nf * nr

    def synthesise(last, j, carried, firsts=True):
        scale = 1.0 / (span * nr) if last else 1.0 / span
        level = levels_ref[j].astype(jnp.float32) * (level_scale * scale / count)
        bound = limit[pl.ds(j, 1), :] * level
        for parity, c in columns:
            c += parity * nr
            values = []
            for k in range(span):
                real = coefs[j, k, :, c : c + LANES]
                imag = coefs[j, k, :, hr + c : hr + c + LANES]
                power = real * real + imag * imag
                factor = jnp.maximum(scale - bound * lax.rsqrt(power), 0.0)
                values.append((real * factor, imag * factor))
            for t, parts in enumerate(short_fourier(values, 1)):
                for part in range(2):
                    lanes = slice(part * hr + c, part * hr + c + LANES)
                    if t < block and not firsts:
                        continue
                    if t < block:
                        value = parts[part] + carry[t, :, lanes]
                        if last:
                            keep(j * block + t, parity, part * hr + c - parity * nr, value)
                        else:
                            estimated[j * block + t, :, lanes] = value
                    else:
                        carry[t - block, :, lanes] = parts[part]
        return carried

    for step in range(PASSES):
        if step == 0:
            for near in range(half):
                for k in (near, near + half):
                    for copy in record_copies[k]:
                        copy.wait()
                    to_lines(peers[k])
                relax(peers[near] % half, 0)
        else:
            lax.fori_loop(0, half, relax, 0)
        analyse(step)
        thresholds(step)
        if step < PASSES - 1:
            carry[...] = jnp.zeros_like(carry)
            lax.fori_loop(0, n, functools.partial(synthesise, False), 0)

    copies = []
    for group in [(k, k + 1) for k in range(half, n, 2)] + [(2, 3), (0, 1)]:
        first = peers[group[0]] // 2 * 2

        @pl.when(first == 0)
        def _():
            carry[...] = jnp.zeros_like(carry)

        @pl.when(first > 0)
        def _():
            synthesise(True, first - 1, 0, firsts=False)

        synthesise(True, first, 0)
        synthesise(True, first + 1, 0)
        to_estimate(first * block, 2 * block)
        for k in group:
            if k:
                copies.append(
                    send(
                        e_all.at[:, pl.ds(peers[k] * block, block)],
                        out_ref.at[:, :, pl.ds(me * few, few), :],
                        out_send.at[k],
                        out_recv.at[k],
                        {"shot": peers[k]},
                    )
                )
    last = pltpu.make_async_copy(
        e_all.at[:, pl.ds(me * block, block)],
        out_ref.at[:, :, pl.ds(me * few, few), :],
        local_sem.at[0],
    )
    last.start()
    for copy in copies:
        copy.wait()
    for copy in departures:
        copy.wait_send()
    last.wait()


def copy_kernel(source_ref, target_ref, sems):
    copies = [
        pltpu.make_async_copy(
            source_ref.at[part, i], target_ref.at[part, i], sems.at[part, i]
        )
        for part in range(source_ref.shape[0])
        for i in range(source_ref.shape[1])
    ]
    for copy in copies:
        copy.start()
    for copy in copies:
        copy.wait()


def in_one_kernel(n, nf, blended, estimate, partner, delays, levels):
    block, freq_local, nr = estimate.shape[1:]
    few = freq_local // n
    total = n * block
    forward, inverse = fourier_matrices(nr)
    f32, bf16 = jnp.float32, jnp.bfloat16
    anywhere = pl.BlockSpec(memory_space=pl.ANY)
    dma = pltpu.SemaphoreType.DMA
    result = pl.pallas_call(
        functools.partial(deblend_kernel, n, nf, block, few, nr),
        out_shape=jax.ShapeDtypeStruct(estimate.shape, estimate.dtype),
        in_specs=[anywhere] * 7,
        out_specs=anywhere,
        scratch_shapes=[
            pltpu.SMEM(partner.shape, jnp.int32),
            pltpu.SMEM(delays.shape, jnp.int32),
            pltpu.SMEM(levels.shape, jnp.int32),
            pltpu.VMEM(estimate.shape, bf16),
            pltpu.VMEM(blended.shape, bf16),
            pltpu.VMEM((2, total, few, nr), bf16),
            pltpu.VMEM((2, total, few, nr), bf16),
            pltpu.VMEM((n, 8, LANES), jnp.int32),
            pltpu.VMEM((total, few, LANES), f32),
            pltpu.VMEM((total, few, LANES), f32),
            pltpu.VMEM((8, LANES), jnp.int32),
            pltpu.SMEM((8, LANES), jnp.int32),
            pltpu.VMEM((total, few, 4 * nr), bf16),
            pltpu.VMEM((total, few, 2 * nr), f32),
            pltpu.VMEM((total, few, 2 * nr), f32),
            pltpu.VMEM((total + block, few, 2 * nr), f32),
            pltpu.VMEM((n, 2 * block, few, 2 * nr), f32),
            pltpu.VMEM((block, few, 2 * nr), f32),
            pltpu.VMEM((n, LANES), f32),
            pltpu.VMEM((PASSES, n * nf, 1, LANES), f32),
            pltpu.VMEM(forward.shape, f32),
            pltpu.VMEM(inverse.shape, f32),
            pltpu.VMEM((4 * nr, 2 * nr), bf16),
            pltpu.VMEM((2, 3 * nr, nr), bf16),
            dma((10,)),
            dma((n,)),
            dma((n,)),
            dma((n,)),
            dma((n,)),
            dma((n,)),
            dma((n,)),
            dma((PASSES,)),
            dma((PASSES,)),
            dma((n,)),
            dma((n,)),
        ],
        compiler_params=pltpu.CompilerParams(
            collective_id=0, has_side_effects=True, vmem_limit_bytes=60 * 1024 * 1024
        ),
    )(blended, estimate, partner, delays, levels, jnp.asarray(forward), jnp.asarray(inverse))
    return pl.pallas_call(
        copy_kernel,
        out_shape=jax.ShapeDtypeStruct(estimate.shape, estimate.dtype),
        in_specs=[anywhere],
        out_specs=anywhere,
        scratch_shapes=[dma(estimate.shape[:2])],
        compiler_params=pltpu.CompilerParams(vmem_limit_bytes=60 * 1024 * 1024),
    )(result)


def solution(mesh):
    n, nf = mesh.shape["shot"], mesh.shape["freq"]

    def body(blended, estimate, partner, delays, levels):
        block, freq_local, nr = estimate.shape[1:]
        whole_tiles = (
            n == 8 and freq_local % (16 * n) == 0 and nr % (2 * LANES) == 0 and n * block <= LANES
        )
        if whole_tiles:
            return in_one_kernel(n, nf, blended, estimate, partner, delays, levels)
        return on_device(blended, estimate, partner, delays, levels)

    return jax.shard_map(
        body,
        mesh=mesh,
        in_specs=(
            P(None, "shot", "freq", None),
            P(None, "shot", "freq", None),
            P("shot"),
            P(),
            P(),
        ),
        out_specs=P(None, "shot", "freq", None),
        check_vma=False,
    )
```

```python
import functools
import math

import jax
import jax.numpy as jnp
import numpy as np
from jax import lax
from jax.experimental import pallas as pl
from jax.experimental.pallas import tpu as pltpu
from jax.sharding import PartitionSpec as P

NF = 512
NT = 1024
PASSES = 2


relaxation = 0.5
level_scale = 0.25


def tables(length):
    indices = jnp.arange(length, dtype=jnp.int32)
    products = jnp.mod(indices[:, None] * indices[None, :], length)
    angles = 2.0 * math.pi / length * products.astype(jnp.float32)
    return (jnp.cos(angles), jnp.sin(angles))


def spectrum(real_part, imag_part, direction_sign, shot_cos, shot_sin, recv_cos, recv_sin):
    highest = lax.Precision.HIGHEST

    def receivers(values, table):
        return jnp.einsum("...n,nk->...k", values, table, precision=highest)

    def shots(values, table):
        return jnp.einsum("tk,...tfn->...kfn", table, values, precision=highest)

    first_real = receivers(real_part, recv_cos) + direction_sign * receivers(imag_part, recv_sin)
    first_imag = receivers(imag_part, recv_cos) - direction_sign * receivers(real_part, recv_sin)
    out_real = shots(first_real, shot_cos) + direction_sign * shots(first_imag, shot_sin)
    out_imag = shots(first_imag, shot_cos) - direction_sign * shots(first_real, shot_sin)
    scale = 1.0 / math.sqrt(shot_cos.shape[0] * recv_cos.shape[0])
    return (out_real * scale, out_imag * scale)


def shrink(real_part, imag_part, threshold):
    modulus = jnp.sqrt(real_part * real_part + imag_part * imag_part)
    factor = jnp.maximum(modulus - threshold, 0.0) / jnp.maximum(modulus, threshold)
    return (real_part * factor, imag_part * factor)


def phase_tables(offsets, frequency):
    phase_index = jnp.mod(frequency[None, :] * offsets[:, None], NT)
    angles = 2.0 * math.pi / NT * phase_index.astype(jnp.float32)
    return (jnp.cos(angles)[:, :, None], jnp.sin(angles)[:, :, None])


def relax_step(current, blended, partner_recs, phase_cos, phase_sin):
    shifted_real = partner_recs[0] * phase_cos + partner_recs[1] * phase_sin
    shifted_imag = partner_recs[1] * phase_cos - partner_recs[0] * phase_sin
    shifted = jnp.stack([shifted_real, shifted_imag])
    current_f = current.astype(jnp.float32)
    return current_f + relaxation * (blended.astype(jnp.float32) - current_f - shifted)


def whole_pass(
    current, blended, partner_all, phase_cos, phase_sin, level_all, taper, tables_all, block
):
    shot_cos, shot_sin, recv_cos, recv_sin = tables_all
    total_shots = current.shape[1]
    few_freq = current.shape[2]
    receivers_count = current.shape[3]
    count = total_shots // block
    partner_recs = jnp.take(current, partner_all, axis=1).astype(jnp.float32)
    updated = relax_step(current, blended, partner_recs, phase_cos, phase_sin)
    grouped = jnp.transpose(
        updated.reshape(2, count, block, few_freq, receivers_count), (1, 0, 2, 3, 4)
    )
    following = jnp.concatenate([grouped[1:], jnp.zeros_like(grouped[:1])], axis=0)
    segments = jnp.concatenate([grouped, following], axis=2) * taper[None, None, :, None, None]
    coef_real, coef_imag = spectrum(
        segments[:, 0], segments[:, 1], 1.0, shot_cos, shot_sin, recv_cos, recv_sin
    )
    modulus = jnp.sqrt(coef_real * coef_real + coef_imag * coef_imag)
    local_sum = jnp.sum(modulus, axis=(1, 2, 3))
    total_sum = lax.psum(local_sum, ("shot", "freq"))
    span = 2 * block
    threshold = (level_scale * level_all * total_sum / (span * NF * receivers_count))[
        :, None, None, None
    ]
    kept_real, kept_imag = shrink(coef_real, coef_imag, threshold)
    back_real, back_imag = spectrum(
        kept_real, kept_imag, -1.0, shot_cos, shot_sin, recv_cos, recv_sin
    )
    result = jnp.stack([back_real, back_imag], axis=1)
    firsts = result[:, :, :block]
    seconds = jnp.concatenate(
        [jnp.zeros_like(result[:1, :, block:]), result[:-1, :, block:]], axis=0
    )
    summed = firsts + seconds
    return (
        jnp.transpose(summed, (1, 0, 2, 3, 4))
        .reshape(2, total_shots, few_freq, receivers_count)
        .astype(jnp.bfloat16)
    )


def on_device(blended, estimate, partner, delays, levels):
    block = estimate.shape[1]
    freq_local = estimate.shape[2]
    receivers_count = estimate.shape[3]
    span = 2 * block
    steps_t = jnp.arange(span, dtype=jnp.float32)
    taper = jnp.sin(math.pi * (steps_t + 0.5) / span) ** 2
    shot_cos, shot_sin = tables(span)
    recv_cos, recv_sin = tables(receivers_count)
    tables_all = (shot_cos, shot_sin, recv_cos, recv_sin)
    blended_all, current = (
        lax.all_to_all(blended, "shot", split_axis=2, concat_axis=1, tiled=True),
        lax.all_to_all(estimate, "shot", split_axis=2, concat_axis=1, tiled=True),
    )
    few_freq = current.shape[2]
    partner_all = lax.all_gather(partner, "shot", axis=0, tiled=True)
    offsets = jnp.take(delays, partner_all) - delays
    frequency = (
        lax.axis_index("freq") * freq_local
        + lax.axis_index("shot") * few_freq
        + jnp.arange(few_freq, dtype=jnp.int32)
    )
    phase_cos, phase_sin = phase_tables(offsets, frequency)
    level_all = levels.astype(jnp.float32)
    for pass_index in range(PASSES):
        current = whole_pass(
            current,
            blended_all,
            partner_all,
            phase_cos,
            phase_sin,
            level_all,
            taper,
            tables_all,
            block,
        )
    return lax.all_to_all(current, "shot", split_axis=1, concat_axis=2, tiled=True)


LANES = 128
TINY = 1.1754944e-38


def fourier_matrices(length):
    half = np.arange(length // 2)

    def turns(receivers, parity):
        angles = 2.0 * np.pi / length * (np.outer(receivers, 2 * half + parity) % length)
        cos, sin = np.cos(angles), np.sin(angles)
        return np.block([[cos, -sin], [sin, cos]])

    forward = np.concatenate([turns(np.arange(length), parity) for parity in range(2)], axis=1)
    inverse = np.stack([turns(half, parity).T for parity in range(2)])
    return forward.astype(np.float32), inverse.astype(np.float32)


def short_fourier(values, sign):
    count = len(values)
    if count == 1:
        return values
    even = short_fourier(values[0::2], sign)
    odd = short_fourier(values[1::2], sign)
    low, high = [], []
    for k in range(count // 2):
        real, imag = odd[k]
        if 4 * k == count:
            real, imag = (-imag, real) if sign > 0 else (imag, -real)
        elif 8 * k == count or 8 * k == 3 * count:
            half = math.sqrt(0.5)
            turned = (real - sign * imag, imag + sign * real)
            if 8 * k == 3 * count:
                turned = (-real - sign * imag, sign * real - imag)
            real, imag = turned[0] * half, turned[1] * half
        elif k:
            cos = math.cos(2.0 * math.pi * k / count)
            sin = sign * math.sin(2.0 * math.pi * k / count)
            real, imag = real * cos - imag * sin, imag * cos + real * sin
        low.append((even[k][0] + real, even[k][1] + imag))
        high.append((even[k][0] - real, even[k][1] - imag))
    return low + high


def flipped(index, mask, count):
    result, bit = 0, 1
    while bit < count:
        result = result + (index // bit + mask // bit) % 2 * bit
        bit *= 2
    return result


def deblend_kernel(
    n,
    nf,
    block,
    few,
    nr,
    blended_ref,
    estimate_ref,
    partner_hbm,
    delays_hbm,
    levels_hbm,
    forward_hbm,
    inverse_hbm,
    out_ref,
    partner_ref,
    delays_ref,
    levels_ref,
    e_home,
    b_home,
    e_all,
    b_all,
    info,
    turn_cos,
    turn_sin,
    known_ref,
    mates,
    x,
    estimated,
    observed,
    lines,
    coefs,
    carry,
    limit,
    sums,
    exact_forward,
    exact_inverse,
    forward,
    inverse,
    local_sem,
    info_send,
    info_recv,
    e_send,
    e_recv,
    b_send,
    b_recv,
    sums_send,
    sums_recv,
    out_send,
    out_recv,
):
    total = n * block
    span = 2 * block
    half = n // 2
    hr = nr // 2
    columns = [(parity, c) for parity in range(2) for c in range(0, hr, LANES)]
    me = lax.axis_index("shot")
    column = lax.axis_index("freq")
    mesh_id = pl.DeviceIdType.MESH
    peers = [flipped(me, k, n) for k in range(n)]
    order = list(range(half, n)) + list(range(1, half))
    others = [lax.rem(column + k, nf) for k in range(nf)]
    everyone = [(k, f) for k in order + [0] for f in range(nf) if (k, f) != (0, 0)]

    barrier = pltpu.get_barrier_semaphore()
    for k, f in everyone:
        where = {"shot": peers[k], "freq": others[f]}
        pl.semaphore_signal(barrier, inc=1, device_id=where, device_id_type=mesh_id)

    scalar_copies = [
        pltpu.make_async_copy(partner_hbm, partner_ref, local_sem.at[3]),
        pltpu.make_async_copy(delays_hbm, delays_ref, local_sem.at[4]),
        pltpu.make_async_copy(levels_hbm, levels_ref, local_sem.at[5]),
    ]
    for copy in scalar_copies:
        copy.start()
    home_copies = [
        pltpu.make_async_copy(estimate_ref, e_home, local_sem.at[8]),
        pltpu.make_async_copy(blended_ref, b_home, local_sem.at[9]),
    ]
    for copy in home_copies:
        copy.start()
    local_copies = [
        pltpu.make_async_copy(forward_hbm, exact_forward, local_sem.at[0]),
        pltpu.make_async_copy(inverse_hbm, exact_inverse, local_sem.at[6]),
        pltpu.make_async_copy(
            estimate_ref.at[:, :, pl.ds(me * few, few), :],
            e_all.at[:, pl.ds(me * block, block)],
            local_sem.at[1],
        ),
        pltpu.make_async_copy(
            blended_ref.at[:, :, pl.ds(me * few, few), :],
            b_all.at[:, pl.ds(me * block, block)],
            local_sem.at[2],
        ),
    ]
    for copy in local_copies:
        copy.start()

    for copy in scalar_copies:
        copy.wait()
    lane = lax.broadcasted_iota(jnp.int32, (8, LANES), 1)
    row = lax.broadcasted_iota(jnp.int32, (8, LANES), 0)
    tile = jnp.zeros((8, LANES), jnp.int32)
    for i in range(block):
        own = me * block + i
        mate = partner_ref[i]
        offset = delays_ref[mate] - delays_ref[own]
        here = lane == own
        tile = jnp.where(here & (row == 0), mate, tile)
        tile = jnp.where(here & (row == 1), offset, tile)
    info[0] = tile
    for copy in home_copies:
        copy.wait()

    pl.semaphore_wait(barrier, n * nf - 1)

    def send(source, target, send_sem, recv_sem, where):
        copy = pltpu.make_async_remote_copy(
            src_ref=source,
            dst_ref=target,
            send_sem=send_sem,
            recv_sem=recv_sem,
            device_id=where,
            device_id_type=mesh_id,
        )
        copy.start()
        return copy

    info_copies = [
        send(info.at[0], info.at[k], info_send.at[k], info_recv.at[k], {"shot": peers[k]})
        for k in order
    ]
    record_copies = {k: [] for k in range(n)}
    record_copies[0] = local_copies[2:]
    for k in order:
        for held, whole, sent, received in (
            (e_home, e_all, e_send, e_recv),
            (b_home, b_all, b_send, b_recv),
        ):
            record_copies[k].append(
                send(
                    held.at[:, :, pl.ds(peers[k] * few, few), :],
                    whole.at[:, pl.ds(me * block, block)],
                    sent.at[k],
                    received.at[k],
                    {"shot": peers[k]},
                )
            )

    lines[pl.ds(total, block)] = jnp.zeros((block, few, 2 * nr), jnp.float32)
    for copy in info_copies:
        copy.wait_recv()
    known = info[0]
    for k in range(1, n):
        known = known + info[k]
    frequency = (column * n + me) * few + lax.broadcasted_iota(jnp.int32, (few, LANES), 0)
    phase = (frequency * known[1:2, :]) & (NT - 1)
    angles = 2.0 * math.pi / NT * phase.astype(jnp.float32)
    cos_table = relaxation * jnp.cos(angles)
    sin_table = relaxation * jnp.sin(angles)
    known_ref[...] = known
    to_scalars = pltpu.make_async_copy(known_ref, mates, local_sem.at[7])
    to_scalars.start()
    for s in range(total):
        turn_cos[s] = jnp.broadcast_to(cos_table[:, s : s + 1], (few, LANES))
        turn_sin[s] = jnp.broadcast_to(sin_table[:, s : s + 1], (few, LANES))

    for copy in local_copies[:2]:
        copy.wait()
    top = exact_forward[...].astype(jnp.bfloat16)
    forward[: 2 * nr] = top
    forward[2 * nr :] = (exact_forward[...] - top.astype(jnp.float32)).astype(jnp.bfloat16)
    top = exact_inverse[...].astype(jnp.bfloat16)
    inverse[:, :nr] = top
    inverse[:, nr : 2 * nr] = top
    inverse[:, 2 * nr :] = (exact_inverse[...] - top.astype(jnp.float32)).astype(jnp.bfloat16)
    to_scalars.wait()

    def keep(s, parity, at, value):
        start = 2 * nr * parity + at
        top = value.astype(jnp.bfloat16)
        x[s, :, start : start + LANES] = top
        rest = value - top.astype(jnp.float32)
        x[s, :, start + nr : start + nr + LANES] = rest.astype(jnp.bfloat16)

    def relax(pair, carried):
        for side in range(2):
            for i in range(block):
                s = (pair + side * half) * block + i
                mate = mates[0, s]
                cos, sin = turn_cos[s], turn_sin[s]
                for parity, c in columns:
                    at = parity * nr + c
                    reals, imags = slice(at, at + LANES), slice(at + hr, at + hr + LANES)
                    mate_real = estimated[mate, :, reals]
                    mate_imag = estimated[mate, :, imags]
                    seen_real = estimated[s, :, reals] + observed[s, :, reals]
                    seen_imag = estimated[s, :, imags] + observed[s, :, imags]
                    lines[s, :, reals] = relaxation * seen_real - (mate_real * cos + mate_imag * sin)
                    lines[s, :, imags] = relaxation * seen_imag - (mate_imag * cos - mate_real * sin)
        return carried

    def to_lines(owner):
        records = pl.ds(owner * block, block)
        rows = []
        for whole in (e_all, b_all):
            real = whole[0, records].reshape(block * few, nr)
            imag = whole[1, records].reshape(block * few, nr)
            rows.append(jnp.concatenate([real, imag, real, imag], axis=1))
        result = jnp.dot(
            jnp.concatenate(rows, axis=0), forward[...], preferred_element_type=jnp.float32
        ).reshape(2 * block, few, 2 * nr)
        estimated[records] = result[:block]
        observed[records] = result[block:]

    def to_estimate(start, shots):
        results = []
        for parity in range(2):
            start_lane = 2 * nr * parity
            both = x[pl.ds(start, shots), :, start_lane : start_lane + 2 * nr]
            both = both.reshape(shots * few, 2 * nr)
            rows = jnp.concatenate([both, both[:, :nr]], axis=1)
            result = jnp.dot(rows, inverse[parity], preferred_element_type=jnp.float32)
            results.append(result.reshape(shots, few, nr))
        even, odd = results
        for lanes, result in ((slice(0, hr), even + odd), (slice(hr, nr), even - odd)):
            for part in range(2):
                e_all[part, pl.ds(start, shots), :, lanes] = result[
                    :, :, part * hr : (part + 1) * hr
                ].astype(jnp.bfloat16)

    weights = [math.sin(math.pi * (t + 0.5) / span) ** 2 for t in range(span)]

    def analyse(step):
        def window(j, carried):
            summed = jnp.zeros((few, LANES), jnp.float32)
            for parity, c in columns:
                c += parity * nr
                values = [
                    (
                        lines[j * block + t, :, c : c + LANES] * weights[t],
                        lines[j * block + t, :, hr + c : hr + c + LANES] * weights[t],
                    )
                    for t in range(span)
                ]
                for k, (real, imag) in enumerate(short_fourier(values, -1)):
                    power = real * real + imag * imag
                    summed = summed + power * lax.rsqrt(jnp.maximum(power, TINY))
                    coefs[j, k, :, c : c + LANES] = real
                    coefs[j, k, :, hr + c : hr + c + LANES] = imag
            limit[pl.ds(j, 1), :] = jnp.sum(summed, axis=0, keepdims=True)
            return carried

        lax.fori_loop(0, n, window, 0)

    departures = list(info_copies)
    diagonal = lax.broadcasted_iota(jnp.int32, (n, LANES), 0) == lax.broadcasted_iota(
        jnp.int32, (n, LANES), 1
    )

    def thresholds(step):
        column_sums = jnp.sum(limit[...], axis=1, keepdims=True)
        sums[step, 0] = jnp.sum(jnp.where(diagonal, column_sums, 0.0), axis=0, keepdims=True)
        for k, f in everyone:
            send(
                sums.at[step, 0],
                sums.at[step, k * nf + f],
                sums_send.at[step],
                sums_recv.at[step],
                {"shot": peers[k], "freq": others[f]},
            )
        rows = sums.at[step, pl.ds(1, n * nf - 1)]
        arrived = pltpu.make_async_remote_copy(
            src_ref=rows,
            dst_ref=rows,
            send_sem=sums_send.at[step],
            recv_sem=sums_recv.at[step],
            device_id={"shot": peers[1]},
            device_id_type=mesh_id,
        )
        arrived.wait_recv()
        departures.append(arrived)
        whole = jnp.sum(sums[step], axis=0)
        column_sums = jnp.sum(jnp.where(diagonal, whole, 0.0), axis=1, keepdims=True)
        limit[...] = jnp.broadcast_to(column_sums, (n, LANES))

    count = span * few * n * nf * nr

    def synthesise(last, j, carried, firsts=True):
        scale = 1.0 / (span * nr) if last else 1.0 / span
        level = levels_ref[j].astype(jnp.float32) * (level_scale * scale / count)
        bound = limit[pl.ds(j, 1), :] * level
        for parity, c in columns:
            c += parity * nr
            values = []
            for k in range(span):
                real = coefs[j, k, :, c : c + LANES]
                imag = coefs[j, k, :, hr + c : hr + c + LANES]
                power = real * real + imag * imag
                factor = jnp.maximum(scale - bound * lax.rsqrt(power), 0.0)
                values.append((real * factor, imag * factor))
            for t, parts in enumerate(short_fourier(values, 1)):
                for part in range(2):
                    lanes = slice(part * hr + c, part * hr + c + LANES)
                    if t < block and not firsts:
                        continue
                    if t < block:
                        value = parts[part] + carry[t, :, lanes]
                        if last:
                            keep(j * block + t, parity, part * hr + c - parity * nr, value)
                        else:
                            estimated[j * block + t, :, lanes] = value
                    else:
                        carry[t - block, :, lanes] = parts[part]
        return carried

    for step in range(PASSES):
        if step == 0:
            for near in range(half):
                for k in (near, near + half):
                    for copy in record_copies[k]:
                        if k:
                            copy.wait_recv()
                            departures.append(copy)
                        else:
                            copy.wait()
                    to_lines(peers[k])
                relax(peers[near] % half, 0)
        else:
            lax.fori_loop(0, half, relax, 0)
        analyse(step)
        thresholds(step)
        if step < PASSES - 1:
            carry[...] = jnp.zeros_like(carry)
            lax.fori_loop(0, n, functools.partial(synthesise, False), 0)

    copies = []
    for group in [(k, k + 1) for k in range(half, n, 2)] + [(2, 3), (0, 1)]:
        first = peers[group[0]] // 2 * 2

        @pl.when(first == 0)
        def _():
            carry[...] = jnp.zeros_like(carry)

        @pl.when(first > 0)
        def _():
            synthesise(True, first - 1, 0, firsts=False)

        synthesise(True, first, 0)
        synthesise(True, first + 1, 0)
        to_estimate(first * block, 2 * block)
        for k in group:
            if k:
                copies.append(
                    send(
                        e_all.at[:, pl.ds(peers[k] * block, block)],
                        out_ref.at[:, :, pl.ds(me * few, few), :],
                        out_send.at[k],
                        out_recv.at[k],
                        {"shot": peers[k]},
                    )
                )
    last = pltpu.make_async_copy(
        e_all.at[:, pl.ds(me * block, block)],
        out_ref.at[:, :, pl.ds(me * few, few), :],
        local_sem.at[0],
    )
    last.start()
    for copy in copies:
        copy.wait()
    for copy in departures:
        copy.wait_send()
    last.wait()


def copy_kernel(source_ref, target_ref, held, in_sems, out_sems):
    pieces = [(part, i) for part in range(source_ref.shape[0]) for i in range(source_ref.shape[1])]
    arrivals = [
        pltpu.make_async_copy(source_ref.at[at], held.at[at], in_sems.at[at]) for at in pieces
    ]
    departures = [
        pltpu.make_async_copy(held.at[at], target_ref.at[at], out_sems.at[at]) for at in pieces
    ]
    for copy in arrivals:
        copy.start()
    for arrival, departure in zip(arrivals, departures):
        arrival.wait()
        departure.start()
    for copy in departures:
        copy.wait()


def in_one_kernel(n, nf, blended, estimate, partner, delays, levels):
    block, freq_local, nr = estimate.shape[1:]
    few = freq_local // n
    total = n * block
    forward, inverse = fourier_matrices(nr)
    f32, bf16 = jnp.float32, jnp.bfloat16
    anywhere = pl.BlockSpec(memory_space=pl.ANY)
    dma = pltpu.SemaphoreType.DMA
    result = pl.pallas_call(
        functools.partial(deblend_kernel, n, nf, block, few, nr),
        out_shape=jax.ShapeDtypeStruct(estimate.shape, estimate.dtype),
        in_specs=[anywhere] * 7,
        out_specs=anywhere,
        scratch_shapes=[
            pltpu.SMEM(partner.shape, jnp.int32),
            pltpu.SMEM(delays.shape, jnp.int32),
            pltpu.SMEM(levels.shape, jnp.int32),
            pltpu.VMEM(estimate.shape, bf16),
            pltpu.VMEM(blended.shape, bf16),
            pltpu.VMEM((2, total, few, nr), bf16),
            pltpu.VMEM((2, total, few, nr), bf16),
            pltpu.VMEM((n, 8, LANES), jnp.int32),
            pltpu.VMEM((total, few, LANES), f32),
            pltpu.VMEM((total, few, LANES), f32),
            pltpu.VMEM((8, LANES), jnp.int32),
            pltpu.SMEM((8, LANES), jnp.int32),
            pltpu.VMEM((total, few, 4 * nr), bf16),
            pltpu.VMEM((total, few, 2 * nr), f32),
            pltpu.VMEM((total, few, 2 * nr), f32),
            pltpu.VMEM((total + block, few, 2 * nr), f32),
            pltpu.VMEM((n, 2 * block, few, 2 * nr), f32),
            pltpu.VMEM((block, few, 2 * nr), f32),
            pltpu.VMEM((n, LANES), f32),
            pltpu.VMEM((PASSES, n * nf, 1, LANES), f32),
            pltpu.VMEM(forward.shape, f32),
            pltpu.VMEM(inverse.shape, f32),
            pltpu.VMEM((4 * nr, 2 * nr), bf16),
            pltpu.VMEM((2, 3 * nr, nr), bf16),
            dma((10,)),
            dma((n,)),
            dma((n,)),
            dma((n,)),
            dma((n,)),
            dma((n,)),
            dma((n,)),
            dma((PASSES,)),
            dma((PASSES,)),
            dma((n,)),
            dma((n,)),
        ],
        compiler_params=pltpu.CompilerParams(
            collective_id=0, has_side_effects=True, vmem_limit_bytes=60 * 1024 * 1024
        ),
    )(blended, estimate, partner, delays, levels, jnp.asarray(forward), jnp.asarray(inverse))
    return pl.pallas_call(
        copy_kernel,
        out_shape=jax.ShapeDtypeStruct(estimate.shape, estimate.dtype),
        in_specs=[anywhere],
        out_specs=anywhere,
        scratch_shapes=[
            pltpu.VMEM(estimate.shape, bf16),
            dma(estimate.shape[:2]),
            dma(estimate.shape[:2]),
        ],
        compiler_params=pltpu.CompilerParams(vmem_limit_bytes=60 * 1024 * 1024),
    )(result)


def solution(mesh):
    n, nf = mesh.shape["shot"], mesh.shape["freq"]

    def body(blended, estimate, partner, delays, levels):
        block, freq_local, nr = estimate.shape[1:]
        whole_tiles = (
            n == 8 and freq_local % (16 * n) == 0 and nr % (2 * LANES) == 0 and n * block <= LANES
        )
        if whole_tiles:
            return in_one_kernel(n, nf, blended, estimate, partner, delays, levels)
        return on_device(blended, estimate, partner, delays, levels)

    return jax.shard_map(
        body,
        mesh=mesh,
        in_specs=(
            P(None, "shot", "freq", None),
            P(None, "shot", "freq", None),
            P("shot"),
            P(),
            P(),
        ),
        out_specs=P(None, "shot", "freq", None),
        check_vma=False,
    )
```

```python
import functools
import math

import jax
import jax.numpy as jnp
import numpy as np
from jax import lax
from jax.experimental import pallas as pl
from jax.experimental.pallas import tpu as pltpu
from jax.sharding import PartitionSpec as P

NF = 512
NT = 1024
PASSES = 2


relaxation = 0.5
level_scale = 0.25


def tables(length):
    indices = jnp.arange(length, dtype=jnp.int32)
    products = jnp.mod(indices[:, None] * indices[None, :], length)
    angles = 2.0 * math.pi / length * products.astype(jnp.float32)
    return (jnp.cos(angles), jnp.sin(angles))


def spectrum(real_part, imag_part, direction_sign, shot_cos, shot_sin, recv_cos, recv_sin):
    highest = lax.Precision.HIGHEST

    def receivers(values, table):
        return jnp.einsum("...n,nk->...k", values, table, precision=highest)

    def shots(values, table):
        return jnp.einsum("tk,...tfn->...kfn", table, values, precision=highest)

    first_real = receivers(real_part, recv_cos) + direction_sign * receivers(imag_part, recv_sin)
    first_imag = receivers(imag_part, recv_cos) - direction_sign * receivers(real_part, recv_sin)
    out_real = shots(first_real, shot_cos) + direction_sign * shots(first_imag, shot_sin)
    out_imag = shots(first_imag, shot_cos) - direction_sign * shots(first_real, shot_sin)
    scale = 1.0 / math.sqrt(shot_cos.shape[0] * recv_cos.shape[0])
    return (out_real * scale, out_imag * scale)


def shrink(real_part, imag_part, threshold):
    modulus = jnp.sqrt(real_part * real_part + imag_part * imag_part)
    factor = jnp.maximum(modulus - threshold, 0.0) / jnp.maximum(modulus, threshold)
    return (real_part * factor, imag_part * factor)


def phase_tables(offsets, frequency):
    phase_index = jnp.mod(frequency[None, :] * offsets[:, None], NT)
    angles = 2.0 * math.pi / NT * phase_index.astype(jnp.float32)
    return (jnp.cos(angles)[:, :, None], jnp.sin(angles)[:, :, None])


def relax_step(current, blended, partner_recs, phase_cos, phase_sin):
    shifted_real = partner_recs[0] * phase_cos + partner_recs[1] * phase_sin
    shifted_imag = partner_recs[1] * phase_cos - partner_recs[0] * phase_sin
    shifted = jnp.stack([shifted_real, shifted_imag])
    current_f = current.astype(jnp.float32)
    return current_f + relaxation * (blended.astype(jnp.float32) - current_f - shifted)


def whole_pass(
    current, blended, partner_all, phase_cos, phase_sin, level_all, taper, tables_all, block
):
    shot_cos, shot_sin, recv_cos, recv_sin = tables_all
    total_shots = current.shape[1]
    few_freq = current.shape[2]
    receivers_count = current.shape[3]
    count = total_shots // block
    partner_recs = jnp.take(current, partner_all, axis=1).astype(jnp.float32)
    updated = relax_step(current, blended, partner_recs, phase_cos, phase_sin)
    grouped = jnp.transpose(
        updated.reshape(2, count, block, few_freq, receivers_count), (1, 0, 2, 3, 4)
    )
    following = jnp.concatenate([grouped[1:], jnp.zeros_like(grouped[:1])], axis=0)
    segments = jnp.concatenate([grouped, following], axis=2) * taper[None, None, :, None, None]
    coef_real, coef_imag = spectrum(
        segments[:, 0], segments[:, 1], 1.0, shot_cos, shot_sin, recv_cos, recv_sin
    )
    modulus = jnp.sqrt(coef_real * coef_real + coef_imag * coef_imag)
    local_sum = jnp.sum(modulus, axis=(1, 2, 3))
    total_sum = lax.psum(local_sum, ("shot", "freq"))
    span = 2 * block
    threshold = (level_scale * level_all * total_sum / (span * NF * receivers_count))[
        :, None, None, None
    ]
    kept_real, kept_imag = shrink(coef_real, coef_imag, threshold)
    back_real, back_imag = spectrum(
        kept_real, kept_imag, -1.0, shot_cos, shot_sin, recv_cos, recv_sin
    )
    result = jnp.stack([back_real, back_imag], axis=1)
    firsts = result[:, :, :block]
    seconds = jnp.concatenate(
        [jnp.zeros_like(result[:1, :, block:]), result[:-1, :, block:]], axis=0
    )
    summed = firsts + seconds
    return (
        jnp.transpose(summed, (1, 0, 2, 3, 4))
        .reshape(2, total_shots, few_freq, receivers_count)
        .astype(jnp.bfloat16)
    )


def on_device(blended, estimate, partner, delays, levels):
    block = estimate.shape[1]
    freq_local = estimate.shape[2]
    receivers_count = estimate.shape[3]
    span = 2 * block
    steps_t = jnp.arange(span, dtype=jnp.float32)
    taper = jnp.sin(math.pi * (steps_t + 0.5) / span) ** 2
    shot_cos, shot_sin = tables(span)
    recv_cos, recv_sin = tables(receivers_count)
    tables_all = (shot_cos, shot_sin, recv_cos, recv_sin)
    blended_all, current = (
        lax.all_to_all(blended, "shot", split_axis=2, concat_axis=1, tiled=True),
        lax.all_to_all(estimate, "shot", split_axis=2, concat_axis=1, tiled=True),
    )
    few_freq = current.shape[2]
    partner_all = lax.all_gather(partner, "shot", axis=0, tiled=True)
    offsets = jnp.take(delays, partner_all) - delays
    frequency = (
        lax.axis_index("freq") * freq_local
        + lax.axis_index("shot") * few_freq
        + jnp.arange(few_freq, dtype=jnp.int32)
    )
    phase_cos, phase_sin = phase_tables(offsets, frequency)
    level_all = levels.astype(jnp.float32)
    for pass_index in range(PASSES):
        current = whole_pass(
            current,
            blended_all,
            partner_all,
            phase_cos,
            phase_sin,
            level_all,
            taper,
            tables_all,
            block,
        )
    return lax.all_to_all(current, "shot", split_axis=1, concat_axis=2, tiled=True)


LANES = 128
TINY = 1.1754944e-38


def fourier_matrices(length):
    half = np.arange(length // 2)

    def turns(receivers, parity):
        angles = 2.0 * np.pi / length * (np.outer(receivers, 2 * half + parity) % length)
        cos, sin = np.cos(angles), np.sin(angles)
        return np.block([[cos, -sin], [sin, cos]])

    forward = np.concatenate([turns(np.arange(length), parity) for parity in range(2)], axis=1)
    inverse = np.stack([turns(half, parity).T for parity in range(2)])
    return forward.astype(np.float32), inverse.astype(np.float32)


def short_fourier(values, sign):
    count = len(values)
    if count == 1:
        return values
    even = short_fourier(values[0::2], sign)
    odd = short_fourier(values[1::2], sign)
    low, high = [], []
    for k in range(count // 2):
        real, imag = odd[k]
        if 4 * k == count:
            real, imag = (-imag, real) if sign > 0 else (imag, -real)
        elif 8 * k == count or 8 * k == 3 * count:
            half = math.sqrt(0.5)
            turned = (real - sign * imag, imag + sign * real)
            if 8 * k == 3 * count:
                turned = (-real - sign * imag, sign * real - imag)
            real, imag = turned[0] * half, turned[1] * half
        elif k:
            cos = math.cos(2.0 * math.pi * k / count)
            sin = sign * math.sin(2.0 * math.pi * k / count)
            real, imag = real * cos - imag * sin, imag * cos + real * sin
        low.append((even[k][0] + real, even[k][1] + imag))
        high.append((even[k][0] - real, even[k][1] - imag))
    return low + high


def flipped(index, mask, count):
    result, bit = 0, 1
    while bit < count:
        result = result + (index // bit + mask // bit) % 2 * bit
        bit *= 2
    return result


def deblend_kernel(
    n,
    nf,
    block,
    few,
    nr,
    blended_ref,
    estimate_ref,
    partner_hbm,
    delays_hbm,
    levels_hbm,
    forward_hbm,
    inverse_hbm,
    out_ref,
    partner_ref,
    delays_ref,
    levels_ref,
    e_home,
    b_home,
    e_all,
    b_all,
    info,
    turn_cos,
    turn_sin,
    known_ref,
    mates,
    x,
    estimated,
    observed,
    lines,
    coefs,
    carry,
    limit,
    sums,
    exact_forward,
    exact_inverse,
    forward,
    inverse,
    local_sem,
    info_send,
    info_recv,
    e_send,
    e_recv,
    b_send,
    b_recv,
    sums_send,
    sums_recv,
    out_send,
    out_recv,
):
    total = n * block
    span = 2 * block
    half = n // 2
    hr = nr // 2
    columns = [(parity, c) for parity in range(2) for c in range(0, hr, LANES)]
    me = lax.axis_index("shot")
    column = lax.axis_index("freq")
    mesh_id = pl.DeviceIdType.MESH
    peers = [flipped(me, k, n) for k in range(n)]
    order = list(range(half, n)) + list(range(1, half))
    others = [lax.rem(column + k, nf) for k in range(nf)]
    everyone = [(k, f) for k in order + [0] for f in range(nf) if (k, f) != (0, 0)]

    second = n - n // 4
    am_second = me >= second
    same = [(peers[k] >= second) == am_second for k in range(n)]
    barrier = pltpu.get_barrier_semaphore()

    def greet(k):
        for f in range(nf):
            if (k, f) != (0, 0):
                where = {"shot": peers[k], "freq": others[f]}
                pl.semaphore_signal(barrier, inc=1, device_id=where, device_id_type=mesh_id)


    scalar_copies = [
        pltpu.make_async_copy(partner_hbm, partner_ref, local_sem.at[3]),
        pltpu.make_async_copy(delays_hbm, delays_ref, local_sem.at[4]),
        pltpu.make_async_copy(levels_hbm, levels_ref, local_sem.at[5]),
    ]
    for copy in scalar_copies:
        copy.start()
    home_copies = [
        pltpu.make_async_copy(estimate_ref, e_home, local_sem.at[8]),
        pltpu.make_async_copy(blended_ref, b_home, local_sem.at[9]),
    ]
    for copy in home_copies:
        copy.start()
    local_copies = [
        pltpu.make_async_copy(forward_hbm, exact_forward, local_sem.at[0]),
        pltpu.make_async_copy(inverse_hbm, exact_inverse, local_sem.at[6]),
        pltpu.make_async_copy(
            estimate_ref.at[:, :, pl.ds(me * few, few), :],
            e_all.at[:, pl.ds(me * block, block)],
            local_sem.at[1],
        ),
        pltpu.make_async_copy(
            blended_ref.at[:, :, pl.ds(me * few, few), :],
            b_all.at[:, pl.ds(me * block, block)],
            local_sem.at[2],
        ),
    ]
    for copy in local_copies:
        copy.start()

    greet(0)
    for k in order:
        pl.when(same[k])(functools.partial(greet, k))

    for copy in scalar_copies:
        copy.wait()
    lane = lax.broadcasted_iota(jnp.int32, (8, LANES), 1)
    row = lax.broadcasted_iota(jnp.int32, (8, LANES), 0)
    tile = jnp.zeros((8, LANES), jnp.int32)
    for i in range(block):
        own = me * block + i
        mate = partner_ref[i]
        offset = delays_ref[mate] - delays_ref[own]
        here = lane == own
        tile = jnp.where(here & (row == 0), mate, tile)
        tile = jnp.where(here & (row == 1), offset, tile)
    info[0] = tile
    for copy in home_copies:
        copy.wait()

    pl.semaphore_wait(barrier, jnp.where(am_second, n * nf - 1, second * nf - 1))
    for k in order:
        pl.when(jnp.logical_not(same[k]))(functools.partial(greet, k))

    def send(source, target, send_sem, recv_sem, where, start=True):
        copy = pltpu.make_async_remote_copy(
            src_ref=source,
            dst_ref=target,
            send_sem=send_sem,
            recv_sem=recv_sem,
            device_id=where,
            device_id_type=mesh_id,
        )
        if start:
            copy.start()
        return copy

    record_copies = {k: [] for k in range(n)}
    record_copies[0] = local_copies[2:]
    info_copies = []
    for k in order:
        where = {"shot": peers[k]}
        info_copies.append(
            send(info.at[0], info.at[k], info_send.at[k], info_recv.at[k], where, start=False)
        )
        for held, whole, sent, received in (
            (e_home, e_all, e_send, e_recv),
            (b_home, b_all, b_send, b_recv),
        ):
            record_copies[k].append(
                send(
                    held.at[:, :, pl.ds(peers[k] * few, few), :],
                    whole.at[:, pl.ds(me * block, block)],
                    sent.at[k],
                    received.at[k],
                    where,
                    start=False,
                )
            )

    def begin(k, info_copy):
        info_copy.start()
        for copy in record_copies[k]:
            copy.start()

    for k, info_copy in zip(order, info_copies):
        pl.when(jnp.logical_or(am_second, same[k]))(functools.partial(begin, k, info_copy))

    @pl.when(jnp.logical_not(am_second))
    def _():
        pl.semaphore_wait(barrier, (n - second) * nf)

    for k, info_copy in zip(order, info_copies):
        late = jnp.logical_not(jnp.logical_or(am_second, same[k]))
        pl.when(late)(functools.partial(begin, k, info_copy))

    lines[pl.ds(total, block)] = jnp.zeros((block, few, 2 * nr), jnp.float32)
    for copy in info_copies:
        copy.wait_recv()
    known = info[0]
    for k in range(1, n):
        known = known + info[k]
    frequency = (column * n + me) * few + lax.broadcasted_iota(jnp.int32, (few, LANES), 0)
    phase = (frequency * known[1:2, :]) & (NT - 1)
    angles = 2.0 * math.pi / NT * phase.astype(jnp.float32)
    cos_table = relaxation * jnp.cos(angles)
    sin_table = relaxation * jnp.sin(angles)
    known_ref[...] = known
    to_scalars = pltpu.make_async_copy(known_ref, mates, local_sem.at[7])
    to_scalars.start()
    for s in range(total):
        turn_cos[s] = jnp.broadcast_to(cos_table[:, s : s + 1], (few, LANES))
        turn_sin[s] = jnp.broadcast_to(sin_table[:, s : s + 1], (few, LANES))

    for copy in local_copies[:2]:
        copy.wait()
    top = exact_forward[...].astype(jnp.bfloat16)
    forward[: 2 * nr] = top
    forward[2 * nr :] = (exact_forward[...] - top.astype(jnp.float32)).astype(jnp.bfloat16)
    top = exact_inverse[...].astype(jnp.bfloat16)
    inverse[:, :nr] = top
    inverse[:, nr : 2 * nr] = top
    inverse[:, 2 * nr :] = (exact_inverse[...] - top.astype(jnp.float32)).astype(jnp.bfloat16)
    to_scalars.wait()

    def keep(s, parity, at, value):
        start = 2 * nr * parity + at
        top = value.astype(jnp.bfloat16)
        x[s, :, start : start + LANES] = top
        rest = value - top.astype(jnp.float32)
        x[s, :, start + nr : start + nr + LANES] = rest.astype(jnp.bfloat16)

    def relax(pair, carried):
        for side in range(2):
            for i in range(block):
                s = (pair + side * half) * block + i
                mate = mates[0, s]
                cos, sin = turn_cos[s], turn_sin[s]
                for parity, c in columns:
                    at = parity * nr + c
                    reals, imags = slice(at, at + LANES), slice(at + hr, at + hr + LANES)
                    mate_real = estimated[mate, :, reals]
                    mate_imag = estimated[mate, :, imags]
                    seen_real = estimated[s, :, reals] + observed[s, :, reals]
                    seen_imag = estimated[s, :, imags] + observed[s, :, imags]
                    lines[s, :, reals] = relaxation * seen_real - (mate_real * cos + mate_imag * sin)
                    lines[s, :, imags] = relaxation * seen_imag - (mate_imag * cos - mate_real * sin)
        return carried

    def to_lines(owner):
        records = pl.ds(owner * block, block)
        rows = []
        for whole in (e_all, b_all):
            real = whole[0, records].reshape(block * few, nr)
            imag = whole[1, records].reshape(block * few, nr)
            rows.append(jnp.concatenate([real, imag, real, imag], axis=1))
        result = jnp.dot(
            jnp.concatenate(rows, axis=0), forward[...], preferred_element_type=jnp.float32
        ).reshape(2 * block, few, 2 * nr)
        estimated[records] = result[:block]
        observed[records] = result[block:]

    def to_estimate(start, shots):
        results = []
        for parity in range(2):
            start_lane = 2 * nr * parity
            both = x[pl.ds(start, shots), :, start_lane : start_lane + 2 * nr]
            both = both.reshape(shots * few, 2 * nr)
            rows = jnp.concatenate([both, both[:, :nr]], axis=1)
            result = jnp.dot(rows, inverse[parity], preferred_element_type=jnp.float32)
            results.append(result.reshape(shots, few, nr))
        even, odd = results
        for lanes, result in ((slice(0, hr), even + odd), (slice(hr, nr), even - odd)):
            for part in range(2):
                e_all[part, pl.ds(start, shots), :, lanes] = result[
                    :, :, part * hr : (part + 1) * hr
                ].astype(jnp.bfloat16)

    weights = [math.sin(math.pi * (t + 0.5) / span) ** 2 for t in range(span)]

    def analyse(step):
        def window(j, carried):
            summed = jnp.zeros((few, LANES), jnp.float32)
            for parity, c in columns:
                c += parity * nr
                values = [
                    (
                        lines[j * block + t, :, c : c + LANES] * weights[t],
                        lines[j * block + t, :, hr + c : hr + c + LANES] * weights[t],
                    )
                    for t in range(span)
                ]
                for k, (real, imag) in enumerate(short_fourier(values, -1)):
                    power = real * real + imag * imag
                    summed = summed + power * lax.rsqrt(jnp.maximum(power, TINY))
                    coefs[j, k, :, c : c + LANES] = real
                    coefs[j, k, :, hr + c : hr + c + LANES] = imag
            limit[pl.ds(j, 1), :] = jnp.sum(summed, axis=0, keepdims=True)
            return carried

        lax.fori_loop(0, n, window, 0)

    departures = list(info_copies)
    diagonal = lax.broadcasted_iota(jnp.int32, (n, LANES), 0) == lax.broadcasted_iota(
        jnp.int32, (n, LANES), 1
    )

    def thresholds(step):
        column_sums = jnp.sum(limit[...], axis=1, keepdims=True)
        sums[step, 0] = jnp.sum(jnp.where(diagonal, column_sums, 0.0), axis=0, keepdims=True)
        for k, f in everyone:
            send(
                sums.at[step, 0],
                sums.at[step, k * nf + f],
                sums_send.at[step],
                sums_recv.at[step],
                {"shot": peers[k], "freq": others[f]},
            )
        rows = sums.at[step, pl.ds(1, n * nf - 1)]
        arrived = pltpu.make_async_remote_copy(
            src_ref=rows,
            dst_ref=rows,
            send_sem=sums_send.at[step],
            recv_sem=sums_recv.at[step],
            device_id={"shot": peers[1]},
            device_id_type=mesh_id,
        )
        arrived.wait_recv()
        departures.append(arrived)
        whole = jnp.sum(sums[step], axis=0)
        column_sums = jnp.sum(jnp.where(diagonal, whole, 0.0), axis=1, keepdims=True)
        limit[...] = jnp.broadcast_to(column_sums, (n, LANES))

    count = span * few * n * nf * nr

    def synthesise(last, j, carried, firsts=True):
        scale = 1.0 / (span * nr) if last else 1.0 / span
        level = levels_ref[j].astype(jnp.float32) * (level_scale * scale / count)
        bound = limit[pl.ds(j, 1), :] * level
        for parity, c in columns:
            c += parity * nr
            values = []
            for k in range(span):
                real = coefs[j, k, :, c : c + LANES]
                imag = coefs[j, k, :, hr + c : hr + c + LANES]
                power = real * real + imag * imag
                factor = jnp.maximum(scale - bound * lax.rsqrt(power), 0.0)
                values.append((real * factor, imag * factor))
            for t, parts in enumerate(short_fourier(values, 1)):
                for part in range(2):
                    lanes = slice(part * hr + c, part * hr + c + LANES)
                    if t < block and not firsts:
                        continue
                    if t < block:
                        value = parts[part] + carry[t, :, lanes]
                        if last:
                            keep(j * block + t, parity, part * hr + c - parity * nr, value)
                        else:
                            estimated[j * block + t, :, lanes] = value
                    else:
                        carry[t - block, :, lanes] = parts[part]
        return carried

    for step in range(PASSES):
        if step == 0:
            for near in range(half):
                for k in (near, near + half):
                    for copy in record_copies[k]:
                        if k:
                            copy.wait_recv()
                            departures.append(copy)
                        else:
                            copy.wait()
                    to_lines(peers[k])
                relax(peers[near] % half, 0)
        else:
            lax.fori_loop(0, half, relax, 0)
        analyse(step)
        thresholds(step)
        if step < PASSES - 1:
            carry[...] = jnp.zeros_like(carry)
            lax.fori_loop(0, n, functools.partial(synthesise, False), 0)

    copies = []
    for group in [(k, k + 1) for k in range(half, n, 2)] + [(2, 3), (0, 1)]:
        first = peers[group[0]] // 2 * 2

        @pl.when(first == 0)
        def _():
            carry[...] = jnp.zeros_like(carry)

        @pl.when(first > 0)
        def _():
            synthesise(True, first - 1, 0, firsts=False)

        synthesise(True, first, 0)
        synthesise(True, first + 1, 0)
        to_estimate(first * block, 2 * block)
        for k in group:
            if k:
                copies.append(
                    send(
                        e_all.at[:, pl.ds(peers[k] * block, block)],
                        out_ref.at[:, :, pl.ds(me * few, few), :],
                        out_send.at[k],
                        out_recv.at[k],
                        {"shot": peers[k]},
                    )
                )
    last = pltpu.make_async_copy(
        e_all.at[:, pl.ds(me * block, block)],
        out_ref.at[:, :, pl.ds(me * few, few), :],
        local_sem.at[0],
    )
    last.start()
    for copy in copies:
        copy.wait()
    for copy in departures:
        copy.wait_send()
    last.wait()


def in_one_kernel(n, nf, blended, estimate, partner, delays, levels):
    block, freq_local, nr = estimate.shape[1:]
    few = freq_local // n
    total = n * block
    forward, inverse = fourier_matrices(nr)
    f32, bf16 = jnp.float32, jnp.bfloat16
    anywhere = pl.BlockSpec(memory_space=pl.ANY)
    dma = pltpu.SemaphoreType.DMA
    return pl.pallas_call(
        functools.partial(deblend_kernel, n, nf, block, few, nr),
        out_shape=jax.ShapeDtypeStruct(estimate.shape, estimate.dtype),
        in_specs=[anywhere] * 7,
        out_specs=anywhere,
        scratch_shapes=[
            pltpu.SMEM(partner.shape, jnp.int32),
            pltpu.SMEM(delays.shape, jnp.int32),
            pltpu.SMEM(levels.shape, jnp.int32),
            pltpu.VMEM(estimate.shape, bf16),
            pltpu.VMEM(blended.shape, bf16),
            pltpu.VMEM((2, total, few, nr), bf16),
            pltpu.VMEM((2, total, few, nr), bf16),
            pltpu.VMEM((n, 8, LANES), jnp.int32),
            pltpu.VMEM((total, few, LANES), f32),
            pltpu.VMEM((total, few, LANES), f32),
            pltpu.VMEM((8, LANES), jnp.int32),
            pltpu.SMEM((8, LANES), jnp.int32),
            pltpu.VMEM((total, few, 4 * nr), bf16),
            pltpu.VMEM((total, few, 2 * nr), f32),
            pltpu.VMEM((total, few, 2 * nr), f32),
            pltpu.VMEM((total + block, few, 2 * nr), f32),
            pltpu.VMEM((n, 2 * block, few, 2 * nr), f32),
            pltpu.VMEM((block, few, 2 * nr), f32),
            pltpu.VMEM((n, LANES), f32),
            pltpu.VMEM((PASSES, n * nf, 1, LANES), f32),
            pltpu.VMEM(forward.shape, f32),
            pltpu.VMEM(inverse.shape, f32),
            pltpu.VMEM((4 * nr, 2 * nr), bf16),
            pltpu.VMEM((2, 3 * nr, nr), bf16),
            dma((10,)),
            dma((n,)),
            dma((n,)),
            dma((n,)),
            dma((n,)),
            dma((n,)),
            dma((n,)),
            dma((PASSES,)),
            dma((PASSES,)),
            dma((n,)),
            dma((n,)),
        ],
        compiler_params=pltpu.CompilerParams(
            collective_id=0, has_side_effects=True, vmem_limit_bytes=60 * 1024 * 1024
        ),
    )(blended, estimate, partner, delays, levels, jnp.asarray(forward), jnp.asarray(inverse))


def solution(mesh):
    n, nf = mesh.shape["shot"], mesh.shape["freq"]

    def body(blended, estimate, partner, delays, levels):
        block, freq_local, nr = estimate.shape[1:]
        whole_tiles = (
            n == 8 and freq_local % (16 * n) == 0 and nr % (2 * LANES) == 0 and n * block <= LANES
        )
        if whole_tiles:
            return in_one_kernel(n, nf, blended, estimate, partner, delays, levels)
        return on_device(blended, estimate, partner, delays, levels)

    return jax.shard_map(
        body,
        mesh=mesh,
        in_specs=(
            P(None, "shot", "freq", None),
            P(None, "shot", "freq", None),
            P("shot"),
            P(),
            P(),
        ),
        out_specs=P(None, "shot", "freq", None),
        check_vma=False,
    )
```

```python
import functools
import math

import jax
import jax.numpy as jnp
import numpy as np
from jax import lax
from jax.experimental import pallas as pl
from jax.experimental.pallas import tpu as pltpu
from jax.sharding import PartitionSpec as P

NF = 512
NT = 1024
PASSES = 2


relaxation = 0.5
level_scale = 0.25


def tables(length):
    indices = jnp.arange(length, dtype=jnp.int32)
    products = jnp.mod(indices[:, None] * indices[None, :], length)
    angles = 2.0 * math.pi / length * products.astype(jnp.float32)
    return (jnp.cos(angles), jnp.sin(angles))


def spectrum(real_part, imag_part, direction_sign, shot_cos, shot_sin, recv_cos, recv_sin):
    highest = lax.Precision.HIGHEST

    def receivers(values, table):
        return jnp.einsum("...n,nk->...k", values, table, precision=highest)

    def shots(values, table):
        return jnp.einsum("tk,...tfn->...kfn", table, values, precision=highest)

    first_real = receivers(real_part, recv_cos) + direction_sign * receivers(imag_part, recv_sin)
    first_imag = receivers(imag_part, recv_cos) - direction_sign * receivers(real_part, recv_sin)
    out_real = shots(first_real, shot_cos) + direction_sign * shots(first_imag, shot_sin)
    out_imag = shots(first_imag, shot_cos) - direction_sign * shots(first_real, shot_sin)
    scale = 1.0 / math.sqrt(shot_cos.shape[0] * recv_cos.shape[0])
    return (out_real * scale, out_imag * scale)


def shrink(real_part, imag_part, threshold):
    modulus = jnp.sqrt(real_part * real_part + imag_part * imag_part)
    factor = jnp.maximum(modulus - threshold, 0.0) / jnp.maximum(modulus, threshold)
    return (real_part * factor, imag_part * factor)


def phase_tables(offsets, frequency):
    phase_index = jnp.mod(frequency[None, :] * offsets[:, None], NT)
    angles = 2.0 * math.pi / NT * phase_index.astype(jnp.float32)
    return (jnp.cos(angles)[:, :, None], jnp.sin(angles)[:, :, None])


def relax_step(current, blended, partner_recs, phase_cos, phase_sin):
    shifted_real = partner_recs[0] * phase_cos + partner_recs[1] * phase_sin
    shifted_imag = partner_recs[1] * phase_cos - partner_recs[0] * phase_sin
    shifted = jnp.stack([shifted_real, shifted_imag])
    current_f = current.astype(jnp.float32)
    return current_f + relaxation * (blended.astype(jnp.float32) - current_f - shifted)


def whole_pass(
    current, blended, partner_all, phase_cos, phase_sin, level_all, taper, tables_all, block
):
    shot_cos, shot_sin, recv_cos, recv_sin = tables_all
    total_shots = current.shape[1]
    few_freq = current.shape[2]
    receivers_count = current.shape[3]
    count = total_shots // block
    partner_recs = jnp.take(current, partner_all, axis=1).astype(jnp.float32)
    updated = relax_step(current, blended, partner_recs, phase_cos, phase_sin)
    grouped = jnp.transpose(
        updated.reshape(2, count, block, few_freq, receivers_count), (1, 0, 2, 3, 4)
    )
    following = jnp.concatenate([grouped[1:], jnp.zeros_like(grouped[:1])], axis=0)
    segments = jnp.concatenate([grouped, following], axis=2) * taper[None, None, :, None, None]
    coef_real, coef_imag = spectrum(
        segments[:, 0], segments[:, 1], 1.0, shot_cos, shot_sin, recv_cos, recv_sin
    )
    modulus = jnp.sqrt(coef_real * coef_real + coef_imag * coef_imag)
    local_sum = jnp.sum(modulus, axis=(1, 2, 3))
    total_sum = lax.psum(local_sum, ("shot", "freq"))
    span = 2 * block
    threshold = (level_scale * level_all * total_sum / (span * NF * receivers_count))[
        :, None, None, None
    ]
    kept_real, kept_imag = shrink(coef_real, coef_imag, threshold)
    back_real, back_imag = spectrum(
        kept_real, kept_imag, -1.0, shot_cos, shot_sin, recv_cos, recv_sin
    )
    result = jnp.stack([back_real, back_imag], axis=1)
    firsts = result[:, :, :block]
    seconds = jnp.concatenate(
        [jnp.zeros_like(result[:1, :, block:]), result[:-1, :, block:]], axis=0
    )
    summed = firsts + seconds
    return (
        jnp.transpose(summed, (1, 0, 2, 3, 4))
        .reshape(2, total_shots, few_freq, receivers_count)
        .astype(jnp.bfloat16)
    )


def on_device(blended, estimate, partner, delays, levels):
    block = estimate.shape[1]
    freq_local = estimate.shape[2]
    receivers_count = estimate.shape[3]
    span = 2 * block
    steps_t = jnp.arange(span, dtype=jnp.float32)
    taper = jnp.sin(math.pi * (steps_t + 0.5) / span) ** 2
    shot_cos, shot_sin = tables(span)
    recv_cos, recv_sin = tables(receivers_count)
    tables_all = (shot_cos, shot_sin, recv_cos, recv_sin)
    blended_all, current = (
        lax.all_to_all(blended, "shot", split_axis=2, concat_axis=1, tiled=True),
        lax.all_to_all(estimate, "shot", split_axis=2, concat_axis=1, tiled=True),
    )
    few_freq = current.shape[2]
    partner_all = lax.all_gather(partner, "shot", axis=0, tiled=True)
    offsets = jnp.take(delays, partner_all) - delays
    frequency = (
        lax.axis_index("freq") * freq_local
        + lax.axis_index("shot") * few_freq
        + jnp.arange(few_freq, dtype=jnp.int32)
    )
    phase_cos, phase_sin = phase_tables(offsets, frequency)
    level_all = levels.astype(jnp.float32)
    for pass_index in range(PASSES):
        current = whole_pass(
            current,
            blended_all,
            partner_all,
            phase_cos,
            phase_sin,
            level_all,
            taper,
            tables_all,
            block,
        )
    return lax.all_to_all(current, "shot", split_axis=1, concat_axis=2, tiled=True)


LANES = 128
TINY = 1.1754944e-38


def fourier_matrices(length):
    half = np.arange(length // 2)

    def turns(receivers, parity):
        angles = 2.0 * np.pi / length * (np.outer(receivers, 2 * half + parity) % length)
        cos, sin = np.cos(angles), np.sin(angles)
        return np.block([[cos, -sin], [sin, cos]])

    forward = np.concatenate([turns(np.arange(length), parity) for parity in range(2)], axis=1)
    inverse = np.stack([turns(half, parity).T for parity in range(2)])
    return forward.astype(np.float32), inverse.astype(np.float32)


def short_fourier(values, sign):
    count = len(values)
    if count == 1:
        return values
    even = short_fourier(values[0::2], sign)
    odd = short_fourier(values[1::2], sign)
    low, high = [], []
    for k in range(count // 2):
        real, imag = odd[k]
        if 4 * k == count:
            real, imag = (-imag, real) if sign > 0 else (imag, -real)
        elif 8 * k == count or 8 * k == 3 * count:
            half = math.sqrt(0.5)
            turned = (real - sign * imag, imag + sign * real)
            if 8 * k == 3 * count:
                turned = (-real - sign * imag, sign * real - imag)
            real, imag = turned[0] * half, turned[1] * half
        elif k:
            cos = math.cos(2.0 * math.pi * k / count)
            sin = sign * math.sin(2.0 * math.pi * k / count)
            real, imag = real * cos - imag * sin, imag * cos + real * sin
        low.append((even[k][0] + real, even[k][1] + imag))
        high.append((even[k][0] - real, even[k][1] - imag))
    return low + high


def flipped(index, mask, count):
    result, bit = 0, 1
    while bit < count:
        result = result + (index // bit + mask // bit) % 2 * bit
        bit *= 2
    return result


def deblend_kernel(
    n,
    nf,
    block,
    few,
    nr,
    blended_ref,
    estimate_ref,
    partner_hbm,
    delays_hbm,
    levels_hbm,
    forward_hbm,
    inverse_hbm,
    out_ref,
    partner_ref,
    delays_ref,
    levels_ref,
    e_home,
    b_home,
    e_all,
    b_all,
    info,
    turn_cos,
    turn_sin,
    known_ref,
    mates,
    x,
    estimated,
    observed,
    lines,
    coefs,
    carry,
    limit,
    sums,
    exact_forward,
    exact_inverse,
    forward,
    inverse,
    local_sem,
    info_send,
    info_recv,
    e_send,
    e_recv,
    b_send,
    b_recv,
    sums_send,
    sums_recv,
    out_send,
    out_recv,
):
    total = n * block
    span = 2 * block
    half = n // 2
    hr = nr // 2
    columns = [(parity, c) for parity in range(2) for c in range(0, hr, LANES)]
    me = lax.axis_index("shot")
    column = lax.axis_index("freq")
    mesh_id = pl.DeviceIdType.MESH
    peers = [flipped(me, k, n) for k in range(n)]
    order = list(range(half, n)) + list(range(1, half))
    others = [lax.rem(column + k, nf) for k in range(nf)]
    everyone = [(k, f) for k in reversed(range(n)) for f in range(nf) if (k, f) != (0, 0)]

    barrier = pltpu.get_barrier_semaphore()

    scalar_copies = [
        pltpu.make_async_copy(partner_hbm, partner_ref, local_sem.at[3]),
        pltpu.make_async_copy(delays_hbm, delays_ref, local_sem.at[4]),
        pltpu.make_async_copy(levels_hbm, levels_ref, local_sem.at[5]),
    ]
    for copy in scalar_copies:
        copy.start()
    home_copies = [
        pltpu.make_async_copy(estimate_ref, e_home, local_sem.at[8]),
        pltpu.make_async_copy(blended_ref, b_home, local_sem.at[9]),
    ]
    for copy in home_copies:
        copy.start()
    local_copies = [
        pltpu.make_async_copy(forward_hbm, exact_forward, local_sem.at[0]),
        pltpu.make_async_copy(inverse_hbm, exact_inverse, local_sem.at[6]),
        pltpu.make_async_copy(
            estimate_ref.at[:, :, pl.ds(me * few, few), :],
            e_all.at[:, pl.ds(me * block, block)],
            local_sem.at[1],
        ),
        pltpu.make_async_copy(
            blended_ref.at[:, :, pl.ds(me * few, few), :],
            b_all.at[:, pl.ds(me * block, block)],
            local_sem.at[2],
        ),
    ]
    for copy in local_copies:
        copy.start()

    for k, f in everyone:
        where = {"shot": peers[k], "freq": others[f]}
        pl.semaphore_signal(barrier, inc=1, device_id=where, device_id_type=mesh_id)
    for copy in scalar_copies:
        copy.wait()
    lane = lax.broadcasted_iota(jnp.int32, (8, LANES), 1)
    row = lax.broadcasted_iota(jnp.int32, (8, LANES), 0)
    tile = jnp.zeros((8, LANES), jnp.int32)
    for i in range(block):
        own = me * block + i
        mate = partner_ref[i]
        offset = delays_ref[mate] - delays_ref[own]
        here = lane == own
        tile = jnp.where(here & (row == 0), mate, tile)
        tile = jnp.where(here & (row == 1), offset, tile)
    info[0] = tile
    for copy in home_copies:
        copy.wait()

    pl.semaphore_wait(barrier, n * nf - 1)

    def send(source, target, send_sem, recv_sem, where):
        copy = pltpu.make_async_remote_copy(
            src_ref=source,
            dst_ref=target,
            send_sem=send_sem,
            recv_sem=recv_sem,
            device_id=where,
            device_id_type=mesh_id,
        )
        copy.start()
        return copy

    info_copies = [
        send(info.at[0], info.at[k], info_send.at[k], info_recv.at[k], {"shot": peers[k]})
        for k in order
    ]
    record_copies = {k: [] for k in range(n)}
    record_copies[0] = local_copies[2:]
    for k in order:
        for held, whole, sent, received in (
            (e_home, e_all, e_send, e_recv),
            (b_home, b_all, b_send, b_recv),
        ):
            record_copies[k].append(
                send(
                    held.at[:, :, pl.ds(peers[k] * few, few), :],
                    whole.at[:, pl.ds(me * block, block)],
                    sent.at[k],
                    received.at[k],
                    {"shot": peers[k]},
                )
            )

    lines[pl.ds(total, block)] = jnp.zeros((block, few, 2 * nr), jnp.float32)
    for copy in info_copies:
        copy.wait_recv()
    known = info[0]
    for k in range(1, n):
        known = known + info[k]
    frequency = (column * n + me) * few + lax.broadcasted_iota(jnp.int32, (few, LANES), 0)
    phase = (frequency * known[1:2, :]) & (NT - 1)
    angles = 2.0 * math.pi / NT * phase.astype(jnp.float32)
    cos_table = relaxation * jnp.cos(angles)
    sin_table = relaxation * jnp.sin(angles)
    known_ref[...] = known
    to_scalars = pltpu.make_async_copy(known_ref, mates, local_sem.at[7])
    to_scalars.start()
    for s in range(total):
        turn_cos[s] = jnp.broadcast_to(cos_table[:, s : s + 1], (few, LANES))
        turn_sin[s] = jnp.broadcast_to(sin_table[:, s : s + 1], (few, LANES))

    for copy in local_copies[:2]:
        copy.wait()
    top = exact_forward[...].astype(jnp.bfloat16)
    forward[: 2 * nr] = top
    forward[2 * nr :] = (exact_forward[...] - top.astype(jnp.float32)).astype(jnp.bfloat16)
    top = exact_inverse[...].astype(jnp.bfloat16)
    inverse[:, :nr] = top
    inverse[:, nr : 2 * nr] = top
    inverse[:, 2 * nr :] = (exact_inverse[...] - top.astype(jnp.float32)).astype(jnp.bfloat16)
    to_scalars.wait()

    def keep(s, parity, at, value):
        start = 2 * nr * parity + at
        top = value.astype(jnp.bfloat16)
        x[s, :, start : start + LANES] = top
        rest = value - top.astype(jnp.float32)
        x[s, :, start + nr : start + nr + LANES] = rest.astype(jnp.bfloat16)

    def relax(pair, carried):
        for side in range(2):
            for i in range(block):
                s = (pair + side * half) * block + i
                mate = mates[0, s]
                cos, sin = turn_cos[s], turn_sin[s]
                for parity, c in columns:
                    at = parity * nr + c
                    reals, imags = slice(at, at + LANES), slice(at + hr, at + hr + LANES)
                    mate_real = estimated[mate, :, reals]
                    mate_imag = estimated[mate, :, imags]
                    seen_real = estimated[s, :, reals] + observed[s, :, reals]
                    seen_imag = estimated[s, :, imags] + observed[s, :, imags]
                    lines[s, :, reals] = relaxation * seen_real - (mate_real * cos + mate_imag * sin)
                    lines[s, :, imags] = relaxation * seen_imag - (mate_imag * cos - mate_real * sin)
        return carried

    def to_lines(owner):
        records = pl.ds(owner * block, block)
        rows = []
        for whole in (e_all, b_all):
            real = whole[0, records].reshape(block * few, nr)
            imag = whole[1, records].reshape(block * few, nr)
            rows.append(jnp.concatenate([real, imag, real, imag], axis=1))
        result = jnp.dot(
            jnp.concatenate(rows, axis=0), forward[...], preferred_element_type=jnp.float32
        ).reshape(2 * block, few, 2 * nr)
        estimated[records] = result[:block]
        observed[records] = result[block:]

    def to_estimate(start, shots):
        results = []
        for parity in range(2):
            start_lane = 2 * nr * parity
            both = x[pl.ds(start, shots), :, start_lane : start_lane + 2 * nr]
            both = both.reshape(shots * few, 2 * nr)
            rows = jnp.concatenate([both, both[:, :nr]], axis=1)
            result = jnp.dot(rows, inverse[parity], preferred_element_type=jnp.float32)
            results.append(result.reshape(shots, few, nr))
        even, odd = results
        for lanes, result in ((slice(0, hr), even + odd), (slice(hr, nr), even - odd)):
            for part in range(2):
                e_all[part, pl.ds(start, shots), :, lanes] = result[
                    :, :, part * hr : (part + 1) * hr
                ].astype(jnp.bfloat16)

    weights = [math.sin(math.pi * (t + 0.5) / span) ** 2 for t in range(span)]

    def analyse(step):
        def window(j, carried):
            summed = jnp.zeros((few, LANES), jnp.float32)
            for parity, c in columns:
                c += parity * nr
                values = [
                    (
                        lines[j * block + t, :, c : c + LANES] * weights[t],
                        lines[j * block + t, :, hr + c : hr + c + LANES] * weights[t],
                    )
                    for t in range(span)
                ]
                for k, (real, imag) in enumerate(short_fourier(values, -1)):
                    power = real * real + imag * imag
                    summed = summed + power * lax.rsqrt(jnp.maximum(power, TINY))
                    coefs[j, k, :, c : c + LANES] = real
                    coefs[j, k, :, hr + c : hr + c + LANES] = imag
            limit[pl.ds(j, 1), :] = jnp.sum(summed, axis=0, keepdims=True)
            return carried

        lax.fori_loop(0, n, window, 0)

    departures = list(info_copies)
    diagonal = lax.broadcasted_iota(jnp.int32, (n, LANES), 0) == lax.broadcasted_iota(
        jnp.int32, (n, LANES), 1
    )

    def thresholds(step):
        column_sums = jnp.sum(limit[...], axis=1, keepdims=True)
        sums[step, 0] = jnp.sum(jnp.where(diagonal, column_sums, 0.0), axis=0, keepdims=True)
        for k, f in everyone:
            send(
                sums.at[step, 0],
                sums.at[step, k * nf + f],
                sums_send.at[step],
                sums_recv.at[step],
                {"shot": peers[k], "freq": others[f]},
            )
        rows = sums.at[step, pl.ds(1, n * nf - 1)]
        arrived = pltpu.make_async_remote_copy(
            src_ref=rows,
            dst_ref=rows,
            send_sem=sums_send.at[step],
            recv_sem=sums_recv.at[step],
            device_id={"shot": peers[1]},
            device_id_type=mesh_id,
        )
        arrived.wait_recv()
        departures.append(arrived)
        whole = jnp.sum(sums[step], axis=0)
        column_sums = jnp.sum(jnp.where(diagonal, whole, 0.0), axis=1, keepdims=True)
        limit[...] = jnp.broadcast_to(column_sums, (n, LANES))

    count = span * few * n * nf * nr

    def synthesise(last, j, carried, firsts=True):
        scale = 1.0 / (span * nr) if last else 1.0 / span
        level = levels_ref[j].astype(jnp.float32) * (level_scale * scale / count)
        bound = limit[pl.ds(j, 1), :] * level
        for parity, c in columns:
            c += parity * nr
            values = []
            for k in range(span):
                real = coefs[j, k, :, c : c + LANES]
                imag = coefs[j, k, :, hr + c : hr + c + LANES]
                power = real * real + imag * imag
                factor = jnp.maximum(scale - bound * lax.rsqrt(power), 0.0)
                values.append((real * factor, imag * factor))
            for t, parts in enumerate(short_fourier(values, 1)):
                for part in range(2):
                    lanes = slice(part * hr + c, part * hr + c + LANES)
                    if t < block and not firsts:
                        continue
                    if t < block:
                        value = parts[part] + carry[t, :, lanes]
                        if last:
                            keep(j * block + t, parity, part * hr + c - parity * nr, value)
                        else:
                            estimated[j * block + t, :, lanes] = value
                    else:
                        carry[t - block, :, lanes] = parts[part]
        return carried

    for step in range(PASSES):
        if step == 0:
            for near in range(half):
                for k in (near, near + half):
                    for copy in record_copies[k]:
                        if k:
                            copy.wait_recv()
                            departures.append(copy)
                        else:
                            copy.wait()
                    to_lines(peers[k])
                relax(peers[near] % half, 0)
        else:
            lax.fori_loop(0, half, relax, 0)
        analyse(step)
        thresholds(step)
        if step < PASSES - 1:
            carry[...] = jnp.zeros_like(carry)
            lax.fori_loop(0, n, functools.partial(synthesise, False), 0)

    copies = []
    for group in [(k, k + 1) for k in range(half, n, 2)] + [(2, 3), (0, 1)]:
        first = peers[group[0]] // 2 * 2

        @pl.when(first == 0)
        def _():
            carry[...] = jnp.zeros_like(carry)

        @pl.when(first > 0)
        def _():
            synthesise(True, first - 1, 0, firsts=False)

        synthesise(True, first, 0)
        synthesise(True, first + 1, 0)
        to_estimate(first * block, 2 * block)
        for k in group:
            if k:
                copies.append(
                    send(
                        e_all.at[:, pl.ds(peers[k] * block, block)],
                        out_ref.at[:, :, pl.ds(me * few, few), :],
                        out_send.at[k],
                        out_recv.at[k],
                        {"shot": peers[k]},
                    )
                )
    last = pltpu.make_async_copy(
        e_all.at[:, pl.ds(me * block, block)],
        out_ref.at[:, :, pl.ds(me * few, few), :],
        local_sem.at[0],
    )
    last.start()
    for copy in copies:
        copy.wait()
    for copy in departures:
        copy.wait_send()
    last.wait()


def in_one_kernel(n, nf, blended, estimate, partner, delays, levels):
    block, freq_local, nr = estimate.shape[1:]
    few = freq_local // n
    total = n * block
    forward, inverse = fourier_matrices(nr)
    f32, bf16 = jnp.float32, jnp.bfloat16
    anywhere = pl.BlockSpec(memory_space=pl.ANY)
    dma = pltpu.SemaphoreType.DMA
    return pl.pallas_call(
        functools.partial(deblend_kernel, n, nf, block, few, nr),
        out_shape=jax.ShapeDtypeStruct(estimate.shape, estimate.dtype),
        in_specs=[anywhere] * 7,
        out_specs=anywhere,
        scratch_shapes=[
            pltpu.SMEM(partner.shape, jnp.int32),
            pltpu.SMEM(delays.shape, jnp.int32),
            pltpu.SMEM(levels.shape, jnp.int32),
            pltpu.VMEM(estimate.shape, bf16),
            pltpu.VMEM(blended.shape, bf16),
            pltpu.VMEM((2, total, few, nr), bf16),
            pltpu.VMEM((2, total, few, nr), bf16),
            pltpu.VMEM((n, 8, LANES), jnp.int32),
            pltpu.VMEM((total, few, LANES), f32),
            pltpu.VMEM((total, few, LANES), f32),
            pltpu.VMEM((8, LANES), jnp.int32),
            pltpu.SMEM((8, LANES), jnp.int32),
            pltpu.VMEM((total, few, 4 * nr), bf16),
            pltpu.VMEM((total, few, 2 * nr), f32),
            pltpu.VMEM((total, few, 2 * nr), f32),
            pltpu.VMEM((total + block, few, 2 * nr), f32),
            pltpu.VMEM((n, 2 * block, few, 2 * nr), f32),
            pltpu.VMEM((block, few, 2 * nr), f32),
            pltpu.VMEM((n, LANES), f32),
            pltpu.VMEM((PASSES, n * nf, 1, LANES), f32),
            pltpu.VMEM(forward.shape, f32),
            pltpu.VMEM(inverse.shape, f32),
            pltpu.VMEM((4 * nr, 2 * nr), bf16),
            pltpu.VMEM((2, 3 * nr, nr), bf16),
            dma((10,)),
            dma((n,)),
            dma((n,)),
            dma((n,)),
            dma((n,)),
            dma((n,)),
            dma((n,)),
            dma((PASSES,)),
            dma((PASSES,)),
            dma((n,)),
            dma((n,)),
        ],
        compiler_params=pltpu.CompilerParams(
            collective_id=0, has_side_effects=True, vmem_limit_bytes=60 * 1024 * 1024
        ),
    )(blended, estimate, partner, delays, levels, jnp.asarray(forward), jnp.asarray(inverse))


def solution(mesh):
    n, nf = mesh.shape["shot"], mesh.shape["freq"]

    def body(blended, estimate, partner, delays, levels):
        block, freq_local, nr = estimate.shape[1:]
        whole_tiles = (
            n == 8 and freq_local % (16 * n) == 0 and nr % (2 * LANES) == 0 and n * block <= LANES
        )
        if whole_tiles:
            return in_one_kernel(n, nf, blended, estimate, partner, delays, levels)
        return on_device(blended, estimate, partner, delays, levels)

    return jax.shard_map(
        body,
        mesh=mesh,
        in_specs=(
            P(None, "shot", "freq", None),
            P(None, "shot", "freq", None),
            P("shot"),
            P(),
            P(),
        ),
        out_specs=P(None, "shot", "freq", None),
        check_vma=False,
    )
```
